128 devices in a mesh: row: 8 (over y, core), col: 16 (over z, x).
Axes of the slice: x: 4, y: 4, z: 4, core: 2. Of those that a mesh axis runs over, the one named last changes fastest.
Arguments:
- src_emb: bfloat16 [32768, 128], P('row'), may hold values from -160 to 160
- tgt_emb: bfloat16 [16384, 128], P('col'), may hold values from -20 to 20
- cost_factor: bfloat16 [128, 128], replicated, may hold values from -1 to 1
- col_start: float32 [16384], P('col'), may hold values from -8 to 8
Outputs:
- bary_src: bfloat16 [32768, 128], P(('row', 'col'))
- bary_tgt: bfloat16 [16384, 128], P('col')
- cross_moment: float32 [128, 128], replicated
- row_potential: float32 [32768], P('row')
- col_potential: float32 [16384], P('col')
The draws below stay inside these ranges and needn't reach their ends.
All inputs are finite; a program needn't handle non-finite values.
Results may differ from the reference program's by a relative error of at most 0.011.
Values sent between devices are 32-bit elements; how exact they have to be, the bound alone decides.
No kernel may reach another device: no remote copies, remote signals or barrier semaphores. Data moves between devices by JAX's collectives and lax.ppermute only.
A program may use at most 64 MiB of HBM per device.

```python
import math
import jax
import jax.numpy as jnp
from jax import lax

D = 128
SWEEPS = 2
NSRC = 32768
NTGT = 16384


def target_shared(key):
    key_scale = jax.random.fold_in(key, 2)
    scales = jnp.exp(jax.random.uniform(key_scale, (NTGT, 1), jnp.float32, math.log(0.5), math.log(5.0)))
    return scales


def draw_tgt_emb(key, part):
    scales = target_shared(key)
    key = jax.random.fold_in(key, 11)
    values = jax.random.truncated_normal(key, -4.0, 4.0, (NTGT, D), jnp.float32) * scales
    return values.astype(jnp.bfloat16)


def draw_src_emb(key, part):
    key = jax.random.fold_in(key, 7)
    key_values, key_scale = jax.random.split(key, 2)
    scales = jnp.exp(jax.random.uniform(key_scale, (NSRC, 1), jnp.float32, math.log(0.5), math.log(5.0)))
    values = jax.random.truncated_normal(key_values, -4.0, 4.0, (NSRC, D), jnp.float32) * scales
    return values.astype(jnp.bfloat16)


def draw_cost_factor(key, part):
    key = jax.random.fold_in(key, 5)
    noise = 0.5 * jax.random.truncated_normal(key, -4.0, 4.0, (D, D), jnp.float32)
    identity = (jnp.arange(D)[:, None] == jnp.arange(D)[None, :]).astype(jnp.float32)
    values = (identity + noise / math.sqrt(D)) / math.sqrt(2.0 * D)
    return values.astype(jnp.bfloat16)


def levels(key, shape, shards, low, high):
    factor_of = 1.0
    for dim, shards_of in shards:
        heights = jax.random.uniform(jax.random.fold_in(jax.random.fold_in(key, 6), dim), (shards_of,), jnp.float32, low / len(shards), high / len(shards))
        factor_of = factor_of * jnp.repeat(jnp.exp(heights), shape[dim] // shards_of).reshape((-1,) + (1,) * (len(shape) - 1 - dim))
    return factor_of


def normal_values(stream_key, extent, width, limit, cuts=(), held_as=jnp.bfloat16):
    drawn = width * jax.random.normal(stream_key, extent, jnp.float32)
    if cuts:
        drawn = drawn * levels(stream_key, extent, cuts, -0.22, 0.18)
    return jnp.clip(drawn, -limit, limit).astype(held_as)


def setup_inputs(seed: int = 0) -> dict:
    key_list = jax.random.split(jax.random.key(seed), 5)
    return {
        "src_emb": draw_src_emb(jax.random.fold_in(key_list[4], 71), 0),
        "tgt_emb": draw_tgt_emb(jax.random.fold_in(key_list[4], 71), 0),
        "cost_factor": draw_cost_factor(jax.random.fold_in(key_list[4], 71), 0),
        "col_start": normal_values(key_list[3], (NTGT,), 2.0, 8.0, ((0, 16),), jnp.float32),
    }


def reference(src_emb, tgt_emb, cost_factor, col_start):
    projected = jnp.dot(src_emb, cost_factor, preferred_element_type=jnp.float32).astype(jnp.bfloat16)
    block_rows = math.gcd(NSRC, 1024)
    block_count = NSRC // block_rows
    proj_blocks = projected.reshape(block_count, block_rows, D)
    src_blocks = src_emb.reshape(block_count, block_rows, D)
    log_src = -math.log(NSRC)
    log_tgt = -math.log(NTGT)

    def scores(proj_block):
        return jnp.dot(proj_block, tgt_emb.T, preferred_element_type=jnp.float32)

    col_potential = col_start
    for sweep_index in range(SWEEPS):
        def row_update(proj_block, potential=col_potential):
            logits = scores(proj_block) + potential[None, :]
            largest = jnp.max(logits, axis=1)
            totals = jnp.sum(jnp.exp(logits - largest[:, None]), axis=1)
            return log_src - (largest + jnp.log(totals))

        row_potential = lax.map(row_update, proj_blocks).reshape(NSRC)

        def col_update(running, inputs):
            largest, totals = running
            proj_block, potential = inputs
            logits = scores(proj_block) + potential[:, None]
            new_largest = jnp.maximum(largest, jnp.max(logits, axis=0))
            totals = totals * jnp.exp(largest - new_largest) + jnp.sum(jnp.exp(logits - new_largest[None, :]), axis=0)
            return (new_largest, totals), None

        initial = (jnp.full((NTGT,), -1e30, jnp.float32), jnp.zeros((NTGT,), jnp.float32))
        (largest, totals), unused = lax.scan(col_update, initial, (proj_blocks, row_potential.reshape(block_count, block_rows)))
        col_potential = log_tgt - (largest + jnp.log(totals))

    def final_update(running, inputs):
        proj_block, src_block, potential = inputs
        logits = scores(proj_block) + potential[:, None] + col_potential[None, :]
        coupling = jnp.exp(logits).astype(jnp.bfloat16)
        target_part = jnp.dot(coupling, tgt_emb, preferred_element_type=jnp.float32)
        running = running + jnp.dot(coupling.T, src_block, preferred_element_type=jnp.float32)
        return running, target_part

    source_mix, mix_blocks = lax.scan(final_update, jnp.zeros((NTGT, D), jnp.float32), (proj_blocks, src_blocks, row_potential.reshape(block_count, block_rows)))
    target_mix = mix_blocks.reshape(NSRC, D)
    cross_moment = jnp.dot(src_emb.astype(jnp.float32).T, target_mix, precision=lax.Precision.HIGHEST, preferred_element_type=jnp.float32)
    bary_src = (NSRC * target_mix).astype(jnp.bfloat16)
    bary_tgt = (NTGT * source_mix).astype(jnp.bfloat16)
    return (bary_src, bary_tgt, cross_moment, row_potential, col_potential)
```

```python
import functools
import math

import jax
import jax.numpy as jnp
from jax import lax
from jax.experimental import pallas as pl
from jax.experimental.pallas import tpu as pltpu
from jax.sharding import PartitionSpec as P

F32 = jnp.float32
BF16 = jnp.bfloat16
NT = (((1,), (1,)), ((), ()))
TINY = 2.0**-80
BLK = 256
CHUNK = 128
VMEM_LIMIT = 24 * 1024 * 1024


def split3(x):
    hi = x.astype(BF16).astype(F32)
    mid = (x - hi).astype(BF16).astype(F32)
    lo = (x - hi - mid).astype(BF16).astype(F32)
    return hi, mid, lo


def iota(shape, dim):
    return lax.broadcasted_iota(jnp.int32, shape, dim)


def lanes(b, size):
    return pl.ds(pl.multiple_of(b * size, size), size)


def aug_columns(shift):
    hi, mid, lo = split3(shift)
    lane = iota((shift.shape[0], 128), 1)
    out = jnp.where(lane < 3, 1.0, 0.0)
    out = jnp.where(lane == 3, hi, out)
    out = jnp.where(lane == 4, mid, out)
    out = jnp.where(lane == 5, lo, out)
    return out.astype(BF16)


def aug_rows(term):
    hi, mid, lo = split3(term)
    sub = iota((16, term.shape[1]), 0)
    out = jnp.where((sub >= 3) & (sub < 6), 1.0, 0.0)
    out = jnp.where(sub == 0, hi, out)
    out = jnp.where(sub == 1, mid, out)
    out = jnp.where(sub == 2, lo, out)
    zeros = jnp.zeros((112, term.shape[1]), BF16)
    return jnp.concatenate([out.astype(BF16), zeros], axis=0)


def log_sum(x):
    largest = jnp.max(x, axis=0, keepdims=True)
    return largest + jnp.log(jnp.sum(jnp.exp(x - largest), axis=0, keepdims=True))


def first_rows(src, tgt, factor, start, lse, proj_t, src_t, tgt_t, aug, *, copies):
    eye = jnp.where(iota((128, 128), 0) == iota((128, 128), 1), 1.0, 0.0).astype(BF16)
    factor_t = factor[...].astype(F32).T.astype(BF16)
    left = jnp.concatenate([factor_t, eye], axis=0)
    tgt_t[...] = lax.dot_general(eye, tgt[...], NT, preferred_element_type=F32).astype(BF16)
    column = jnp.broadcast_to(start[...], (8, start.shape[1])).T[:, :1]
    aug[:, :128] = tgt[...]
    aug[:, 128:] = aug_columns(column)
    under = aug_rows(jnp.zeros((1, BLK), F32))

    def block(b, carry):
        at = lanes(b, BLK)
        both = lax.dot_general(left, src[at, :], NT, preferred_element_type=F32).astype(BF16)
        proj_t[:, at] = both[:128]
        src_t[:, at] = both[128:]
        right = jnp.concatenate([both[:128], under], axis=0)
        largest = jnp.full((8, BLK), -jnp.inf, F32)
        total = jnp.zeros((8, BLK), F32)
        for c in range(tgt.shape[0] // CHUNK):
            x = jnp.dot(aug[c * CHUNK : (c + 1) * CHUNK, :], right, preferred_element_type=F32)
            x = x.reshape(CHUNK // 8, 8, BLK)
            new = jnp.maximum(largest, jnp.max(x, axis=0))
            total = total * jnp.exp(largest - new) + jnp.sum(jnp.exp(x - new[None]), axis=0)
            largest = new
        top = jnp.max(largest, axis=0, keepdims=True)
        value = top + jnp.log(jnp.sum(total * jnp.exp(largest - top), axis=0, keepdims=True))
        lse[:, at] = jnp.broadcast_to(value, (copies, BLK))
        return carry

    lax.fori_loop(0, src.shape[0] // BLK, block, 0)


def first_columns(parts, proj_t, aug_in, start, kernel_t, lse, shift, rho, aug, sums, *, copies):
    blocks = proj_t.shape[1] // BLK
    chunks = aug.shape[0] // CHUNK
    rho[...] = -log_sum(parts[...])
    aug[...] = aug_in[...]
    shift[...] = start[...]

    def scores(c, right):
        return jnp.dot(aug[c * CHUNK : (c + 1) * CHUNK, :], right, preferred_element_type=F32)

    def right_of(at):
        return jnp.concatenate([proj_t[:, at], aug_rows(rho[:, at])], axis=0)

    def fill():
        sums[...] = jnp.zeros_like(sums)

        def block(b, carry):
            at = lanes(b, BLK)
            right = right_of(at)
            for c in range(chunks):
                rows = slice(c * CHUNK, (c + 1) * CHUNK)
                e = jnp.exp(scores(c, right))
                kernel_t[rows, at] = e.astype(BF16)
                sums[rows, :] += e[:, :128] + e[:, 128:]
            return carry

        lax.fori_loop(0, blocks, block, 0)
        return jnp.sum(sums[...].T, axis=0, keepdims=True)

    total = fill()
    lse[...] = jnp.broadcast_to(jnp.log(total) - shift[...], lse.shape)

    @pl.when(jnp.min(total) < TINY)
    def _():
        sums[...] = jnp.full(sums.shape, -jnp.inf, F32)

        def block(b, carry):
            right = right_of(lanes(b, BLK))
            for c in range(chunks):
                rows = slice(c * CHUNK, (c + 1) * CHUNK)
                x = scores(c, right)
                sums[rows, :] = jnp.maximum(sums[rows, :], jnp.maximum(x[:, :128], x[:, 128:]))
            return carry

        lax.fori_loop(0, blocks, block, 0)
        top = jnp.max(sums[...], axis=1, keepdims=True)
        old = jnp.broadcast_to(start[...], (8, start.shape[1])).T[:, :1]
        aug[:, 128:] = aug_columns(old - top)
        wide = jnp.broadcast_to(top, sums.shape).T
        shift[...] = start[...] - wide[:1]
        again = fill()
        lse[...] = jnp.broadcast_to(jnp.log(again) - shift[...], lse.shape)


def second_rows(parts, shift, kernel_t, sums, weight, potential, *, src_count, tgt_count):
    total = log_sum(parts[...])
    potential[...] = math.log(src_count) - math.log(tgt_count) - total
    w = jnp.exp(-math.log(tgt_count) - total - shift[...])
    weight[...] = w
    hi = w.astype(BF16).astype(F32)
    sub = iota((16, w.shape[1]), 0)
    left = jnp.where(sub == 0, hi, jnp.where(sub == 1, w - hi, 0.0)).astype(BF16)
    size = 512

    def block(b, carry):
        at = lanes(b, size)
        x = jnp.dot(left, kernel_t[:, at], preferred_element_type=F32)
        sums[:, at] = jnp.broadcast_to(x[:1] + x[1:2], (sums.shape[0], size))
        return carry

    lax.fori_loop(0, kernel_t.shape[1] // size, block, 0)


def second_columns(
    core, parts, rho, kernel_t, src_t, weight, sums, keep, send, scale, potential, total, *, src_count
):
    q = jnp.sum(parts[...], axis=0, keepdims=True)
    u = 1.0 / (src_count * q)
    scale[...] = u
    potential[...] = rho[...] - 2.0 * math.log(src_count) - jnp.log(q)
    size = 512
    for b in range(kernel_t.shape[1] // size):
        at = slice(b * size, (b + 1) * size)
        ub = u[:, at]
        hi = ub.astype(BF16).astype(F32)
        sub = iota((16, size), 0)
        low = jnp.where(sub == 0, hi, jnp.where(sub == 1, ub - hi, 0.0)).astype(BF16)
        left = jnp.concatenate([(src_t[:, at].astype(F32) * ub).astype(BF16), low], axis=0)
        x = lax.dot_general(left, kernel_t[:, at], NT, preferred_element_type=F32)
        if b == 0:
            total[...] = x
        else:
            total[...] += x
    w = weight[...]
    sums[...] = jnp.broadcast_to(w * (total[128:129, :] + total[129:130, :]), sums.shape)
    half = keep.shape[0]
    own = core[0] * half
    keep[...] = total[pl.ds(pl.multiple_of(own, half), half), :] * w
    send[...] = total[pl.ds(pl.multiple_of(half - own, half), half), :] * w


def target_sums(parts, weight, before, tgt_t, kernel_t, scale, out, potential, gain, *, src_count, tgt_count):
    total = jnp.sum(parts[...], axis=0, keepdims=True)
    g = 1.0 / (tgt_count * total)
    gain[...] = g
    potential[...] = before[...] - math.log(tgt_count) - jnp.log(total)
    left = (tgt_t[...].astype(F32) * (weight[...] * g)).astype(BF16)
    share = out.shape[2]

    def block(b, carry):
        at = lanes(b, share)
        x = jnp.dot(left, kernel_t[:, at], preferred_element_type=F32)
        out[b] = x * (scale[:, at] * src_count)
        return carry

    lax.fori_loop(0, out.shape[0], block, 0)


def finish_sources(low, high, gain, tgt, moment, out, *, tgt_count):
    full = jnp.concatenate([low[...], high[...]], axis=0) * gain[...]
    moment[...] = jnp.dot(
        full, tgt[...].astype(F32), precision=lax.Precision.HIGHEST, preferred_element_type=F32
    )
    out[...] = (full * tgt_count).T.astype(BF16)


def finish_targets(parts, out):
    out[...] = jnp.sum(parts[...], axis=0).T.astype(BF16)


def call(body, outs, *args, scratch=(), smem=0):
    specs = [pl.BlockSpec(memory_space=pltpu.SMEM)] * smem
    specs += [pl.BlockSpec(memory_space=pltpu.VMEM)] * (len(args) - smem)
    return pl.pallas_call(
        body,
        out_shape=outs,
        in_specs=specs,
        out_specs=jax.tree.map(lambda _: pl.BlockSpec(memory_space=pltpu.VMEM), outs),
        scratch_shapes=list(scratch),
        compiler_params=pltpu.CompilerParams(vmem_limit_bytes=VMEM_LIMIT),
    )(*args)


def f32(*shape):
    return jax.ShapeDtypeStruct(shape, F32)


def bf16(*shape):
    return jax.ShapeDtypeStruct(shape, BF16)


def local(src_emb, tgt_emb, cost_factor, col_start):
    rows, cols = src_emb.shape[0], tgt_emb.shape[0]
    width = src_emb.shape[1]
    row_size, col_size = lax.axis_size("row"), lax.axis_size("col")
    src_count, tgt_count = rows * row_size, cols * col_size
    share = rows // col_size
    start = col_start.reshape(1, cols)
    core = lax.rem(lax.axis_index("row"), 2).reshape(1).astype(jnp.int32)

    def swap(x):
        return lax.ppermute(x, "row", [(i, i ^ 1) for i in range(row_size)])

    ring = ({0: 1, 1: 0, 2: 3, 3: 2}, {1: 2, 2: 1, 3: 0, 0: 3})

    def along_y(x, step):
        return lax.ppermute(x, "row", [(i, ring[step][i // 2] * 2 + i % 2) for i in range(row_size)])

    def along_z(x, step):
        return lax.ppermute(x, "col", [(i, ring[step][i // 4] * 4 + i % 4) for i in range(col_size)])

    def along_x(x, step):
        return lax.ppermute(x, "col", [(i, i // 4 * 4 + ring[step][i % 4]) for i in range(col_size)])

    def exchange(x, axis):
        return lax.all_to_all(x, axis, 0, 0)

    lse, proj_t, src_t, tgt_t, aug = call(
        functools.partial(first_rows, copies=col_size),
        [f32(col_size, rows), bf16(width, rows), bf16(width, rows), bf16(width, cols), bf16(cols, 2 * width)],
        src_emb, tgt_emb, cost_factor, start,
    )
    parts = exchange(lse, "col")
    kernel_t, lse, shift, rho = call(
        functools.partial(first_columns, copies=row_size),
        [pltpu.VMEM((cols, rows), BF16), f32(row_size, cols), f32(1, cols), f32(1, rows)],
        parts, proj_t, aug, start,
        scratch=[pltpu.VMEM((cols, 2 * width), BF16), pltpu.VMEM((cols, 128), F32)],
    )
    parts = exchange(lse, "row")
    sums, weight, before = call(
        functools.partial(second_rows, src_count=src_count, tgt_count=tgt_count),
        [f32(col_size, rows), f32(1, cols), f32(1, cols)],
        parts, shift, kernel_t,
    )
    parts = exchange(sums, "col")
    sums, keep, send, scale, row_potential = call(
        functools.partial(second_columns, src_count=src_count),
        [f32(row_size, cols), f32(width // 2, cols), f32(width // 2, cols), f32(1, rows), f32(1, rows)],
        core, parts, rho, kernel_t, src_t, weight,
        scratch=[pltpu.VMEM((width + 16, cols), F32)], smem=1,
    )
    parts = exchange(sums, "row")
    out, col_potential, gain = call(
        functools.partial(target_sums, src_count=src_count, tgt_count=tgt_count),
        [f32(col_size, width, share), f32(1, cols), f32(1, cols)],
        parts, weight, before, tgt_t, kernel_t, scale,
    )
    bary_src, = call(finish_targets, [bf16(share, width)], exchange(out, "col"))

    half = keep + swap(send)
    half = half + along_y(half, 0)
    half = half + along_y(half, 1)
    other = swap(half)
    first = core[0] == 0
    low = jnp.where(first, half, other)
    high = jnp.where(first, other, half)
    moment, bary_tgt = call(
        functools.partial(finish_sources, tgt_count=tgt_count),
        [f32(width, width), bf16(cols, width)],
        low, high, gain, tgt_emb,
    )
    for step in range(2):
        moment = moment + along_z(moment, step)
    for step in range(2):
        moment = moment + along_x(moment, step)
    return (bary_src, bary_tgt, moment, row_potential.reshape(rows), col_potential.reshape(cols))


def solution(mesh):
    placed = (P("row", None), P("col", None), P(), P("col"))
    return jax.shard_map(
        local,
        mesh=mesh,
        in_specs=placed,
        out_specs=(P(("row", "col"), None), P("col", None), P(), P("row"), P("col")),
        check_vma=False,
    )
```

```python
import functools
import math

import jax
import jax.numpy as jnp
from jax import lax
from jax.experimental import pallas as pl
from jax.experimental.pallas import tpu as pltpu
from jax.sharding import PartitionSpec as P

F32 = jnp.float32
BF16 = jnp.bfloat16
NT = (((1,), (1,)), ((), ()))
TINY = 2.0**-80
BLK = 512
CHUNK = 256
SLABS = BLK // 128
VMEM_LIMIT = 24 * 1024 * 1024


def split3(x):
    hi = x.astype(BF16).astype(F32)
    mid = (x - hi).astype(BF16).astype(F32)
    lo = (x - hi - mid).astype(BF16).astype(F32)
    return hi, mid, lo


def iota(shape, dim):
    return lax.broadcasted_iota(jnp.int32, shape, dim)


def lanes(b, size):
    if isinstance(b, int):
        return slice(b * size, (b + 1) * size)
    return pl.ds(pl.multiple_of(b * size, size), size)


def aug_columns(shift):
    hi, mid, lo = split3(shift)
    lane = iota((shift.shape[0], 128), 1)
    out = jnp.where(lane < 3, 1.0, 0.0)
    out = jnp.where(lane == 3, hi, out)
    out = jnp.where(lane == 4, mid, out)
    out = jnp.where(lane == 5, lo, out)
    return out.astype(BF16)


def aug_rows(term):
    hi, mid, lo = split3(term)
    sub = iota((16, term.shape[1]), 0)
    out = jnp.where((sub >= 3) & (sub < 6), 1.0, 0.0)
    out = jnp.where(sub == 0, hi, out)
    out = jnp.where(sub == 1, mid, out)
    out = jnp.where(sub == 2, lo, out)
    zeros = jnp.zeros((112, term.shape[1]), BF16)
    return jnp.concatenate([out.astype(BF16), zeros], axis=0)


def log_sum(x):
    largest = jnp.max(x, axis=0, keepdims=True)
    return largest + jnp.log(jnp.sum(jnp.exp(x - largest), axis=0, keepdims=True))


def flat(x):
    return jnp.concatenate([x[i : i + 1, :] for i in range(x.shape[0])], axis=1)


def stack(x, width):
    return jnp.concatenate([x[:, i * width : (i + 1) * width] for i in range(x.shape[1] // width)], axis=0)


def column(x):
    return jnp.broadcast_to(x, (8, x.shape[1])).T[:, :1]


def identity(n):
    return jnp.where(iota((n, n), 0) == iota((n, n), 1), 1.0, 0.0).astype(BF16)


def first_rows(src_in, tgt_in, factor_in, start_in, lse, proj_t, aug, src, factor, start, sems):
    copies = [
        pltpu.make_async_copy(factor_in, factor, sems.at[0]),
        pltpu.make_async_copy(src_in, src, sems.at[1]),
        pltpu.make_async_copy(start_in, start, sems.at[2]),
        pltpu.make_async_copy(tgt_in, aug.at[:, pl.ds(0, 128)], sems.at[3]),
    ]
    for copy in copies:
        copy.start()
    under = aug_rows(jnp.zeros((1, BLK), F32))
    for copy in copies:
        copy.wait()
    factor_t = factor[...].astype(F32).T.astype(BF16)
    proj_t[...] = lax.dot_general(factor_t, src[...], NT, preferred_element_type=F32).astype(BF16)
    aug[:, 128:] = aug_columns(column(flat(start[...])))
    values = []
    for b in range(src.shape[0] // BLK):
        right = jnp.concatenate([proj_t[:, b * BLK : (b + 1) * BLK], under], axis=0)
        largest = jnp.full((8, BLK), -jnp.inf, F32)
        total = jnp.zeros((8, BLK), F32)
        for c in range(aug.shape[0] // CHUNK):
            x = jnp.dot(aug[c * CHUNK : (c + 1) * CHUNK, :], right, preferred_element_type=F32)
            x = x.reshape(CHUNK // 8, 8, BLK)
            new = jnp.maximum(largest, jnp.max(x, axis=0))
            total = total * jnp.exp(largest - new) + jnp.sum(jnp.exp(x - new[None]), axis=0)
            largest = new
        top = jnp.max(largest, axis=0, keepdims=True)
        values.append(top + jnp.log(jnp.sum(total * jnp.exp(largest - top), axis=0, keepdims=True)))
    lse[...] = jnp.broadcast_to(jnp.concatenate([stack(v, 128) for v in values], axis=0)[None], lse.shape)


def transposes(src, tgt, src_t, tgt_t):
    eye = identity(128)
    tgt_t[...] = lax.dot_general(eye, tgt[...], NT, preferred_element_type=F32).astype(BF16)
    src_t[...] = lax.dot_general(eye, src[...], NT, preferred_element_type=F32).astype(BF16)


def first_columns(parts, proj_t, aug, start, kernel_t, lse, shift, rho, sums, spare):
    blocks = proj_t.shape[1] // BLK
    chunks = aug.shape[0] // CHUNK
    rho[...] = -log_sum(parts[...])[0]
    shift[...] = start[...]

    def right_of(b):
        term = jnp.concatenate([rho[pl.ds(b * SLABS + i, 1), :] for i in range(SLABS)], axis=1)
        return jnp.concatenate([proj_t[:, lanes(b, BLK)], aug_rows(term)], axis=0)

    def fold(x, op):
        out = x[:, :128]
        for i in range(1, BLK // 128):
            out = op(out, x[:, i * 128 : (i + 1) * 128])
        return out

    def fill(left, b):
        right = right_of(b)
        for c in range(chunks):
            rows = slice(c * CHUNK, (c + 1) * CHUNK)
            e = jnp.exp(jnp.dot(left[rows, :], right, preferred_element_type=F32))
            for i in range(SLABS):
                kernel_t[b * SLABS + i, rows, :] = e[:, i * 128 : (i + 1) * 128].astype(BF16)
            sums[rows, :] += fold(e, jnp.add)

    def column_sums():
        return stack(jnp.sum(sums[...].T, axis=0, keepdims=True), 128)

    sums[...] = jnp.zeros_like(sums)
    for b in range(blocks):
        fill(aug, b)
    total = column_sums()
    lse[...] = jnp.broadcast_to((jnp.log(total) - shift[...])[None], lse.shape)

    @pl.when(jnp.min(total) < TINY)
    def _():
        sums[...] = jnp.full(sums.shape, -jnp.inf, F32)

        def largest(b, carry):
            right = right_of(b)
            for c in range(chunks):
                rows = slice(c * CHUNK, (c + 1) * CHUNK)
                x = jnp.dot(aug[rows, :], right, preferred_element_type=F32)
                sums[rows, :] = jnp.maximum(sums[rows, :], fold(x, jnp.maximum))
            return carry

        lax.fori_loop(0, blocks, largest, 0)
        top = jnp.max(sums[...], axis=1, keepdims=True)
        spare[:, :128] = aug[:, :128]
        spare[:, 128:] = aug_columns(column(flat(start[...])) - top)
        shift[...] = start[...] - stack(jnp.broadcast_to(top, sums.shape).T[:1], 128)
        sums[...] = jnp.zeros_like(sums)

        def again(b, carry):
            fill(spare, b)
            return carry

        lax.fori_loop(0, blocks, again, 0)
        lse[...] = jnp.broadcast_to((jnp.log(column_sums()) - shift[...])[None], lse.shape)


def slabs(ref, first, count):
    return jnp.concatenate([ref[first + i] for i in range(count)], axis=1)


def second_rows(parts, shift, kernel_t, sums, weight, potential, *, src_count, tgt_count):
    total = log_sum(parts[...])[0]
    potential[...] = math.log(src_count) - math.log(tgt_count) - total
    w = jnp.exp(-math.log(tgt_count) - total - shift[...])
    weight[...] = w
    w = flat(w)
    hi = w.astype(BF16).astype(F32)
    sub = iota((16, w.shape[1]), 0)
    left = jnp.where(sub == 0, hi, jnp.where(sub == 1, w - hi, 0.0)).astype(BF16)
    values = []
    for b in range(kernel_t.shape[0] // SLABS):
        x = jnp.dot(left, slabs(kernel_t, b * SLABS, SLABS), preferred_element_type=F32)
        values.append(stack(x[:1] + x[1:2], 128))
    sums[...] = jnp.broadcast_to(jnp.concatenate(values, axis=0)[None], sums.shape)


def second_columns(parts, rho, kernel_t, src_t, weight, sums, keep, send, scale, potential, total, *, src_count):
    q = jnp.sum(parts[...], axis=0)
    u = 1.0 / (src_count * q)
    scale[...] = u
    potential[...] = rho[...] - 2.0 * math.log(src_count) - jnp.log(q)
    for b in range(kernel_t.shape[0] // SLABS):
        ub = flat(u[b * SLABS : (b + 1) * SLABS, :])
        hi = ub.astype(BF16).astype(F32)
        sub = iota((16, BLK), 0)
        low = jnp.where(sub == 0, hi, jnp.where(sub == 1, ub - hi, 0.0)).astype(BF16)
        scaled = (src_t[:, b * BLK : (b + 1) * BLK].astype(F32) * ub).astype(BF16)
        left = jnp.concatenate([scaled, low], axis=0)
        x = lax.dot_general(left, slabs(kernel_t, b * SLABS, SLABS), NT, preferred_element_type=F32)
        if b == 0:
            total[...] = x
        else:
            total[...] += x
    w = weight[...]
    sums[...] = jnp.broadcast_to((w * stack(total[128:129, :] + total[129:130, :], 128))[None], sums.shape)
    w = flat(w)
    half = keep.shape[0]
    own = lax.rem(lax.axis_index("row"), 2) * half
    keep[...] = total[pl.ds(pl.multiple_of(own, half), half), :] * w
    send[...] = total[pl.ds(pl.multiple_of(half - own, half), half), :] * w


def share_of(major, minor):
    col = lax.axis_index("col")
    return ((col // 4) ^ major) * 4 + ((col % 4) ^ minor)


def halves(offsets):
    first = [2 * share_of(a, b) for a in offsets for b in range(4)]
    second = [2 * share_of(b, a) + 1 for a in offsets for b in range(4)]
    return first + second


def mix(left, kernel_t, scale, held, sems, outs, offsets, src_count):
    places = halves(offsets)
    copies = [pltpu.make_async_copy(kernel_t.at[at], held.at[k], sems.at[k]) for k, at in enumerate(places)]
    for copy in copies:
        copy.start()
    factor = left()
    for copy in copies:
        copy.wait()
    for k in range(0, len(places), 2):
        x = jnp.dot(factor, slabs(held, k, 2), preferred_element_type=F32)
        for i in range(2):
            out = outs[(k + i) // 8]
            out[(k + i) % 8] = x[:, i * 128 : (i + 1) * 128] * (scale[pl.ds(places[k + i], 1), :] * src_count)


def target_send(
    parts, weight, before, tgt_t, kernel_t, scale, out_a, out_b, left, potential, gain, held, sems, *, src_count, tgt_count
):
    def factor():
        total = jnp.sum(parts[...], axis=0)
        g = 1.0 / (tgt_count * total)
        gain[...] = g
        potential[...] = before[...] - math.log(tgt_count) - jnp.log(total)
        value = (tgt_t[...].astype(F32) * flat(weight[...] * g)).astype(BF16)
        left[...] = value
        return value

    mix(factor, kernel_t, scale, held, sems, (out_a, out_b), (1, 2), src_count)


def target_keep(left, kernel_t, scale, out_a, out_b, held, sems, *, src_count):
    mix(lambda: left[...], kernel_t, scale, held, sems, (out_a, out_b), (0, 3), src_count)


def finish_sources(mine, other, gain, tgt, moment, out, *, tgt_count):
    even = lax.rem(lax.axis_index("row"), 2) == 0
    low = jnp.where(even, mine[...], other[...])
    high = jnp.where(even, other[...], mine[...])
    full = jnp.concatenate([low, high], axis=0) * flat(gain[...])
    moment[...] = jnp.dot(
        full, tgt[...].astype(F32), precision=lax.Precision.HIGHEST, preferred_element_type=F32
    )
    out[...] = (full * tgt_count).T.astype(BF16)


def merge_first(keep_a, got_a, keep_b, got_b, moment, send_a, hold_a, send_b, hold_b):
    for i, (keep, got, send, hold) in enumerate(((keep_a, got_a, send_a, hold_a), (keep_b, got_b, send_b, hold_b))):
        for k in range(4):
            hold[k] = keep[k] + got[k]
            send[k * 128 : (k + 1) * 128, :] = keep[4 + k] + got[4 + k]
        send[512:576, :] = moment[i * 64 : (i + 1) * 64, :]


def merge_second(hold_a, sent_a, got_a, hold_b, sent_b, got_b, send_a, next_a, send_b, next_b):
    for hold, sent, got, send, after in (
        (hold_a, sent_a, got_a, send_a, next_a),
        (hold_b, sent_b, got_b, send_b, next_b),
    ):
        for k in range(4):
            value = hold[k] + got[k * 128 : (k + 1) * 128, :]
            if k in (1, 2):
                send[(k - 1) * 128 : k * 128, :] = value
            else:
                after[k // 3] = value
        send[256:320, :] = sent[512:576, :] + got[512:576, :]


def merge_third(hold_a, sent_a, got_a, hold_b, sent_b, got_b, send_a, next_a, send_b, next_b):
    for hold, sent, got, send, after in (
        (hold_a, sent_a, got_a, send_a, next_a),
        (hold_b, sent_b, got_b, send_b, next_b),
    ):
        after[...] = hold[0] + got[:128, :]
        send[:128, :] = hold[1] + got[128:256, :]
        send[128:192, :] = sent[256:320, :] + got[256:320, :]


def merge_last(hold_a, sent_a, got_a, hold_b, sent_b, got_b, bary, moment_a, moment_b):
    bary[:128, :] = (hold_a[...] + got_a[:128, :]).T.astype(BF16)
    bary[128:, :] = (hold_b[...] + got_b[:128, :]).T.astype(BF16)
    moment_a[...] = sent_a[128:192, :] + got_a[128:192, :]
    moment_b[...] = sent_b[128:192, :] + got_b[128:192, :]


def call(body, outs, *args, scratch=(), spaces=None):
    spaces = spaces or {}
    return pl.pallas_call(
        body,
        out_shape=outs,
        in_specs=[pl.BlockSpec(memory_space=spaces.get(i, pltpu.VMEM)) for i in range(len(args))],
        out_specs=jax.tree.map(lambda _: pl.BlockSpec(memory_space=pltpu.VMEM), outs),
        scratch_shapes=list(scratch),
        compiler_params=pltpu.CompilerParams(vmem_limit_bytes=VMEM_LIMIT),
    )(*args)


def f32(*shape):
    return jax.ShapeDtypeStruct(shape, F32)


def bf16(*shape):
    return jax.ShapeDtypeStruct(shape, BF16)


def near(x):
    return pltpu.with_memory_space_constraint(x, pltpu.VMEM)


def far(x):
    return pltpu.with_memory_space_constraint(x, pltpu.HBM)


def local(src_emb, tgt_emb, cost_factor, col_start):
    rows, cols = src_emb.shape[0], tgt_emb.shape[0]
    width = src_emb.shape[1]
    row_size, col_size = lax.axis_size("row"), lax.axis_size("col")
    src_count, tgt_count = rows * row_size, cols * col_size
    counts = dict(src_count=src_count, tgt_count=tgt_count)
    share = rows // col_size
    row_shape, col_shape = (rows // 128, 128), (cols // 128, 128)
    start = col_start.reshape(col_shape)

    def swap(x):
        return lax.ppermute(x, "row", [(i, i ^ 1) for i in range(row_size)])

    def along_y(x, k):
        return lax.ppermute(x, "row", [(i, i ^ (2 * k)) for i in range(row_size)])

    def along_z(x, k):
        return lax.ppermute(x, "col", [(i, i ^ (4 * k)) for i in range(col_size)])

    def along_x(x, k):
        return lax.ppermute(x, "col", [(i, i ^ k) for i in range(col_size)])

    def exchange(x, axis):
        return lax.all_to_all(x, axis, 0, 0)

    lse, proj_t, aug = call(
        first_rows,
        [f32(col_size, *row_shape), bf16(width, rows), bf16(cols, 2 * width)],
        far(src_emb), far(tgt_emb), far(cost_factor), far(start),
        scratch=[
            pltpu.VMEM((rows, width), BF16),
            pltpu.VMEM((width, width), BF16),
            pltpu.VMEM(col_shape, F32),
            pltpu.SemaphoreType.DMA((4,)),
        ],
        spaces={i: pltpu.HBM for i in range(4)},
    )
    parts = exchange(lse, "col")
    src_late, tgt_late, _ = lax.optimization_barrier((src_emb, tgt_emb, proj_t))
    src_t, tgt_t = call(transposes, [bf16(width, rows), bf16(width, cols)], src_late, tgt_late)
    parts, src_t, tgt_t = lax.optimization_barrier((parts, src_t, tgt_t))
    kernel_t, lse, shift, rho = call(
        first_columns,
        [pltpu.VMEM((rows // 128, cols, 128), BF16), f32(row_size, *col_shape), f32(*col_shape), f32(*row_shape)],
        parts, proj_t, aug, start,
        scratch=[pltpu.VMEM((cols, 128), F32), pltpu.VMEM((cols, 2 * width), BF16)],
    )
    parts = exchange(lse, "row")
    sums, weight, before = call(
        functools.partial(second_rows, **counts),
        [f32(col_size, *row_shape), f32(*col_shape), f32(*col_shape)],
        parts, shift, near(kernel_t),
    )
    parts = exchange(sums, "col")
    sums, keep, send, scale, row_potential = call(
        functools.partial(second_columns, src_count=src_count),
        [f32(row_size, *col_shape), f32(width // 2, cols), f32(width // 2, cols), f32(*row_shape), f32(*row_shape)],
        parts, rho, near(kernel_t), src_t, weight,
        scratch=[pltpu.VMEM((width + 16, cols), F32)],
    )
    mine = keep + swap(send)
    sums, mine = lax.optimization_barrier((sums, mine))
    parts = exchange(sums, "row")
    mine = mine + along_y(mine, 1)
    parts, mine = lax.optimization_barrier((parts, mine))
    arrived = along_y(mine, 3)
    held = [pltpu.VMEM((16, cols, 128), BF16), pltpu.SemaphoreType.DMA((16,))]
    message = f32(8, width, 128)
    send_a, send_b, left, col_potential, gain = call(
        functools.partial(target_send, **counts),
        [message, message, bf16(width, cols), f32(*col_shape), f32(*col_shape)],
        parts, weight, before, tgt_t, far(kernel_t), scale,
        scratch=held, spaces={4: pltpu.HBM},
    )
    got_a, got_b = along_z(send_a, 1), along_x(send_b, 1)
    keep_a, keep_b = call(
        functools.partial(target_keep, src_count=src_count),
        [message, message],
        left, far(kernel_t), scale,
        scratch=held, spaces={1: pltpu.HBM},
    )
    mine, gain = lax.optimization_barrier((mine, gain))
    mine = mine + arrived
    moment, bary_tgt = call(
        functools.partial(finish_sources, tgt_count=tgt_count),
        [f32(width, width), bf16(cols, width)],
        mine, swap(mine), gain, tgt_emb,
    )
    send_a, hold_a, send_b, hold_b = call(
        merge_first, [f32(576, 128), f32(4, 128, 128)] * 2, keep_a, got_a, keep_b, got_b, moment
    )
    got_a, got_b = along_z(send_a, 3), along_x(send_b, 3)
    send_a, hold_a, send_b, hold_b = call(
        merge_second, [f32(320, 128), f32(2, 128, 128)] * 2, hold_a, send_a, got_a, hold_b, send_b, got_b
    )
    got_a, got_b = along_x(send_a, 1), along_z(send_b, 1)
    send_a, hold_a, send_b, hold_b = call(
        merge_third, [f32(192, 128), f32(128, 128)] * 2, hold_a, send_a, got_a, hold_b, send_b, got_b
    )
    got_a, got_b = along_x(send_a, 3), along_z(send_b, 3)
    bary_src, moment_a, moment_b = call(
        merge_last,
        [bf16(share, width), f32(64, 128), f32(64, 128)],
        hold_a, send_a, got_a, hold_b, send_b, got_b,
    )
    moment = jnp.concatenate([moment_a + along_z(moment_a, 1), moment_b + along_x(moment_b, 1)], axis=0)
    return (bary_src, bary_tgt, moment, row_potential.reshape(rows), col_potential.reshape(cols))


def solution(mesh):
    placed = (P("row", None), P("col", None), P(), P("col"))
    return jax.shard_map(
        local,
        mesh=mesh,
        in_specs=placed,
        out_specs=(P(("row", "col"), None), P("col", None), P(), P("row"), P("col")),
        check_vma=False,
    )
```

```python
import functools
import math

import jax
import jax.numpy as jnp
from jax import lax
from jax.experimental import pallas as pl
from jax.experimental.pallas import tpu as pltpu
from jax.sharding import PartitionSpec as P

F32 = jnp.float32
BF16 = jnp.bfloat16
NT = (((1,), (1,)), ((), ()))
TINY = 2.0**-80
BLK = 512
CHUNK = 256
SLABS = BLK // 128
VMEM_LIMIT = 24 * 1024 * 1024


def split3(x):
    hi = x.astype(BF16).astype(F32)
    mid = (x - hi).astype(BF16).astype(F32)
    lo = (x - hi - mid).astype(BF16).astype(F32)
    return hi, mid, lo


def iota(shape, dim):
    return lax.broadcasted_iota(jnp.int32, shape, dim)


def lanes(b, size):
    if isinstance(b, int):
        return slice(b * size, (b + 1) * size)
    return pl.ds(pl.multiple_of(b * size, size), size)


def aug_columns(shift):
    hi, mid, lo = split3(shift)
    lane = iota((shift.shape[0], 128), 1)
    out = jnp.where(lane < 3, 1.0, 0.0)
    out = jnp.where(lane == 3, hi, out)
    out = jnp.where(lane == 4, mid, out)
    out = jnp.where(lane == 5, lo, out)
    return out.astype(BF16)


def aug_rows(term):
    hi, mid, lo = split3(term)
    sub = iota((16, term.shape[1]), 0)
    out = jnp.where((sub >= 3) & (sub < 6), 1.0, 0.0)
    out = jnp.where(sub == 0, hi, out)
    out = jnp.where(sub == 1, mid, out)
    out = jnp.where(sub == 2, lo, out)
    zeros = jnp.zeros((112, term.shape[1]), BF16)
    return jnp.concatenate([out.astype(BF16), zeros], axis=0)


def log_sum(x):
    largest = jnp.max(x, axis=0, keepdims=True)
    return largest + jnp.log(jnp.sum(jnp.exp(x - largest), axis=0, keepdims=True))


def flat(x):
    return jnp.concatenate([x[i : i + 1, :] for i in range(x.shape[0])], axis=1)


def stack(x, width):
    return jnp.concatenate([x[:, i * width : (i + 1) * width] for i in range(x.shape[1] // width)], axis=0)


def column(x):
    return jnp.broadcast_to(x, (8, x.shape[1])).T[:, :1]


def identity(n):
    return jnp.where(iota((n, n), 0) == iota((n, n), 1), 1.0, 0.0).astype(BF16)


def first_rows(src_in, tgt_in, factor_in, start_in, lse, proj_t, aug, start, src, factor, sems):
    copies = [
        pltpu.make_async_copy(factor_in, factor, sems.at[0]),
        pltpu.make_async_copy(src_in, src, sems.at[1]),
        pltpu.make_async_copy(start_in, start, sems.at[2]),
        pltpu.make_async_copy(tgt_in, aug.at[:, pl.ds(0, 128)], sems.at[3]),
    ]
    for copy in copies:
        copy.start()
    under = aug_rows(jnp.zeros((1, BLK), F32))
    for copy in copies:
        copy.wait()
    factor_t = factor[...].astype(F32).T.astype(BF16)
    proj_t[...] = lax.dot_general(factor_t, src[...], NT, preferred_element_type=F32).astype(BF16)
    aug[:, 128:] = aug_columns(column(flat(start[...])))
    values = []
    for b in range(src.shape[0] // BLK):
        right = jnp.concatenate([proj_t[:, b * BLK : (b + 1) * BLK], under], axis=0)
        largest = jnp.full((8, BLK), -jnp.inf, F32)
        total = jnp.zeros((8, BLK), F32)
        for c in range(aug.shape[0] // CHUNK):
            x = jnp.dot(aug[c * CHUNK : (c + 1) * CHUNK, :], right, preferred_element_type=F32)
            x = x.reshape(CHUNK // 8, 8, BLK)
            new = jnp.maximum(largest, jnp.max(x, axis=0))
            total = total * jnp.exp(largest - new) + jnp.sum(jnp.exp(x - new[None]), axis=0)
            largest = new
        top = jnp.max(largest, axis=0, keepdims=True)
        values.append(top + jnp.log(jnp.sum(total * jnp.exp(largest - top), axis=0, keepdims=True)))
    lse[...] = jnp.broadcast_to(jnp.concatenate([stack(v, 128) for v in values], axis=0)[None], lse.shape)


def transposes(src, tgt, src_t, tgt_t):
    eye = identity(128)
    tgt_t[...] = lax.dot_general(eye, tgt[...], NT, preferred_element_type=F32).astype(BF16)
    src_t[...] = lax.dot_general(eye, src[...], NT, preferred_element_type=F32).astype(BF16)


def first_columns(parts, proj_t, aug, start, kernel_t, lse, shift, rho, sums, spare):
    blocks = proj_t.shape[1] // BLK
    chunks = aug.shape[0] // CHUNK
    rho[...] = -log_sum(parts[...])[0]
    shift[...] = start[...]

    def right_of(b):
        term = jnp.concatenate([rho[pl.ds(b * SLABS + i, 1), :] for i in range(SLABS)], axis=1)
        return jnp.concatenate([proj_t[:, lanes(b, BLK)], aug_rows(term)], axis=0)

    def fold(x, op):
        out = x[:, :128]
        for i in range(1, BLK // 128):
            out = op(out, x[:, i * 128 : (i + 1) * 128])
        return out

    def fill(left, b):
        right = right_of(b)
        for c in range(chunks):
            rows = slice(c * CHUNK, (c + 1) * CHUNK)
            e = jnp.exp(jnp.dot(left[rows, :], right, preferred_element_type=F32))
            for i in range(SLABS):
                kernel_t[b * SLABS + i, rows, :] = e[:, i * 128 : (i + 1) * 128].astype(BF16)
            sums[rows, :] += fold(e, jnp.add)

    def column_sums():
        return stack(jnp.sum(sums[...].T, axis=0, keepdims=True), 128)

    sums[...] = jnp.zeros_like(sums)
    for b in range(blocks):
        fill(aug, b)
    total = column_sums()
    lse[...] = jnp.broadcast_to((jnp.log(total) - shift[...])[None], lse.shape)

    @pl.when(jnp.min(total) < TINY)
    def _():
        sums[...] = jnp.full(sums.shape, -jnp.inf, F32)

        def largest(b, carry):
            right = right_of(b)
            for c in range(chunks):
                rows = slice(c * CHUNK, (c + 1) * CHUNK)
                x = jnp.dot(aug[rows, :], right, preferred_element_type=F32)
                sums[rows, :] = jnp.maximum(sums[rows, :], fold(x, jnp.maximum))
            return carry

        lax.fori_loop(0, blocks, largest, 0)
        top = jnp.max(sums[...], axis=1, keepdims=True)
        spare[:, :128] = aug[:, :128]
        spare[:, 128:] = aug_columns(column(flat(start[...])) - top)
        shift[...] = start[...] - stack(jnp.broadcast_to(top, sums.shape).T[:1], 128)
        sums[...] = jnp.zeros_like(sums)

        def again(b, carry):
            fill(spare, b)
            return carry

        lax.fori_loop(0, blocks, again, 0)
        lse[...] = jnp.broadcast_to((jnp.log(column_sums()) - shift[...])[None], lse.shape)


def slabs(ref, first, count):
    return jnp.concatenate([ref[first + i] for i in range(count)], axis=1)


def second_rows(parts, shift, kernel_t, sums, weight, potential, *, src_count, tgt_count):
    total = log_sum(parts[...])[0]
    potential[...] = math.log(src_count) - math.log(tgt_count) - total
    w = jnp.exp(-math.log(tgt_count) - total - shift[...])
    weight[...] = w
    w = flat(w)
    hi = w.astype(BF16).astype(F32)
    sub = iota((16, w.shape[1]), 0)
    left = jnp.where(sub == 0, hi, jnp.where(sub == 1, w - hi, 0.0)).astype(BF16)
    values = []
    for b in range(kernel_t.shape[0] // SLABS):
        x = jnp.dot(left, slabs(kernel_t, b * SLABS, SLABS), preferred_element_type=F32)
        values.append(stack(x[:1] + x[1:2], 128))
    sums[...] = jnp.broadcast_to(jnp.concatenate(values, axis=0)[None], sums.shape)


def second_columns(parts, rho, kernel_t, src_t, weight, sums, keep, send, scale, potential, total, *, src_count):
    q = jnp.sum(parts[...], axis=0)
    u = 1.0 / (src_count * q)
    scale[...] = u
    potential[...] = rho[...] - 2.0 * math.log(src_count) - jnp.log(q)
    for b in range(kernel_t.shape[0] // SLABS):
        ub = flat(u[b * SLABS : (b + 1) * SLABS, :])
        hi = ub.astype(BF16).astype(F32)
        sub = iota((16, BLK), 0)
        low = jnp.where(sub == 0, hi, jnp.where(sub == 1, ub - hi, 0.0)).astype(BF16)
        scaled = (src_t[:, b * BLK : (b + 1) * BLK].astype(F32) * ub).astype(BF16)
        left = jnp.concatenate([scaled, low], axis=0)
        x = lax.dot_general(left, slabs(kernel_t, b * SLABS, SLABS), NT, preferred_element_type=F32)
        if b == 0:
            total[...] = x
        else:
            total[...] += x
    w = weight[...]
    sums[...] = jnp.broadcast_to((w * stack(total[128:129, :] + total[129:130, :], 128))[None], sums.shape)
    w = flat(w)
    half = keep.shape[0]
    own = lax.rem(lax.axis_index("row"), 2) * half
    keep[...] = total[pl.ds(pl.multiple_of(own, half), half), :] * w
    send[...] = total[pl.ds(pl.multiple_of(half - own, half), half), :] * w


def share_of(major, minor):
    col = lax.axis_index("col")
    return ((col // 4) ^ major) * 4 + ((col % 4) ^ minor)


def halves(offsets):
    first = [2 * share_of(a, b) for a in offsets for b in range(4)]
    second = [2 * share_of(b, a) + 1 for a in offsets for b in range(4)]
    return first + second


def mix(left, kernel_t, scale, outs, offsets, src_count):
    places = halves(offsets)
    for k in range(0, len(places), 2):
        pair = jnp.concatenate([kernel_t[places[k]], kernel_t[places[k + 1]]], axis=1)
        x = jnp.dot(left, pair, preferred_element_type=F32)
        for i in range(2):
            out = outs[(k + i) // 8]
            out[(k + i) % 8] = x[:, i * 128 : (i + 1) * 128] * (scale[pl.ds(places[k + i], 1), :] * src_count)


def target_send(
    parts, weight, before, tgt_t, kernel_t, scale, out_a, out_b, left, potential, gain, *, src_count, tgt_count
):
    total = jnp.sum(parts[...], axis=0)
    g = 1.0 / (tgt_count * total)
    gain[...] = g
    potential[...] = before[...] - math.log(tgt_count) - jnp.log(total)
    value = (tgt_t[...].astype(F32) * flat(weight[...] * g)).astype(BF16)
    left[...] = value
    mix(value, kernel_t, scale, (out_a, out_b), (1, 2), src_count)


def target_keep(left, kernel_t, scale, out_a, out_b, *, src_count):
    mix(left[...], kernel_t, scale, (out_a, out_b), (0, 3), src_count)


def finish_sources(mine, other, gain, tgt, moment, out, *, tgt_count):
    even = lax.rem(lax.axis_index("row"), 2) == 0
    low = jnp.where(even, mine[...], other[...])
    high = jnp.where(even, other[...], mine[...])
    full = jnp.concatenate([low, high], axis=0) * flat(gain[...])
    moment[...] = jnp.dot(
        full, tgt[...].astype(F32), precision=lax.Precision.HIGHEST, preferred_element_type=F32
    )
    out[...] = (full * tgt_count).T.astype(BF16)


def merge_first(keep_a, got_a, keep_b, got_b, moment, send_a, hold_a, send_b, hold_b):
    for i, (keep, got, send, hold) in enumerate(((keep_a, got_a, send_a, hold_a), (keep_b, got_b, send_b, hold_b))):
        for k in range(4):
            hold[k] = keep[k] + got[k]
            send[k * 128 : (k + 1) * 128, :] = keep[4 + k] + got[4 + k]
        send[512:576, :] = moment[i * 64 : (i + 1) * 64, :]


def merge_second(hold_a, sent_a, got_a, hold_b, sent_b, got_b, send_a, next_a, send_b, next_b):
    for hold, sent, got, send, after in (
        (hold_a, sent_a, got_a, send_a, next_a),
        (hold_b, sent_b, got_b, send_b, next_b),
    ):
        for k in range(4):
            value = hold[k] + got[k * 128 : (k + 1) * 128, :]
            if k in (1, 2):
                send[(k - 1) * 128 : k * 128, :] = value
            else:
                after[k // 3] = value
        send[256:320, :] = sent[512:576, :] + got[512:576, :]


def merge_third(hold_a, sent_a, got_a, hold_b, sent_b, got_b, send_a, next_a, send_b, next_b):
    for hold, sent, got, send, after in (
        (hold_a, sent_a, got_a, send_a, next_a),
        (hold_b, sent_b, got_b, send_b, next_b),
    ):
        after[...] = hold[0] + got[:128, :]
        send[:128, :] = hold[1] + got[128:256, :]
        send[128:192, :] = sent[256:320, :] + got[256:320, :]


def merge_last(hold_a, sent_a, got_a, hold_b, sent_b, got_b, bary, moment_a, moment_b):
    bary[:128, :] = (hold_a[...] + got_a[:128, :]).T.astype(BF16)
    bary[128:, :] = (hold_b[...] + got_b[:128, :]).T.astype(BF16)
    moment_a[...] = sent_a[128:192, :] + got_a[128:192, :]
    moment_b[...] = sent_b[128:192, :] + got_b[128:192, :]


def call(body, outs, *args, scratch=(), spaces=None):
    spaces = spaces or {}
    return pl.pallas_call(
        body,
        out_shape=outs,
        in_specs=[pl.BlockSpec(memory_space=spaces.get(i, pltpu.VMEM)) for i in range(len(args))],
        out_specs=jax.tree.map(lambda _: pl.BlockSpec(memory_space=pltpu.VMEM), outs),
        scratch_shapes=list(scratch),
        compiler_params=pltpu.CompilerParams(vmem_limit_bytes=VMEM_LIMIT),
    )(*args)


def f32(*shape):
    return jax.ShapeDtypeStruct(shape, F32)


def bf16(*shape):
    return jax.ShapeDtypeStruct(shape, BF16)


def near(x):
    return pltpu.with_memory_space_constraint(x, pltpu.VMEM)


def far(x):
    return pltpu.with_memory_space_constraint(x, pltpu.HBM)


def local(src_emb, tgt_emb, cost_factor, col_start):
    rows, cols = src_emb.shape[0], tgt_emb.shape[0]
    width = src_emb.shape[1]
    row_size, col_size = lax.axis_size("row"), lax.axis_size("col")
    src_count, tgt_count = rows * row_size, cols * col_size
    counts = dict(src_count=src_count, tgt_count=tgt_count)
    share = rows // col_size
    row_shape, col_shape = (rows // 128, 128), (cols // 128, 128)

    def swap(x):
        return lax.ppermute(x, "row", [(i, i ^ 1) for i in range(row_size)])

    def along_y(x, k):
        return lax.ppermute(x, "row", [(i, i ^ (2 * k)) for i in range(row_size)])

    def along_z(x, k):
        return lax.ppermute(x, "col", [(i, i ^ (4 * k)) for i in range(col_size)])

    def along_x(x, k):
        return lax.ppermute(x, "col", [(i, i ^ k) for i in range(col_size)])

    def exchange(x, axis):
        return lax.all_to_all(x, axis, 0, 0)

    lse, proj_t, aug, start = call(
        first_rows,
        [f32(col_size, *row_shape), bf16(width, rows), bf16(cols, 2 * width), f32(*col_shape)],
        far(src_emb), far(tgt_emb), far(cost_factor), far(col_start.reshape(col_shape)),
        scratch=[
            pltpu.VMEM((rows, width), BF16),
            pltpu.VMEM((width, width), BF16),
            pltpu.SemaphoreType.DMA((4,)),
        ],
        spaces={i: pltpu.HBM for i in range(4)},
    )
    parts = exchange(lse, "col")
    src_late, tgt_late, _ = lax.optimization_barrier((src_emb, tgt_emb, proj_t))
    src_t, tgt_t = call(transposes, [bf16(width, rows), bf16(width, cols)], src_late, tgt_late)
    parts, src_t, tgt_t = lax.optimization_barrier((parts, src_t, tgt_t))
    kernel_t, lse, shift, rho = call(
        first_columns,
        [pltpu.VMEM((rows // 128, cols, 128), BF16), f32(row_size, *col_shape), f32(*col_shape), f32(*row_shape)],
        parts, proj_t, aug, start,
        scratch=[pltpu.VMEM((cols, 128), F32), pltpu.VMEM((cols, 2 * width), BF16)],
    )
    parts = exchange(lse, "row")
    sums, weight, before = call(
        functools.partial(second_rows, **counts),
        [f32(col_size, *row_shape), f32(*col_shape), f32(*col_shape)],
        parts, shift, near(kernel_t),
    )
    parts = exchange(sums, "col")
    sums, keep, send, scale, row_potential = call(
        functools.partial(second_columns, src_count=src_count),
        [f32(row_size, *col_shape), f32(width // 2, cols), f32(width // 2, cols), f32(*row_shape), f32(*row_shape)],
        parts, rho, near(kernel_t), src_t, weight,
        scratch=[pltpu.VMEM((width + 16, cols), F32)],
    )
    mine = keep + swap(send)
    sums, mine = lax.optimization_barrier((sums, mine))
    parts = exchange(sums, "row")
    arrived = along_y(mine, 1)
    message = f32(8, width, 128)
    send_a, send_b, left, col_potential, gain = call(
        functools.partial(target_send, **counts),
        [message, message, bf16(width, cols), f32(*col_shape), f32(*col_shape)],
        parts, weight, before, tgt_t, near(kernel_t), scale,
    )
    got_a, got_b = along_z(send_a, 1), along_x(send_b, 1)
    keep_a, keep_b = call(
        functools.partial(target_keep, src_count=src_count),
        [message, message],
        left, near(kernel_t), scale,
    )
    mine, keep_a = lax.optimization_barrier((mine, keep_a))
    mine = mine + arrived
    mine = mine + along_y(mine, 3)
    moment, bary_tgt = call(
        functools.partial(finish_sources, tgt_count=tgt_count),
        [f32(width, width), bf16(cols, width)],
        mine, swap(mine), gain, tgt_emb,
    )
    send_a, hold_a, send_b, hold_b = call(
        merge_first, [f32(576, 128), f32(4, 128, 128)] * 2, keep_a, got_a, keep_b, got_b, moment
    )
    got_a, got_b = along_z(send_a, 3), along_x(send_b, 3)
    send_a, hold_a, send_b, hold_b = call(
        merge_second, [f32(320, 128), f32(2, 128, 128)] * 2, hold_a, send_a, got_a, hold_b, send_b, got_b
    )
    got_a, got_b = along_x(send_a, 1), along_z(send_b, 1)
    send_a, hold_a, send_b, hold_b = call(
        merge_third, [f32(192, 128), f32(128, 128)] * 2, hold_a, send_a, got_a, hold_b, send_b, got_b
    )
    got_a, got_b = along_x(send_a, 3), along_z(send_b, 3)
    bary_src, moment_a, moment_b = call(
        merge_last,
        [bf16(share, width), f32(64, 128), f32(64, 128)],
        hold_a, send_a, got_a, hold_b, send_b, got_b,
    )
    moment = jnp.concatenate([moment_a + along_z(moment_a, 1), moment_b + along_x(moment_b, 1)], axis=0)
    return (bary_src, bary_tgt, moment, row_potential.reshape(rows), col_potential.reshape(cols))


def solution(mesh):
    placed = (P("row", None), P("col", None), P(), P("col"))
    return jax.shard_map(
        local,
        mesh=mesh,
        in_specs=placed,
        out_specs=(P(("row", "col"), None), P("col", None), P(), P("row"), P("col")),
        check_vma=False,
    )
```

```python
import functools
import math

import jax
import jax.numpy as jnp
from jax import lax
from jax.experimental import pallas as pl
from jax.experimental.pallas import tpu as pltpu
from jax.sharding import PartitionSpec as P

F32 = jnp.float32
BF16 = jnp.bfloat16
NT = (((1,), (1,)), ((), ()))
TINY = 2.0**-80
BLK = 512
CHUNK = 256
SLABS = BLK // 128
VMEM_LIMIT = 24 * 1024 * 1024


def split3(x):
    hi = x.astype(BF16).astype(F32)
    mid = (x - hi).astype(BF16).astype(F32)
    lo = (x - hi - mid).astype(BF16).astype(F32)
    return hi, mid, lo


def iota(shape, dim):
    return lax.broadcasted_iota(jnp.int32, shape, dim)


def lanes(b, size):
    if isinstance(b, int):
        return slice(b * size, (b + 1) * size)
    return pl.ds(pl.multiple_of(b * size, size), size)


def aug_columns(shift):
    hi, mid, lo = split3(shift)
    lane = iota((shift.shape[0], 128), 1)
    out = jnp.where(lane < 3, 1.0, 0.0)
    out = jnp.where(lane == 3, hi, out)
    out = jnp.where(lane == 4, mid, out)
    out = jnp.where(lane == 5, lo, out)
    return out.astype(BF16)


def aug_rows(term):
    hi, mid, lo = split3(term)
    sub = iota((16, term.shape[1]), 0)
    out = jnp.where((sub >= 3) & (sub < 6), 1.0, 0.0)
    out = jnp.where(sub == 0, hi, out)
    out = jnp.where(sub == 1, mid, out)
    out = jnp.where(sub == 2, lo, out)
    zeros = jnp.zeros((112, term.shape[1]), BF16)
    return jnp.concatenate([out.astype(BF16), zeros], axis=0)


def log_sum(x):
    largest = jnp.max(x, axis=0, keepdims=True)
    return largest + jnp.log(jnp.sum(jnp.exp(x - largest), axis=0, keepdims=True))


def flat(x):
    return jnp.concatenate([x[i : i + 1, :] for i in range(x.shape[0])], axis=1)


def stack(x, width):
    return jnp.concatenate([x[:, i * width : (i + 1) * width] for i in range(x.shape[1] // width)], axis=0)


def column(x):
    return jnp.broadcast_to(x, (8, x.shape[1])).T[:, :1]


def identity(n):
    return jnp.where(iota((n, n), 0) == iota((n, n), 1), 1.0, 0.0).astype(BF16)


def first_rows(src_in, tgt_in, factor_in, start_in, lse, proj_t, aug, start, src, factor, sems):
    copies = [
        pltpu.make_async_copy(factor_in, factor, sems.at[0]),
        pltpu.make_async_copy(src_in, src, sems.at[1]),
        pltpu.make_async_copy(start_in, start, sems.at[2]),
        pltpu.make_async_copy(tgt_in, aug.at[:, pl.ds(0, 128)], sems.at[3]),
    ]
    for copy in copies:
        copy.start()
    under = aug_rows(jnp.zeros((1, BLK), F32))
    for copy in copies:
        copy.wait()
    factor_t = factor[...].astype(F32).T.astype(BF16)
    proj_t[...] = lax.dot_general(factor_t, src[...], NT, preferred_element_type=F32).astype(BF16)
    aug[:, 128:] = aug_columns(column(flat(start[...])))
    values = []
    for b in range(src.shape[0] // BLK):
        right = jnp.concatenate([proj_t[:, b * BLK : (b + 1) * BLK], under], axis=0)
        largest = jnp.full((8, BLK), -jnp.inf, F32)
        total = jnp.zeros((8, BLK), F32)
        for c in range(aug.shape[0] // CHUNK):
            x = jnp.dot(aug[c * CHUNK : (c + 1) * CHUNK, :], right, preferred_element_type=F32)
            x = x.reshape(CHUNK // 8, 8, BLK)
            new = jnp.maximum(largest, jnp.max(x, axis=0))
            total = total * jnp.exp(largest - new) + jnp.sum(jnp.exp(x - new[None]), axis=0)
            largest = new
        top = jnp.max(largest, axis=0, keepdims=True)
        values.append(top + jnp.log(jnp.sum(total * jnp.exp(largest - top), axis=0, keepdims=True)))
    lse[...] = jnp.broadcast_to(jnp.concatenate([stack(v, 128) for v in values], axis=0)[None], lse.shape)


def transposes(src, tgt, src_t, tgt_t):
    eye = identity(128)
    tgt_t[...] = lax.dot_general(eye, tgt[...], NT, preferred_element_type=F32).astype(BF16)
    src_t[...] = lax.dot_general(eye, src[...], NT, preferred_element_type=F32).astype(BF16)


def first_columns(parts, proj_t, aug, start, kernel_t, lse, shift, rho, sums, spare):
    blocks = proj_t.shape[1] // BLK
    chunks = aug.shape[0] // CHUNK
    rho[...] = -log_sum(parts[...])[0]
    shift[...] = start[...]

    def right_of(b):
        term = jnp.concatenate([rho[pl.ds(b * SLABS + i, 1), :] for i in range(SLABS)], axis=1)
        return jnp.concatenate([proj_t[:, lanes(b, BLK)], aug_rows(term)], axis=0)

    def fold(x, op):
        out = x[:, :128]
        for i in range(1, BLK // 128):
            out = op(out, x[:, i * 128 : (i + 1) * 128])
        return out

    def fill(left, b):
        right = right_of(b)
        for c in range(chunks):
            rows = slice(c * CHUNK, (c + 1) * CHUNK)
            e = jnp.exp(jnp.dot(left[rows, :], right, preferred_element_type=F32))
            for i in range(SLABS):
                kernel_t[b * SLABS + i, rows, :] = e[:, i * 128 : (i + 1) * 128].astype(BF16)
            sums[rows, :] += fold(e, jnp.add)

    def column_sums():
        return stack(jnp.sum(sums[...].T, axis=0, keepdims=True), 128)

    sums[...] = jnp.zeros_like(sums)
    for b in range(blocks):
        fill(aug, b)
    total = column_sums()
    lse[...] = jnp.broadcast_to((jnp.log(total) - shift[...])[None], lse.shape)

    @pl.when(jnp.min(total) < TINY)
    def _():
        sums[...] = jnp.full(sums.shape, -jnp.inf, F32)

        def largest(b, carry):
            right = right_of(b)
            for c in range(chunks):
                rows = slice(c * CHUNK, (c + 1) * CHUNK)
                x = jnp.dot(aug[rows, :], right, preferred_element_type=F32)
                sums[rows, :] = jnp.maximum(sums[rows, :], fold(x, jnp.maximum))
            return carry

        lax.fori_loop(0, blocks, largest, 0)
        top = jnp.max(sums[...], axis=1, keepdims=True)
        spare[:, :128] = aug[:, :128]
        spare[:, 128:] = aug_columns(column(flat(start[...])) - top)
        shift[...] = start[...] - stack(jnp.broadcast_to(top, sums.shape).T[:1], 128)
        sums[...] = jnp.zeros_like(sums)

        def again(b, carry):
            fill(spare, b)
            return carry

        lax.fori_loop(0, blocks, again, 0)
        lse[...] = jnp.broadcast_to((jnp.log(column_sums()) - shift[...])[None], lse.shape)


def slabs(ref, first, count):
    return jnp.concatenate([ref[first + i] for i in range(count)], axis=1)


def second_rows(parts, shift, kernel_t, sums, weight, potential, *, src_count, tgt_count):
    total = log_sum(parts[...])[0]
    potential[...] = math.log(src_count) - math.log(tgt_count) - total
    w = jnp.exp(-math.log(tgt_count) - total - shift[...])
    weight[...] = w
    w = flat(w)
    hi = w.astype(BF16).astype(F32)
    sub = iota((16, w.shape[1]), 0)
    left = jnp.where(sub == 0, hi, jnp.where(sub == 1, w - hi, 0.0)).astype(BF16)
    values = []
    for b in range(kernel_t.shape[0] // SLABS):
        x = jnp.dot(left, slabs(kernel_t, b * SLABS, SLABS), preferred_element_type=F32)
        values.append(stack(x[:1] + x[1:2], 128))
    sums[...] = jnp.broadcast_to(jnp.concatenate(values, axis=0)[None], sums.shape)


def second_columns(parts, rho, kernel_t, src_t, weight, sums, keep, send, scale, potential, total, *, src_count):
    q = jnp.sum(parts[...], axis=0)
    u = 1.0 / (src_count * q)
    scale[...] = u
    potential[...] = rho[...] - 2.0 * math.log(src_count) - jnp.log(q)
    for b in range(kernel_t.shape[0] // SLABS):
        ub = flat(u[b * SLABS : (b + 1) * SLABS, :])
        hi = ub.astype(BF16).astype(F32)
        sub = iota((16, BLK), 0)
        low = jnp.where(sub == 0, hi, jnp.where(sub == 1, ub - hi, 0.0)).astype(BF16)
        scaled = (src_t[:, b * BLK : (b + 1) * BLK].astype(F32) * ub).astype(BF16)
        left = jnp.concatenate([scaled, low], axis=0)
        x = lax.dot_general(left, slabs(kernel_t, b * SLABS, SLABS), NT, preferred_element_type=F32)
        if b == 0:
            total[...] = x
        else:
            total[...] += x
    w = weight[...]
    sums[...] = jnp.broadcast_to((w * stack(total[128:129, :] + total[129:130, :], 128))[None], sums.shape)
    w = flat(w)
    half = keep.shape[0]
    own = lax.rem(lax.axis_index("row"), 2) * half
    keep[...] = total[pl.ds(pl.multiple_of(own, half), half), :] * w
    send[...] = total[pl.ds(pl.multiple_of(half - own, half), half), :] * w


def on_first_core():
    return lax.rem(lax.axis_index("row"), 2) == 0


def share_of(major, minor):
    first = on_first_core()
    col = lax.axis_index("col")
    z = (col // 4) ^ jnp.where(first, major, minor)
    x = (col % 4) ^ jnp.where(first, minor, major)
    return z * 4 + x


SEND = ((1, 2), (3, 2))
STAY = ((0, 3), (0, 1))


def mix(left, kernel_t, scale, outs, offsets, src_count):
    for k in range(8):
        at = [share_of(offsets[h][k // 4], k % 4) * 2 + h for h in range(2)]
        pair = jnp.concatenate([kernel_t[i] for i in at], axis=1)
        x = jnp.dot(left, pair, preferred_element_type=F32)
        for h in range(2):
            u = scale[pl.ds(at[h], 1), :] * src_count
            outs[h][k * 128 : (k + 1) * 128, :] = x[:, h * 128 : (h + 1) * 128] * u


def target_send(
    parts, weight, before, tgt_t, kernel_t, scale, out_a, out_b, left, potential, gain, *, src_count, tgt_count
):
    total = jnp.sum(parts[...], axis=0)
    g = 1.0 / (tgt_count * total)
    gain[...] = g
    potential[...] = before[...] - math.log(tgt_count) - jnp.log(total)
    value = (tgt_t[...].astype(F32) * flat(weight[...] * g)).astype(BF16)
    left[...] = value
    mix(value, kernel_t, scale, (out_a, out_b), SEND, src_count)


def target_keep(left, kernel_t, scale, out_a, out_b, *, src_count):
    mix(left[...], kernel_t, scale, (out_a, out_b), STAY, src_count)


def moment_half(mine, gain, tgt, out):
    out[...] = jnp.dot(
        mine[...] * flat(gain[...]), tgt[...].astype(F32), precision=lax.Precision.HIGHEST, preferred_element_type=F32
    )


def in_order(mine, other):
    first = on_first_core()
    return jnp.concatenate([jnp.where(first, mine, other), jnp.where(first, other, mine)], axis=0)


def finish_sources(mine, other, gain, out, *, tgt_count):
    out[...] = (in_order(mine[...], other[...]) * (flat(gain[...]) * tgt_count)).T.astype(BF16)


def merge_first(keep_a, got_a, keep_b, got_b, send_a, hold_a, send_b, hold_b):
    for keep, got, send, hold in ((keep_a, got_a, send_a, hold_a), (keep_b, got_b, send_b, hold_b)):
        hold[...] = keep[:512, :] + got[:512, :]
        send[...] = keep[512:, :] + got[512:, :]


def merge_second(hold_a, got_a, hold_b, got_b, send_a, next_a, send_b, next_b):
    for half, (hold, got, send, after) in enumerate(
        ((hold_a, got_a, send_a, next_a), (hold_b, got_b, send_b, next_b))
    ):
        for out, offsets in ((send, SEND[half]), (after, STAY[half])):
            for k, minor in enumerate(offsets):
                rows = slice(minor * 128, (minor + 1) * 128)
                out[k * 128 : (k + 1) * 128, :] = hold[rows, :] + got[rows, :]


def merge_third(hold_a, got_a, hold_b, got_b, send_a, next_a, send_b, next_b):
    for hold, got, send, after in ((hold_a, got_a, send_a, next_a), (hold_b, got_b, send_b, next_b)):
        after[...] = hold[:128, :] + got[:128, :]
        send[...] = hold[128:, :] + got[128:, :]


def merge_last(hold_a, got_a, hold_b, got_b, bary):
    bary[:128, :] = (hold_a[...] + got_a[...]).T.astype(BF16)
    bary[128:, :] = (hold_b[...] + got_b[...]).T.astype(BF16)


def finish_moment(mine, other, out):
    out[...] = in_order(mine[...], other[...])


def call(body, outs, *args, scratch=(), spaces=None):
    spaces = spaces or {}
    return pl.pallas_call(
        body,
        out_shape=outs,
        in_specs=[pl.BlockSpec(memory_space=spaces.get(i, pltpu.VMEM)) for i in range(len(args))],
        out_specs=jax.tree.map(lambda _: pl.BlockSpec(memory_space=pltpu.VMEM), outs),
        scratch_shapes=list(scratch),
        cost_estimate=pl.CostEstimate(flops=1, bytes_accessed=1, transcendentals=0),
        compiler_params=pltpu.CompilerParams(vmem_limit_bytes=VMEM_LIMIT),
    )(*args)


def f32(*shape):
    return jax.ShapeDtypeStruct(shape, F32)


def bf16(*shape):
    return jax.ShapeDtypeStruct(shape, BF16)


def near(x):
    return pltpu.with_memory_space_constraint(x, pltpu.VMEM)


def far(x):
    return pltpu.with_memory_space_constraint(x, pltpu.HBM)


def local(src_emb, tgt_emb, cost_factor, col_start):
    rows, cols = src_emb.shape[0], tgt_emb.shape[0]
    width = src_emb.shape[1]
    row_size, col_size = lax.axis_size("row"), lax.axis_size("col")
    src_count, tgt_count = rows * row_size, cols * col_size
    counts = dict(src_count=src_count, tgt_count=tgt_count)
    share = rows // col_size
    row_shape, col_shape = (rows // 128, 128), (cols // 128, 128)

    def swap(x):
        return lax.ppermute(x, "row", [(i, i ^ 1) for i in range(row_size)])

    def by_core(x, step):
        pairs = []
        for i in range(row_size * col_size):
            row, col = divmod(i, col_size)
            y, z, w = step(row % 2, row // 2, col // 4, col % 4)
            pairs.append((i, (y * 2 + row % 2) * col_size + z * 4 + w))
        return lax.ppermute(x, ("row", "col"), pairs)

    def major(x, k):
        return by_core(x, lambda c, y, z, w: (y, z, w ^ k) if c else (y, z ^ k, w))

    def minor(x, k):
        return by_core(x, lambda c, y, z, w: (y, z ^ k, w) if c else (y, z, w ^ k))

    def along_y(x, k):
        return by_core(x, lambda c, y, z, w: (y ^ k ^ 2 * c, z, w))

    def exchange(x, axis):
        return lax.all_to_all(x, axis, 0, 0)

    lse, proj_t, aug, start = call(
        first_rows,
        [f32(col_size, *row_shape), bf16(width, rows), bf16(cols, 2 * width), f32(*col_shape)],
        far(src_emb), far(tgt_emb), far(cost_factor), far(col_start.reshape(col_shape)),
        scratch=[
            pltpu.VMEM((rows, width), BF16),
            pltpu.VMEM((width, width), BF16),
            pltpu.SemaphoreType.DMA((4,)),
        ],
        spaces={i: pltpu.HBM for i in range(4)},
    )
    parts = exchange(lse, "col")
    src_late, tgt_late, _ = lax.optimization_barrier((src_emb, tgt_emb, proj_t))
    src_t, tgt_t = call(transposes, [bf16(width, rows), bf16(width, cols)], src_late, tgt_late)
    parts, src_t, tgt_t = lax.optimization_barrier((parts, src_t, tgt_t))
    kernel_t, lse, shift, rho = call(
        first_columns,
        [pltpu.VMEM((rows // 128, cols, 128), BF16), f32(row_size, *col_shape), f32(*col_shape), f32(*row_shape)],
        parts, proj_t, aug, start,
        scratch=[pltpu.VMEM((cols, 128), F32), pltpu.VMEM((cols, 2 * width), BF16)],
    )
    parts = exchange(lse, "row")
    sums, weight, before = call(
        functools.partial(second_rows, **counts),
        [f32(col_size, *row_shape), f32(*col_shape), f32(*col_shape)],
        parts, shift, near(kernel_t),
    )
    parts = exchange(sums, "col")
    sums, keep, send, scale, row_potential = call(
        functools.partial(second_columns, src_count=src_count),
        [f32(row_size, *col_shape), f32(width // 2, cols), f32(width // 2, cols), f32(*row_shape), f32(*row_shape)],
        parts, rho, near(kernel_t), src_t, weight,
        scratch=[pltpu.VMEM((width + 16, cols), F32)],
    )
    parts = exchange(sums, "row")
    message = f32(8 * width, share // 2)
    send_a, send_b, left, col_potential, gain = call(
        functools.partial(target_send, **counts),
        [message, message, bf16(width, cols), f32(*col_shape), f32(*col_shape)],
        parts, weight, before, tgt_t, near(kernel_t), scale,
    )
    got_a, got_b = major(send_a, 1), major(send_b, 3)
    keep_a, keep_b = call(
        functools.partial(target_keep, src_count=src_count), [message, message], left, near(kernel_t), scale
    )
    send, _ = lax.optimization_barrier((send, left))
    mine = keep + swap(send)
    mine = mine + along_y(mine, 1)
    keep_a, mine = lax.optimization_barrier((keep_a, mine))
    mine = mine + along_y(mine, 3)
    moment, = call(moment_half, [f32(width // 2, width)], mine, gain, tgt_emb)
    bary_tgt, = call(
        functools.partial(finish_sources, tgt_count=tgt_count), [bf16(cols, width)], mine, swap(mine), gain
    )
    send_a, hold_a, send_b, hold_b = call(merge_first, [f32(512, 128)] * 4, keep_a, got_a, keep_b, got_b)
    got_a, got_b = major(send_a, 3), major(send_b, 1)
    hold_a, moment = lax.optimization_barrier((hold_a, moment))
    rest = major(moment, 1)
    send_a, hold_a, send_b, hold_b = call(merge_second, [f32(256, 128)] * 4, hold_a, got_a, hold_b, got_b)
    got_a, got_b = minor(send_a, 1), minor(send_b, 3)
    hold_a, bary_tgt, moment = lax.optimization_barrier((hold_a, bary_tgt, moment))
    moment = moment + rest
    moment = moment + major(moment, 3)
    hold_a, moment = lax.optimization_barrier((hold_a, moment))
    rest = minor(moment, 1)
    send_a, hold_a, send_b, hold_b = call(merge_third, [f32(128, 128)] * 4, hold_a, got_a, hold_b, got_b)
    got_a, got_b = minor(send_a, 3), minor(send_b, 1)
    hold_a, moment = lax.optimization_barrier((hold_a, moment))
    moment = moment + rest
    moment = moment + minor(moment, 3)
    bary_src, = call(merge_last, [bf16(share, width)], hold_a, got_a, hold_b, got_b)
    bary_src, moment = lax.optimization_barrier((bary_src, moment))
    moment, = call(finish_moment, [f32(width, width)], moment, swap(moment))
    return (bary_src, bary_tgt, moment, row_potential.reshape(rows), col_potential.reshape(cols))


def solution(mesh):
    placed = (P("row", None), P("col", None), P(), P("col"))
    return jax.shard_map(
        local,
        mesh=mesh,
        in_specs=placed,
        out_specs=(P(("row", "col"), None), P("col", None), P(), P("row"), P("col")),
        check_vma=False,
    )
```

```python
import functools
import math

import jax
import jax.numpy as jnp
from jax import lax
from jax.experimental import pallas as pl
from jax.experimental.pallas import tpu as pltpu
from jax.sharding import PartitionSpec as P

F32 = jnp.float32
BF16 = jnp.bfloat16
NT = (((1,), (1,)), ((), ()))
TINY = 2.0**-80
SMALL, LARGE = 1e-30, 1e30
GUESS = 0.3
BLK = 512
CHUNK = 256
SLABS = BLK // 128
VMEM_LIMIT = 24 * 1024 * 1024


def split3(x):
    hi = x.astype(BF16).astype(F32)
    mid = (x - hi).astype(BF16).astype(F32)
    lo = (x - hi - mid).astype(BF16).astype(F32)
    return hi, mid, lo


def iota(shape, dim):
    return lax.broadcasted_iota(jnp.int32, shape, dim)


def lanes(b, size):
    if isinstance(b, int):
        return slice(b * size, (b + 1) * size)
    return pl.ds(pl.multiple_of(b * size, size), size)


def aug_columns(shift):
    hi, mid, lo = split3(shift)
    lane = iota((shift.shape[0], 128), 1)
    out = jnp.where(lane < 3, 1.0, 0.0)
    out = jnp.where(lane == 3, hi, out)
    out = jnp.where(lane == 4, mid, out)
    out = jnp.where(lane == 5, lo, out)
    return out.astype(BF16)


def aug_rows(term):
    hi, mid, lo = split3(term)
    sub = iota((16, term.shape[1]), 0)
    out = jnp.where((sub >= 3) & (sub < 6), 1.0, 0.0)
    out = jnp.where(sub == 0, hi, out)
    out = jnp.where(sub == 1, mid, out)
    out = jnp.where(sub == 2, lo, out)
    zeros = jnp.zeros((112, term.shape[1]), BF16)
    return jnp.concatenate([out.astype(BF16), zeros], axis=0)


def log_sum(x):
    largest = jnp.max(x, axis=0, keepdims=True)
    return largest + jnp.log(jnp.sum(jnp.exp(x - largest), axis=0, keepdims=True))


def flat(x):
    return jnp.concatenate([x[i : i + 1, :] for i in range(x.shape[0])], axis=1)


def stack(x, width):
    return jnp.concatenate([x[:, i * width : (i + 1) * width] for i in range(x.shape[1] // width)], axis=0)


def column(x):
    return jnp.broadcast_to(x, (8, x.shape[1])).T[:, :1]


def identity(n):
    return jnp.where(iota((n, n), 0) == iota((n, n), 1), 1.0, 0.0).astype(BF16)


def first_rows(src_in, tgt_in, factor_in, start_in, lse, proj_t, aug, start, src, factor, sems):
    copies = [
        pltpu.make_async_copy(start_in, start, sems.at[0]),
        pltpu.make_async_copy(factor_in, factor, sems.at[1]),
        pltpu.make_async_copy(src_in, src, sems.at[2]),
        pltpu.make_async_copy(tgt_in, aug.at[:, pl.ds(0, 128)], sems.at[3]),
    ]
    for copy in copies:
        copy.start()
    copies[0].wait()
    aug[:, 128:] = aug_columns(column(flat(start[...])))
    for copy in copies[1:]:
        copy.wait()
    factor_t = factor[...].astype(F32).T.astype(BF16)
    proj_t[...] = lax.dot_general(factor_t, src[...], NT, preferred_element_type=F32).astype(BF16)
    blocks = src.shape[0] // BLK
    chunks = aug.shape[0] // CHUNK

    def scores(c, right):
        x = jnp.dot(aug[c * CHUNK : (c + 1) * CHUNK, :], right, preferred_element_type=F32)
        return x.reshape(CHUNK // 8, 8, BLK)

    tgt = aug[:, :128].astype(F32)
    reach = GUESS * jnp.sqrt(jnp.max(jnp.sum(tgt * tgt, axis=1, keepdims=True), axis=0, keepdims=True))
    totals, values = [], []
    for b in range(blocks):
        proj = proj_t[:, b * BLK : (b + 1) * BLK]
        wide = proj.astype(F32)
        shift = reach * jnp.sqrt(jnp.sum(wide * wide, axis=0, keepdims=True))
        right = jnp.concatenate([proj, aug_rows(-shift)], axis=0)
        total = jnp.zeros((8, BLK), F32)
        for c in range(chunks):
            total += jnp.sum(jnp.exp(scores(c, right)), axis=0)
        total = jnp.sum(total, axis=0, keepdims=True)
        totals.append(total)
        values.append(stack(shift + jnp.log(total), 128))
    lse[...] = jnp.broadcast_to(jnp.concatenate(values, axis=0)[None], lse.shape)
    totals = jnp.concatenate(totals, axis=0)
    good = jnp.where((totals > SMALL) & (totals < LARGE), 1.0, 0.0)

    @pl.when(jnp.min(good) < 0.5)
    def _():
        under = aug_rows(jnp.zeros((1, BLK), F32))

        def block(b, carry):
            right = jnp.concatenate([proj_t[:, lanes(b, BLK)], under], axis=0)
            largest = jnp.full((8, BLK), -jnp.inf, F32)
            total = jnp.zeros((8, BLK), F32)
            for c in range(chunks):
                x = scores(c, right)
                new = jnp.maximum(largest, jnp.max(x, axis=0))
                total = total * jnp.exp(largest - new) + jnp.sum(jnp.exp(x - new[None]), axis=0)
                largest = new
            top = jnp.max(largest, axis=0, keepdims=True)
            value = top + jnp.log(jnp.sum(total * jnp.exp(largest - top), axis=0, keepdims=True))
            for i in range(SLABS):
                row = jnp.broadcast_to(value[:, i * 128 : (i + 1) * 128][None], (lse.shape[0], 1, 128))
                lse[:, pl.ds(b * SLABS + i, 1), :] = row
            return carry

        lax.fori_loop(0, blocks, block, 0)


def transposes(src, tgt, src_t, tgt_t):
    eye = identity(128)
    tgt_t[...] = lax.dot_general(eye, tgt[...], NT, preferred_element_type=F32).astype(BF16)
    src_t[...] = lax.dot_general(eye, src[...], NT, preferred_element_type=F32).astype(BF16)


def first_columns(parts, proj_t, aug, start, kernel_t, lse, shift, rho, sums, spare):
    blocks = proj_t.shape[1] // BLK
    chunks = aug.shape[0] // CHUNK
    rho[...] = -log_sum(parts[...])[0]
    shift[...] = start[...]

    def right_of(b):
        term = jnp.concatenate([rho[pl.ds(b * SLABS + i, 1), :] for i in range(SLABS)], axis=1)
        return jnp.concatenate([proj_t[:, lanes(b, BLK)], aug_rows(term)], axis=0)

    def fold(x, op):
        out = x[:, :128]
        for i in range(1, BLK // 128):
            out = op(out, x[:, i * 128 : (i + 1) * 128])
        return out

    def fill(left, b):
        right = right_of(b)
        for c in range(chunks):
            rows = slice(c * CHUNK, (c + 1) * CHUNK)
            e = jnp.exp(jnp.dot(left[rows, :], right, preferred_element_type=F32))
            for i in range(SLABS):
                kernel_t[b * SLABS + i, rows, :] = e[:, i * 128 : (i + 1) * 128].astype(BF16)
            sums[rows, :] += fold(e, jnp.add)

    def column_sums():
        return stack(jnp.sum(sums[...].T, axis=0, keepdims=True), 128)

    sums[...] = jnp.zeros_like(sums)
    for b in range(blocks):
        fill(aug, b)
    total = column_sums()
    lse[...] = jnp.broadcast_to((jnp.log(total) - shift[...])[None], lse.shape)

    @pl.when(jnp.min(total) < TINY)
    def _():
        sums[...] = jnp.full(sums.shape, -jnp.inf, F32)

        def largest(b, carry):
            right = right_of(b)
            for c in range(chunks):
                rows = slice(c * CHUNK, (c + 1) * CHUNK)
                x = jnp.dot(aug[rows, :], right, preferred_element_type=F32)
                sums[rows, :] = jnp.maximum(sums[rows, :], fold(x, jnp.maximum))
            return carry

        lax.fori_loop(0, blocks, largest, 0)
        top = jnp.max(sums[...], axis=1, keepdims=True)
        spare[:, :128] = aug[:, :128]
        spare[:, 128:] = aug_columns(column(flat(start[...])) - top)
        shift[...] = start[...] - stack(jnp.broadcast_to(top, sums.shape).T[:1], 128)
        sums[...] = jnp.zeros_like(sums)

        def again(b, carry):
            fill(spare, b)
            return carry

        lax.fori_loop(0, blocks, again, 0)
        lse[...] = jnp.broadcast_to((jnp.log(column_sums()) - shift[...])[None], lse.shape)


def slabs(ref, first, count):
    return jnp.concatenate([ref[first + i] for i in range(count)], axis=1)


def second_rows(parts, shift, kernel_t, sums, weight, potential, *, src_count, tgt_count):
    total = log_sum(parts[...])[0]
    potential[...] = math.log(src_count) - math.log(tgt_count) - total
    w = jnp.exp(-math.log(tgt_count) - total - shift[...])
    weight[...] = w
    w = flat(w)
    hi = w.astype(BF16).astype(F32)
    sub = iota((16, w.shape[1]), 0)
    left = jnp.where(sub == 0, hi, jnp.where(sub == 1, w - hi, 0.0)).astype(BF16)
    values = []
    for b in range(kernel_t.shape[0] // SLABS):
        x = jnp.dot(left, slabs(kernel_t, b * SLABS, SLABS), preferred_element_type=F32)
        values.append(stack(x[:1] + x[1:2], 128))
    sums[...] = jnp.broadcast_to(jnp.concatenate(values, axis=0)[None], sums.shape)


def second_columns(parts, rho, kernel_t, src_t, weight, sums, keep, send, scale, potential, total, *, src_count):
    q = jnp.sum(parts[...], axis=0)
    u = 1.0 / (src_count * q)
    scale[...] = u
    potential[...] = rho[...] - 2.0 * math.log(src_count) - jnp.log(q)
    for b in range(kernel_t.shape[0] // SLABS):
        ub = flat(u[b * SLABS : (b + 1) * SLABS, :])
        hi = ub.astype(BF16).astype(F32)
        sub = iota((16, BLK), 0)
        low = jnp.where(sub == 0, hi, jnp.where(sub == 1, ub - hi, 0.0)).astype(BF16)
        scaled = (src_t[:, b * BLK : (b + 1) * BLK].astype(F32) * ub).astype(BF16)
        left = jnp.concatenate([scaled, low], axis=0)
        x = lax.dot_general(left, slabs(kernel_t, b * SLABS, SLABS), NT, preferred_element_type=F32)
        if b == 0:
            total[...] = x
        else:
            total[...] += x
    w = weight[...]
    sums[...] = jnp.broadcast_to((w * stack(total[128:129, :] + total[129:130, :], 128))[None], sums.shape)
    w = flat(w)
    half = keep.shape[0]
    own = lax.rem(lax.axis_index("row"), 2) * half
    keep[...] = total[pl.ds(pl.multiple_of(own, half), half), :] * w
    send[...] = total[pl.ds(pl.multiple_of(half - own, half), half), :] * w


def on_first_core():
    return lax.rem(lax.axis_index("row"), 2) == 0


def share_of(major, minor):
    first = on_first_core()
    col = lax.axis_index("col")
    z = (col // 4) ^ jnp.where(first, major, minor)
    x = (col % 4) ^ jnp.where(first, minor, major)
    return z * 4 + x


SEND = ((1, 2), (3, 2))
STAY = ((0, 3), (0, 1))


def mix(left, kernel_t, scale, outs, offsets, src_count):
    for k in range(8):
        at = [share_of(offsets[h][k // 4], k % 4) * 2 + h for h in range(2)]
        pair = jnp.concatenate([kernel_t[i] for i in at], axis=1)
        x = jnp.dot(left, pair, preferred_element_type=F32)
        for h in range(2):
            u = scale[pl.ds(at[h], 1), :] * src_count
            outs[h][k * 128 : (k + 1) * 128, :] = x[:, h * 128 : (h + 1) * 128] * u


def target_send(
    parts, weight, before, tgt_t, kernel_t, scale, out_a, out_b, left, potential, gain, *, src_count, tgt_count
):
    total = jnp.sum(parts[...], axis=0)
    g = 1.0 / (tgt_count * total)
    gain[...] = g
    potential[...] = before[...] - math.log(tgt_count) - jnp.log(total)
    value = (tgt_t[...].astype(F32) * flat(weight[...] * g)).astype(BF16)
    left[...] = value
    mix(value, kernel_t, scale, (out_a, out_b), SEND, src_count)


def target_keep(left, kernel_t, scale, out_a, out_b, *, src_count):
    mix(left[...], kernel_t, scale, (out_a, out_b), STAY, src_count)


def moment_half(mine, gain, tgt, out):
    out[...] = jnp.dot(
        mine[...] * flat(gain[...]), tgt[...].astype(F32), precision=lax.Precision.HIGHEST, preferred_element_type=F32
    )


def in_order(mine, other):
    first = on_first_core()
    return jnp.concatenate([jnp.where(first, mine, other), jnp.where(first, other, mine)], axis=0)


def finish_sources(mine, other, gain, out, *, tgt_count):
    out[...] = (in_order(mine[...], other[...]) * (flat(gain[...]) * tgt_count)).T.astype(BF16)


def merge_first(keep_a, got_a, keep_b, got_b, send_a, hold_a, send_b, hold_b):
    for keep, got, send, hold in ((keep_a, got_a, send_a, hold_a), (keep_b, got_b, send_b, hold_b)):
        hold[...] = keep[:512, :] + got[:512, :]
        send[...] = keep[512:, :] + got[512:, :]


def merge_second(hold_a, got_a, hold_b, got_b, send_a, next_a, send_b, next_b):
    for half, (hold, got, send, after) in enumerate(
        ((hold_a, got_a, send_a, next_a), (hold_b, got_b, send_b, next_b))
    ):
        for out, offsets in ((send, SEND[half]), (after, STAY[half])):
            for k, minor in enumerate(offsets):
                rows = slice(minor * 128, (minor + 1) * 128)
                out[k * 128 : (k + 1) * 128, :] = hold[rows, :] + got[rows, :]


def merge_third(hold_a, got_a, hold_b, got_b, send_a, next_a, send_b, next_b):
    for hold, got, send, after in ((hold_a, got_a, send_a, next_a), (hold_b, got_b, send_b, next_b)):
        after[...] = hold[:128, :] + got[:128, :]
        send[...] = hold[128:, :] + got[128:, :]


def merge_last(hold_a, got_a, hold_b, got_b, bary):
    bary[:128, :] = (hold_a[...] + got_a[...]).T.astype(BF16)
    bary[128:, :] = (hold_b[...] + got_b[...]).T.astype(BF16)


def finish_moment(mine, other, out):
    out[...] = in_order(mine[...], other[...])


def call(body, outs, *args, scratch=(), spaces=None):
    spaces = spaces or {}
    return pl.pallas_call(
        body,
        out_shape=outs,
        in_specs=[pl.BlockSpec(memory_space=spaces.get(i, pltpu.VMEM)) for i in range(len(args))],
        out_specs=jax.tree.map(lambda _: pl.BlockSpec(memory_space=pltpu.VMEM), outs),
        scratch_shapes=list(scratch),
        cost_estimate=pl.CostEstimate(flops=1, bytes_accessed=1, transcendentals=0),
        compiler_params=pltpu.CompilerParams(vmem_limit_bytes=VMEM_LIMIT),
    )(*args)


def f32(*shape):
    return jax.ShapeDtypeStruct(shape, F32)


def bf16(*shape):
    return jax.ShapeDtypeStruct(shape, BF16)


def near(x):
    return pltpu.with_memory_space_constraint(x, pltpu.VMEM)


def far(x):
    return pltpu.with_memory_space_constraint(x, pltpu.HBM)


def local(src_emb, tgt_emb, cost_factor, col_start):
    rows, cols = src_emb.shape[0], tgt_emb.shape[0]
    width = src_emb.shape[1]
    row_size, col_size = lax.axis_size("row"), lax.axis_size("col")
    src_count, tgt_count = rows * row_size, cols * col_size
    counts = dict(src_count=src_count, tgt_count=tgt_count)
    share = rows // col_size
    row_shape, col_shape = (rows // 128, 128), (cols // 128, 128)

    def swap(x):
        return lax.ppermute(x, "row", [(i, i ^ 1) for i in range(row_size)])

    def by_core(x, step):
        pairs = []
        for i in range(row_size * col_size):
            row, col = divmod(i, col_size)
            y, z, w = step(row % 2, row // 2, col // 4, col % 4)
            pairs.append((i, (y * 2 + row % 2) * col_size + z * 4 + w))
        return lax.ppermute(x, ("row", "col"), pairs)

    def major(x, k):
        return by_core(x, lambda c, y, z, w: (y, z, w ^ k) if c else (y, z ^ k, w))

    def minor(x, k):
        return by_core(x, lambda c, y, z, w: (y, z ^ k, w) if c else (y, z, w ^ k))

    def along_y(x, k):
        return by_core(x, lambda c, y, z, w: (y ^ k ^ 2 * c, z, w))

    def exchange(x, axis):
        return lax.all_to_all(x, axis, 0, 0)

    lse, proj_t, aug, start = call(
        first_rows,
        [f32(col_size, *row_shape), bf16(width, rows), bf16(cols, 2 * width), f32(*col_shape)],
        far(src_emb), far(tgt_emb), far(cost_factor), far(col_start.reshape(col_shape)),
        scratch=[
            pltpu.VMEM((rows, width), BF16),
            pltpu.VMEM((width, width), BF16),
            pltpu.SemaphoreType.DMA((4,)),
        ],
        spaces={i: pltpu.HBM for i in range(4)},
    )
    parts = exchange(lse, "col")
    src_late, tgt_late, _ = lax.optimization_barrier((src_emb, tgt_emb, proj_t))
    src_t, tgt_t = call(transposes, [bf16(width, rows), bf16(width, cols)], src_late, tgt_late)
    parts, src_t, tgt_t = lax.optimization_barrier((parts, src_t, tgt_t))
    kernel_t, lse, shift, rho = call(
        first_columns,
        [pltpu.VMEM((rows // 128, cols, 128), BF16), f32(row_size, *col_shape), f32(*col_shape), f32(*row_shape)],
        parts, proj_t, aug, start,
        scratch=[pltpu.VMEM((cols, 128), F32), pltpu.VMEM((cols, 2 * width), BF16)],
    )
    parts = exchange(lse, "row")
    sums, weight, before = call(
        functools.partial(second_rows, **counts),
        [f32(col_size, *row_shape), f32(*col_shape), f32(*col_shape)],
        parts, shift, near(kernel_t),
    )
    parts = exchange(sums, "col")
    sums, keep, send, scale, row_potential = call(
        functools.partial(second_columns, src_count=src_count),
        [f32(row_size, *col_shape), f32(width // 2, cols), f32(width // 2, cols), f32(*row_shape), f32(*row_shape)],
        parts, rho, near(kernel_t), src_t, weight,
        scratch=[pltpu.VMEM((width + 16, cols), F32)],
    )
    parts = exchange(sums, "row")
    message = f32(8 * width, share // 2)
    send_a, send_b, left, col_potential, gain = call(
        functools.partial(target_send, **counts),
        [message, message, bf16(width, cols), f32(*col_shape), f32(*col_shape)],
        parts, weight, before, tgt_t, near(kernel_t), scale,
    )
    got_a, got_b = major(send_a, 1), major(send_b, 3)
    keep_a, keep_b = call(
        functools.partial(target_keep, src_count=src_count), [message, message], left, near(kernel_t), scale
    )
    send, _ = lax.optimization_barrier((send, left))
    mine = keep + swap(send)
    mine = mine + along_y(mine, 1)
    keep_a, mine = lax.optimization_barrier((keep_a, mine))
    mine = mine + along_y(mine, 3)
    moment, = call(moment_half, [f32(width // 2, width)], mine, gain, tgt_emb)
    bary_tgt, = call(
        functools.partial(finish_sources, tgt_count=tgt_count), [bf16(cols, width)], mine, swap(mine), gain
    )
    send_a, hold_a, send_b, hold_b = call(merge_first, [f32(512, 128)] * 4, keep_a, got_a, keep_b, got_b)
    got_a, got_b = major(send_a, 3), major(send_b, 1)
    hold_a, moment = lax.optimization_barrier((hold_a, moment))
    rest = major(moment, 1)
    send_a, hold_a, send_b, hold_b = call(merge_second, [f32(256, 128)] * 4, hold_a, got_a, hold_b, got_b)
    got_a, got_b = minor(send_a, 1), minor(send_b, 3)
    hold_a, bary_tgt, moment = lax.optimization_barrier((hold_a, bary_tgt, moment))
    moment = moment + rest
    moment = moment + major(moment, 3)
    hold_a, moment = lax.optimization_barrier((hold_a, moment))
    rest = minor(moment, 1)
    send_a, hold_a, send_b, hold_b = call(merge_third, [f32(128, 128)] * 4, hold_a, got_a, hold_b, got_b)
    got_a, got_b = minor(send_a, 3), minor(send_b, 1)
    hold_a, moment = lax.optimization_barrier((hold_a, moment))
    moment = moment + rest
    moment = moment + minor(moment, 3)
    bary_src, = call(merge_last, [bf16(share, width)], hold_a, got_a, hold_b, got_b)
    bary_src, moment = lax.optimization_barrier((bary_src, moment))
    moment, = call(finish_moment, [f32(width, width)], moment, swap(moment))
    return (bary_src, bary_tgt, moment, row_potential.reshape(rows), col_potential.reshape(cols))


def solution(mesh):
    placed = (P("row", None), P("col", None), P(), P("col"))
    return jax.shard_map(
        local,
        mesh=mesh,
        in_specs=placed,
        out_specs=(P(("row", "col"), None), P("col", None), P(), P("row"), P("col")),
        check_vma=False,
    )
```

```python
import functools
import math

import jax
import jax.numpy as jnp
from jax import lax
from jax.experimental import pallas as pl
from jax.experimental.pallas import tpu as pltpu
from jax.sharding import PartitionSpec as P

F32 = jnp.float32
BF16 = jnp.bfloat16
NT = (((1,), (1,)), ((), ()))
TINY = 2.0**-80
SMALL, LARGE = 1e-30, 1e30
GUESS = 0.3
BLK = 512
CHUNK = 256
SLABS = BLK // 128
VMEM_LIMIT = 24 * 1024 * 1024


def split3(x):
    hi = x.astype(BF16).astype(F32)
    mid = (x - hi).astype(BF16).astype(F32)
    lo = (x - hi - mid).astype(BF16).astype(F32)
    return hi, mid, lo


def iota(shape, dim):
    return lax.broadcasted_iota(jnp.int32, shape, dim)


def lanes(b, size):
    if isinstance(b, int):
        return slice(b * size, (b + 1) * size)
    return pl.ds(pl.multiple_of(b * size, size), size)


def aug_columns(shift):
    hi, mid, lo = split3(shift)
    lane = iota((shift.shape[0], 128), 1)
    out = jnp.where(lane < 3, 1.0, 0.0)
    out = jnp.where(lane == 3, hi, out)
    out = jnp.where(lane == 4, mid, out)
    out = jnp.where(lane == 5, lo, out)
    return out.astype(BF16)


def aug_rows(term):
    hi, mid, lo = split3(term)
    sub = iota((16, term.shape[1]), 0)
    out = jnp.where((sub >= 3) & (sub < 6), 1.0, 0.0)
    out = jnp.where(sub == 0, hi, out)
    out = jnp.where(sub == 1, mid, out)
    out = jnp.where(sub == 2, lo, out)
    zeros = jnp.zeros((112, term.shape[1]), BF16)
    return jnp.concatenate([out.astype(BF16), zeros], axis=0)


def log_sum(x):
    largest = jnp.max(x, axis=0, keepdims=True)
    return largest + jnp.log(jnp.sum(jnp.exp(x - largest), axis=0, keepdims=True))


def flat(x):
    return jnp.concatenate([x[i : i + 1, :] for i in range(x.shape[0])], axis=1)


def stack(x, width):
    return jnp.concatenate([x[:, i * width : (i + 1) * width] for i in range(x.shape[1] // width)], axis=0)


def column(x):
    return jnp.broadcast_to(x, (8, x.shape[1])).T[:, :1]


def identity(n):
    return jnp.where(iota((n, n), 0) == iota((n, n), 1), 1.0, 0.0).astype(BF16)


def first_rows(src_in, tgt_in, factor_in, start_in, lse, proj_t, aug, start, src, factor, sems):
    copies = [
        pltpu.make_async_copy(start_in, start, sems.at[0]),
        pltpu.make_async_copy(factor_in, factor, sems.at[1]),
        pltpu.make_async_copy(src_in, src, sems.at[2]),
        pltpu.make_async_copy(tgt_in, aug.at[:, pl.ds(0, 128)], sems.at[3]),
    ]
    for copy in copies:
        copy.start()
    copies[0].wait()
    aug[:, 128:] = aug_columns(column(flat(start[...])))
    for copy in copies[1:]:
        copy.wait()
    factor_t = factor[...].astype(F32).T.astype(BF16)
    proj_t[...] = lax.dot_general(factor_t, src[...], NT, preferred_element_type=F32).astype(BF16)
    blocks = src.shape[0] // BLK
    chunks = aug.shape[0] // CHUNK

    def scores(c, right):
        x = jnp.dot(aug[c * CHUNK : (c + 1) * CHUNK, :], right, preferred_element_type=F32)
        return x.reshape(CHUNK // 8, 8, BLK)

    tgt = aug[:, :128].astype(F32)
    reach = GUESS * jnp.sqrt(jnp.max(jnp.sum(tgt * tgt, axis=1, keepdims=True), axis=0, keepdims=True))
    totals, values = [], []
    for b in range(blocks):
        proj = proj_t[:, b * BLK : (b + 1) * BLK]
        wide = proj.astype(F32)
        shift = reach * jnp.sqrt(jnp.sum(wide * wide, axis=0, keepdims=True))
        right = jnp.concatenate([proj, aug_rows(-shift)], axis=0)
        total = jnp.zeros((8, BLK), F32)
        for c in range(chunks):
            total += jnp.sum(jnp.exp(scores(c, right)), axis=0)
        total = jnp.sum(total, axis=0, keepdims=True)
        totals.append(total)
        values.append(stack(shift + jnp.log(total), 128))
    lse[...] = jnp.broadcast_to(jnp.concatenate(values, axis=0)[None], lse.shape)
    totals = jnp.concatenate(totals, axis=0)
    good = jnp.where((totals > SMALL) & (totals < LARGE), 1.0, 0.0)

    @pl.when(jnp.min(good) < 0.5)
    def _():
        under = aug_rows(jnp.zeros((1, BLK), F32))

        def block(b, carry):
            right = jnp.concatenate([proj_t[:, lanes(b, BLK)], under], axis=0)
            largest = jnp.full((8, BLK), -jnp.inf, F32)
            total = jnp.zeros((8, BLK), F32)
            for c in range(chunks):
                x = scores(c, right)
                new = jnp.maximum(largest, jnp.max(x, axis=0))
                total = total * jnp.exp(largest - new) + jnp.sum(jnp.exp(x - new[None]), axis=0)
                largest = new
            top = jnp.max(largest, axis=0, keepdims=True)
            value = top + jnp.log(jnp.sum(total * jnp.exp(largest - top), axis=0, keepdims=True))
            for i in range(SLABS):
                row = jnp.broadcast_to(value[:, i * 128 : (i + 1) * 128][None], (lse.shape[0], 1, 128))
                lse[:, pl.ds(b * SLABS + i, 1), :] = row
            return carry

        lax.fori_loop(0, blocks, block, 0)


def transposes(src, tgt, src_t, tgt_t):
    eye = identity(128)
    tgt_t[...] = lax.dot_general(eye, tgt[...], NT, preferred_element_type=F32).astype(BF16)
    src_t[...] = lax.dot_general(eye, src[...], NT, preferred_element_type=F32).astype(BF16)


def first_columns(parts, proj_t, aug, start, kernel_t, lse, shift, rho, sums, spare):
    blocks = proj_t.shape[1] // BLK
    chunks = aug.shape[0] // CHUNK
    rho[...] = -log_sum(parts[...])[0]
    shift[...] = start[...]

    def right_of(b):
        term = jnp.concatenate([rho[pl.ds(b * SLABS + i, 1), :] for i in range(SLABS)], axis=1)
        return jnp.concatenate([proj_t[:, lanes(b, BLK)], aug_rows(term)], axis=0)

    def fold(x, op):
        out = x[:, :128]
        for i in range(1, BLK // 128):
            out = op(out, x[:, i * 128 : (i + 1) * 128])
        return out

    def fill(left, b):
        right = right_of(b)
        for c in range(chunks):
            rows = slice(c * CHUNK, (c + 1) * CHUNK)
            e = jnp.exp(jnp.dot(left[rows, :], right, preferred_element_type=F32))
            for i in range(SLABS):
                kernel_t[b * SLABS + i, rows, :] = e[:, i * 128 : (i + 1) * 128].astype(BF16)
            sums[rows, :] += fold(e, jnp.add)

    def column_sums():
        return stack(jnp.sum(sums[...].T, axis=0, keepdims=True), 128)

    sums[...] = jnp.zeros_like(sums)
    for b in range(blocks):
        fill(aug, b)
    total = column_sums()
    lse[...] = jnp.broadcast_to((jnp.log(total) - shift[...])[None], lse.shape)

    @pl.when(jnp.min(total) < TINY)
    def _():
        sums[...] = jnp.full(sums.shape, -jnp.inf, F32)

        def largest(b, carry):
            right = right_of(b)
            for c in range(chunks):
                rows = slice(c * CHUNK, (c + 1) * CHUNK)
                x = jnp.dot(aug[rows, :], right, preferred_element_type=F32)
                sums[rows, :] = jnp.maximum(sums[rows, :], fold(x, jnp.maximum))
            return carry

        lax.fori_loop(0, blocks, largest, 0)
        top = jnp.max(sums[...], axis=1, keepdims=True)
        spare[:, :128] = aug[:, :128]
        spare[:, 128:] = aug_columns(column(flat(start[...])) - top)
        shift[...] = start[...] - stack(jnp.broadcast_to(top, sums.shape).T[:1], 128)
        sums[...] = jnp.zeros_like(sums)

        def again(b, carry):
            fill(spare, b)
            return carry

        lax.fori_loop(0, blocks, again, 0)
        lse[...] = jnp.broadcast_to((jnp.log(column_sums()) - shift[...])[None], lse.shape)


def slabs(ref, first, count):
    return jnp.concatenate([ref[first + i] for i in range(count)], axis=1)


def second_rows(parts, shift, kernel_t, sums, weight, potential, *, src_count, tgt_count):
    total = log_sum(parts[...])[0]
    potential[...] = math.log(src_count) - math.log(tgt_count) - total
    w = jnp.exp(-math.log(tgt_count) - total - shift[...])
    weight[...] = w
    w = flat(w)
    hi = w.astype(BF16).astype(F32)
    sub = iota((16, w.shape[1]), 0)
    left = jnp.where(sub == 0, hi, jnp.where(sub == 1, w - hi, 0.0)).astype(BF16)
    values = []
    for b in range(kernel_t.shape[0] // SLABS):
        x = jnp.dot(left, slabs(kernel_t, b * SLABS, SLABS), preferred_element_type=F32)
        values.append(stack(x[:1] + x[1:2], 128))
    sums[...] = jnp.broadcast_to(jnp.concatenate(values, axis=0)[None], sums.shape)


def second_columns(parts, rho, kernel_t, src_t, weight, sums, keep, send, scale, potential, total, *, src_count):
    q = jnp.sum(parts[...], axis=0)
    u = 1.0 / (src_count * q)
    scale[...] = u
    potential[...] = rho[...] - 2.0 * math.log(src_count) - jnp.log(q)
    for b in range(kernel_t.shape[0] // SLABS):
        ub = flat(u[b * SLABS : (b + 1) * SLABS, :])
        hi = ub.astype(BF16).astype(F32)
        sub = iota((16, BLK), 0)
        low = jnp.where(sub == 0, hi, jnp.where(sub == 1, ub - hi, 0.0)).astype(BF16)
        scaled = (src_t[:, b * BLK : (b + 1) * BLK].astype(F32) * ub).astype(BF16)
        left = jnp.concatenate([scaled, low], axis=0)
        x = lax.dot_general(left, slabs(kernel_t, b * SLABS, SLABS), NT, preferred_element_type=F32)
        if b == 0:
            total[...] = x
        else:
            total[...] += x
    w = weight[...]
    sums[...] = jnp.broadcast_to((w * stack(total[128:129, :] + total[129:130, :], 128))[None], sums.shape)
    w = flat(w)
    half = keep.shape[0]
    own = lax.rem(lax.axis_index("row"), 2) * half
    keep[...] = total[pl.ds(pl.multiple_of(own, half), half), :] * w
    send[...] = total[pl.ds(pl.multiple_of(half - own, half), half), :] * w


def on_first_core():
    return lax.rem(lax.axis_index("row"), 2) == 0


def share_of(major, minor):
    first = on_first_core()
    col = lax.axis_index("col")
    z = (col // 4) ^ jnp.where(first, major, minor)
    x = (col % 4) ^ jnp.where(first, minor, major)
    return z * 4 + x


SEND = ((1, 2), (3, 2))
STAY = ((0, 3), (0, 1))


def mix(left, kernel_t, scale, outs, offsets, src_count):
    for k in range(8):
        at = [share_of(offsets[h][k // 4], k % 4) * 2 + h for h in range(2)]
        pair = jnp.concatenate([kernel_t[i] for i in at], axis=1)
        x = jnp.dot(left, pair, preferred_element_type=F32)
        for h in range(2):
            u = scale[pl.ds(at[h], 1), :] * src_count
            outs[h][k * 128 : (k + 1) * 128, :] = x[:, h * 128 : (h + 1) * 128] * u


def target_send(
    parts, weight, before, tgt_t, kernel_t, scale, out_a, out_b, left, potential, gain, *, src_count, tgt_count
):
    total = jnp.sum(parts[...], axis=0)
    g = 1.0 / (tgt_count * total)
    gain[...] = g
    potential[...] = before[...] - math.log(tgt_count) - jnp.log(total)
    value = (tgt_t[...].astype(F32) * flat(weight[...] * g)).astype(BF16)
    left[...] = value
    mix(value, kernel_t, scale, (out_a, out_b), SEND, src_count)


def target_keep(left, kernel_t, scale, out_a, out_b, *, src_count):
    mix(left[...], kernel_t, scale, (out_a, out_b), STAY, src_count)


def moment_half(mine, gain, tgt, out):
    out[...] = jnp.dot(
        mine[...] * flat(gain[...]), tgt[...].astype(F32), precision=lax.Precision.HIGHEST, preferred_element_type=F32
    )


def in_order(mine, other):
    first = on_first_core()
    return jnp.concatenate([jnp.where(first, mine, other), jnp.where(first, other, mine)], axis=0)


def finish_sources(mine, other, gain, out, *, tgt_count):
    out[...] = (in_order(mine[...], other[...]) * (flat(gain[...]) * tgt_count)).T.astype(BF16)


def merge_first(keep_a, got_a, keep_b, got_b, moment, send_a, hold_a, send_b, hold_b):
    for keep, got, send, hold in ((keep_a, got_a, send_a, hold_a), (keep_b, got_b, send_b, hold_b)):
        hold[...] = keep[:512, :] + got[:512, :]
        send[:512, :] = keep[512:, :] + got[512:, :]
        send[512:, :] = moment[...]


def merge_second(hold_a, got_a, hold_b, got_b, moment, across, send_a, next_a, send_b, next_b):
    for half, (hold, got, send, after) in enumerate(
        ((hold_a, got_a, send_a, next_a), (hold_b, got_b, send_b, next_b))
    ):
        for out, offsets in ((send, SEND[half]), (after, STAY[half])):
            for k, minor in enumerate(offsets):
                rows = slice(minor * 128, (minor + 1) * 128)
                out[k * 128 : (k + 1) * 128, :] = hold[rows, :] + got[rows, :]
    send_a[256:, :] = (moment[...] + got_b[512:, :]) + (across[...] + got_a[512:, :])


def merge_third(hold_a, sent_a, got_a, hold_b, got_b, send_a, next_a, send_b, next_b):
    for hold, got, send, after in ((hold_a, got_a, send_a, next_a), (hold_b, got_b, send_b, next_b)):
        after[...] = hold[:128, :] + got[:128, :]
        send[:128, :] = hold[128:, :] + got[128:256, :]
    send_a[128:, :] = sent_a[256:, :] + got_a[256:, :]


def merge_moment(sent, got, out):
    out[...] = sent[128:, :] + got[128:, :]


def merge_last(hold_a, got_a, hold_b, got_b, bary):
    bary[:128, :] = (hold_a[...] + got_a[:128, :]).T.astype(BF16)
    bary[128:, :] = (hold_b[...] + got_b[...]).T.astype(BF16)


def finish_moment(mine, other, out):
    out[...] = in_order(mine[...], other[...])


def call(body, outs, *args, scratch=(), spaces=None):
    spaces = spaces or {}
    return pl.pallas_call(
        body,
        out_shape=outs,
        in_specs=[pl.BlockSpec(memory_space=spaces.get(i, pltpu.VMEM)) for i in range(len(args))],
        out_specs=jax.tree.map(lambda _: pl.BlockSpec(memory_space=pltpu.VMEM), outs),
        scratch_shapes=list(scratch),
        cost_estimate=pl.CostEstimate(flops=1, bytes_accessed=1, transcendentals=0),
        compiler_params=pltpu.CompilerParams(vmem_limit_bytes=VMEM_LIMIT),
    )(*args)


def f32(*shape):
    return jax.ShapeDtypeStruct(shape, F32)


def bf16(*shape):
    return jax.ShapeDtypeStruct(shape, BF16)


def near(x):
    return pltpu.with_memory_space_constraint(x, pltpu.VMEM)


def far(x):
    return pltpu.with_memory_space_constraint(x, pltpu.HBM)


def local(src_emb, tgt_emb, cost_factor, col_start):
    rows, cols = src_emb.shape[0], tgt_emb.shape[0]
    width = src_emb.shape[1]
    row_size, col_size = lax.axis_size("row"), lax.axis_size("col")
    src_count, tgt_count = rows * row_size, cols * col_size
    counts = dict(src_count=src_count, tgt_count=tgt_count)
    share = rows // col_size
    row_shape, col_shape = (rows // 128, 128), (cols // 128, 128)

    def swap(x):
        return lax.ppermute(x, "row", [(i, i ^ 1) for i in range(row_size)])

    def by_core(x, step):
        pairs = []
        for i in range(row_size * col_size):
            row, col = divmod(i, col_size)
            y, z, w = step(row % 2, row // 2, col // 4, col % 4)
            pairs.append((i, (y * 2 + row % 2) * col_size + z * 4 + w))
        return lax.ppermute(x, ("row", "col"), pairs)

    def major(x, k):
        return by_core(x, lambda c, y, z, w: (y, z, w ^ k) if c else (y, z ^ k, w))

    def minor(x, k):
        return by_core(x, lambda c, y, z, w: (y, z ^ k, w) if c else (y, z, w ^ k))

    def along_y(x, k):
        return by_core(x, lambda c, y, z, w: (y ^ k ^ 2 * c, z, w))

    def exchange(x, axis):
        return lax.all_to_all(x, axis, 0, 0)

    lse, proj_t, aug, start = call(
        first_rows,
        [f32(col_size, *row_shape), bf16(width, rows), bf16(cols, 2 * width), f32(*col_shape)],
        far(src_emb), far(tgt_emb), far(cost_factor), far(col_start.reshape(col_shape)),
        scratch=[
            pltpu.VMEM((rows, width), BF16),
            pltpu.VMEM((width, width), BF16),
            pltpu.SemaphoreType.DMA((4,)),
        ],
        spaces={i: pltpu.HBM for i in range(4)},
    )
    parts = exchange(lse, "col")
    src_late, tgt_late, _ = lax.optimization_barrier((src_emb, tgt_emb, proj_t))
    src_t, tgt_t = call(transposes, [bf16(width, rows), bf16(width, cols)], src_late, tgt_late)
    parts, src_t, tgt_t = lax.optimization_barrier((parts, src_t, tgt_t))
    kernel_t, lse, shift, rho = call(
        first_columns,
        [pltpu.VMEM((rows // 128, cols, 128), BF16), f32(row_size, *col_shape), f32(*col_shape), f32(*row_shape)],
        parts, proj_t, aug, start,
        scratch=[pltpu.VMEM((cols, 128), F32), pltpu.VMEM((cols, 2 * width), BF16)],
    )
    parts = exchange(lse, "row")
    sums, weight, before = call(
        functools.partial(second_rows, **counts),
        [f32(col_size, *row_shape), f32(*col_shape), f32(*col_shape)],
        parts, shift, near(kernel_t),
    )
    parts = exchange(sums, "col")
    sums, keep, send, scale, row_potential = call(
        functools.partial(second_columns, src_count=src_count),
        [f32(row_size, *col_shape), f32(width // 2, cols), f32(width // 2, cols), f32(*row_shape), f32(*row_shape)],
        parts, rho, near(kernel_t), src_t, weight,
        scratch=[pltpu.VMEM((width + 16, cols), F32)],
    )
    parts = exchange(sums, "row")
    message = f32(8 * width, share // 2)
    send_a, send_b, left, col_potential, gain = call(
        functools.partial(target_send, **counts),
        [message, message, bf16(width, cols), f32(*col_shape), f32(*col_shape)],
        parts, weight, before, tgt_t, near(kernel_t), scale,
    )
    got_a, got_b = major(send_a, 1), major(send_b, 3)
    keep_a, keep_b = call(
        functools.partial(target_keep, src_count=src_count), [message, message], left, near(kernel_t), scale
    )
    send, _ = lax.optimization_barrier((send, left))
    mine = keep + swap(send)
    moment, = call(moment_half, [f32(width // 2, width)], mine, gain, tgt_emb)
    moment = moment + along_y(moment, 1)
    moment = moment + along_y(moment, 3)
    keep_a, moment, mine = lax.optimization_barrier((keep_a, moment, mine))
    both = [f32(576, 128), f32(512, 128)] * 2
    send_a, hold_a, send_b, hold_b = call(merge_first, both, keep_a, got_a, keep_b, got_b, moment)
    got_a, got_b, across = major(send_a, 3), major(send_b, 1), major(moment, 2)
    hold_a, mine = lax.optimization_barrier((hold_a, mine))
    rest = along_y(mine, 1)
    both = [f32(320, 128), f32(256, 128), f32(256, 128), f32(256, 128)]
    send_a, hold_a, send_b, hold_b = call(merge_second, both, hold_a, got_a, hold_b, got_b, moment, across)
    sent_a = send_a
    got_a, got_b = minor(send_a, 1), minor(send_b, 3)
    hold_a, mine = lax.optimization_barrier((hold_a, mine))
    mine = mine + rest
    rest = along_y(mine, 3)
    both = [f32(192, 128), f32(128, 128), f32(128, 128), f32(128, 128)]
    send_a, hold_a, send_b, hold_b = call(merge_third, both, hold_a, sent_a, got_a, hold_b, got_b)
    got_a, got_b = minor(send_a, 3), minor(send_b, 1)
    hold_a, mine = lax.optimization_barrier((hold_a, mine))
    mine = mine + rest
    bary_tgt, = call(
        functools.partial(finish_sources, tgt_count=tgt_count), [bf16(cols, width)], mine, swap(mine), gain
    )
    hold_a, send_a, bary_tgt = lax.optimization_barrier((hold_a, send_a, bary_tgt))
    moment, = call(merge_moment, [f32(width // 2, width)], send_a, got_a)
    other = swap(moment)
    bary_src, = call(merge_last, [bf16(share, width)], hold_a, got_a, hold_b, got_b)
    bary_src, moment = lax.optimization_barrier((bary_src, moment))
    moment, = call(finish_moment, [f32(width, width)], moment, other)
    return (bary_src, bary_tgt, moment, row_potential.reshape(rows), col_potential.reshape(cols))


def solution(mesh):
    placed = (P("row", None), P("col", None), P(), P("col"))
    return jax.shard_map(
        local,
        mesh=mesh,
        in_specs=placed,
        out_specs=(P(("row", "col"), None), P("col", None), P(), P("row"), P("col")),
        check_vma=False,
    )
```

```python
import functools
import math

import jax
import jax.numpy as jnp
from jax import lax
from jax.experimental import pallas as pl
from jax.experimental.pallas import tpu as pltpu
from jax.sharding import PartitionSpec as P

F32 = jnp.float32
BF16 = jnp.bfloat16
NT = (((1,), (1,)), ((), ()))
TINY = 2.0**-80
SMALL, LARGE = 1e-30, 1e30
GUESS = 0.3
BLK = 512
CHUNK = 256
SLABS = BLK // 128
VMEM_LIMIT = 24 * 1024 * 1024


def split3(x):
    hi = x.astype(BF16).astype(F32)
    mid = (x - hi).astype(BF16).astype(F32)
    lo = (x - hi - mid).astype(BF16).astype(F32)
    return hi, mid, lo


def iota(shape, dim):
    return lax.broadcasted_iota(jnp.int32, shape, dim)


def lanes(b, size):
    if isinstance(b, int):
        return slice(b * size, (b + 1) * size)
    return pl.ds(pl.multiple_of(b * size, size), size)


def aug_columns(shift):
    hi, mid, lo = split3(shift)
    lane = iota((shift.shape[0], 128), 1)
    out = jnp.where(lane < 3, 1.0, 0.0)
    out = jnp.where(lane == 3, hi, out)
    out = jnp.where(lane == 4, mid, out)
    out = jnp.where(lane == 5, lo, out)
    return out.astype(BF16)


def aug_rows(term):
    hi, mid, lo = split3(term)
    sub = iota((16, term.shape[1]), 0)
    out = jnp.where((sub >= 3) & (sub < 6), 1.0, 0.0)
    out = jnp.where(sub == 0, hi, out)
    out = jnp.where(sub == 1, mid, out)
    out = jnp.where(sub == 2, lo, out)
    zeros = jnp.zeros((112, term.shape[1]), BF16)
    return jnp.concatenate([out.astype(BF16), zeros], axis=0)


def log_sum(x):
    largest = jnp.max(x, axis=0, keepdims=True)
    return largest + jnp.log(jnp.sum(jnp.exp(x - largest), axis=0, keepdims=True))


def flat(x):
    return jnp.concatenate([x[i : i + 1, :] for i in range(x.shape[0])], axis=1)


def stack(x, width):
    return jnp.concatenate([x[:, i * width : (i + 1) * width] for i in range(x.shape[1] // width)], axis=0)


def column(x):
    return jnp.broadcast_to(x, (8, x.shape[1])).T[:, :1]


def identity(n):
    return jnp.where(iota((n, n), 0) == iota((n, n), 1), 1.0, 0.0).astype(BF16)


def first_rows(src_in, tgt_in, factor_in, start_in, lse, proj_t, aug, start, src, factor, sems):
    copies = [
        pltpu.make_async_copy(start_in, start, sems.at[0]),
        pltpu.make_async_copy(factor_in, factor, sems.at[1]),
        pltpu.make_async_copy(src_in, src, sems.at[2]),
        pltpu.make_async_copy(tgt_in, aug.at[:, pl.ds(0, 128)], sems.at[3]),
    ]
    for copy in copies:
        copy.start()
    copies[0].wait()
    aug[:, 128:] = aug_columns(column(flat(start[...])))
    for copy in copies[1:]:
        copy.wait()
    factor_t = factor[...].astype(F32).T.astype(BF16)
    proj_t[...] = lax.dot_general(factor_t, src[...], NT, preferred_element_type=F32).astype(BF16)
    blocks = src.shape[0] // BLK
    chunks = aug.shape[0] // CHUNK

    def scores(c, right):
        x = jnp.dot(aug[c * CHUNK : (c + 1) * CHUNK, :], right, preferred_element_type=F32)
        return x.reshape(CHUNK // 8, 8, BLK)

    tgt = aug[:, :128].astype(F32)
    reach = GUESS * jnp.sqrt(jnp.max(jnp.sum(tgt * tgt, axis=1, keepdims=True), axis=0, keepdims=True))
    totals, values = [], []
    for b in range(blocks):
        proj = proj_t[:, b * BLK : (b + 1) * BLK]
        wide = proj.astype(F32)
        shift = reach * jnp.sqrt(jnp.sum(wide * wide, axis=0, keepdims=True))
        right = jnp.concatenate([proj, aug_rows(-shift)], axis=0)
        total = jnp.zeros((8, BLK), F32)
        for c in range(chunks):
            total += jnp.sum(jnp.exp(scores(c, right)), axis=0)
        total = jnp.sum(total, axis=0, keepdims=True)
        totals.append(total)
        values.append(stack(shift + jnp.log(total), 128))
    lse[...] = jnp.broadcast_to(jnp.concatenate(values, axis=0)[None], lse.shape)
    totals = jnp.concatenate(totals, axis=0)
    good = jnp.where((totals > SMALL) & (totals < LARGE), 1.0, 0.0)

    @pl.when(jnp.min(good) < 0.5)
    def _():
        under = aug_rows(jnp.zeros((1, BLK), F32))

        def block(b, carry):
            right = jnp.concatenate([proj_t[:, lanes(b, BLK)], under], axis=0)
            largest = jnp.full((8, BLK), -jnp.inf, F32)
            total = jnp.zeros((8, BLK), F32)
            for c in range(chunks):
                x = scores(c, right)
                new = jnp.maximum(largest, jnp.max(x, axis=0))
                total = total * jnp.exp(largest - new) + jnp.sum(jnp.exp(x - new[None]), axis=0)
                largest = new
            top = jnp.max(largest, axis=0, keepdims=True)
            value = top + jnp.log(jnp.sum(total * jnp.exp(largest - top), axis=0, keepdims=True))
            for i in range(SLABS):
                row = jnp.broadcast_to(value[:, i * 128 : (i + 1) * 128][None], (lse.shape[0], 1, 128))
                lse[:, pl.ds(b * SLABS + i, 1), :] = row
            return carry

        lax.fori_loop(0, blocks, block, 0)


def transposes(src, tgt, src_t, tgt_t):
    eye = identity(128)
    tgt_t[...] = lax.dot_general(eye, tgt[...], NT, preferred_element_type=F32).astype(BF16)
    src_t[...] = lax.dot_general(eye, src[...], NT, preferred_element_type=F32).astype(BF16)


def first_columns(parts, proj_t, aug, start, kernel_t, lse, shift, rho, sums, spare):
    blocks = proj_t.shape[1] // BLK
    chunks = aug.shape[0] // CHUNK
    rho[...] = -log_sum(parts[...])[0]
    shift[...] = start[...]

    def right_of(b):
        term = jnp.concatenate([rho[pl.ds(b * SLABS + i, 1), :] for i in range(SLABS)], axis=1)
        return jnp.concatenate([proj_t[:, lanes(b, BLK)], aug_rows(term)], axis=0)

    def fold(x, op):
        out = x[:, :128]
        for i in range(1, BLK // 128):
            out = op(out, x[:, i * 128 : (i + 1) * 128])
        return out

    def fill(left, b):
        right = right_of(b)
        for c in range(chunks):
            rows = slice(c * CHUNK, (c + 1) * CHUNK)
            e = jnp.exp(jnp.dot(left[rows, :], right, preferred_element_type=F32))
            for i in range(SLABS):
                kernel_t[b * SLABS + i, rows, :] = e[:, i * 128 : (i + 1) * 128].astype(BF16)
            sums[rows, :] += fold(e, jnp.add)

    def column_sums():
        return stack(jnp.sum(sums[...].T, axis=0, keepdims=True), 128)

    sums[...] = jnp.zeros_like(sums)
    for b in range(blocks):
        fill(aug, b)
    total = column_sums()
    lse[...] = jnp.broadcast_to((jnp.log(total) - shift[...])[None], lse.shape)

    @pl.when(jnp.min(total) < TINY)
    def _():
        sums[...] = jnp.full(sums.shape, -jnp.inf, F32)

        def largest(b, carry):
            right = right_of(b)
            for c in range(chunks):
                rows = slice(c * CHUNK, (c + 1) * CHUNK)
                x = jnp.dot(aug[rows, :], right, preferred_element_type=F32)
                sums[rows, :] = jnp.maximum(sums[rows, :], fold(x, jnp.maximum))
            return carry

        lax.fori_loop(0, blocks, largest, 0)
        top = jnp.max(sums[...], axis=1, keepdims=True)
        spare[:, :128] = aug[:, :128]
        spare[:, 128:] = aug_columns(column(flat(start[...])) - top)
        shift[...] = start[...] - stack(jnp.broadcast_to(top, sums.shape).T[:1], 128)
        sums[...] = jnp.zeros_like(sums)

        def again(b, carry):
            fill(spare, b)
            return carry

        lax.fori_loop(0, blocks, again, 0)
        lse[...] = jnp.broadcast_to((jnp.log(column_sums()) - shift[...])[None], lse.shape)


def slabs(ref, first, count):
    return jnp.concatenate([ref[first + i] for i in range(count)], axis=1)


def second_rows(parts, shift, kernel_t, sums, weight, potential, *, src_count, tgt_count):
    total = log_sum(parts[...])[0]
    potential[...] = math.log(src_count) - math.log(tgt_count) - total
    w = jnp.exp(-math.log(tgt_count) - total - shift[...])
    weight[...] = w
    w = flat(w)
    hi = w.astype(BF16).astype(F32)
    sub = iota((16, w.shape[1]), 0)
    left = jnp.where(sub == 0, hi, jnp.where(sub == 1, w - hi, 0.0)).astype(BF16)
    values = []
    for b in range(kernel_t.shape[0] // SLABS):
        x = jnp.dot(left, slabs(kernel_t, b * SLABS, SLABS), preferred_element_type=F32)
        values.append(stack(x[:1] + x[1:2], 128))
    sums[...] = jnp.broadcast_to(jnp.concatenate(values, axis=0)[None], sums.shape)


def second_columns(parts, rho, kernel_t, src_t, weight, sums, keep, send, scale, potential, total, *, src_count):
    q = jnp.sum(parts[...], axis=0)
    u = 1.0 / (src_count * q)
    scale[...] = u
    potential[...] = rho[...] - 2.0 * math.log(src_count) - jnp.log(q)
    for b in range(kernel_t.shape[0] // SLABS):
        ub = flat(u[b * SLABS : (b + 1) * SLABS, :])
        hi = ub.astype(BF16).astype(F32)
        sub = iota((16, BLK), 0)
        low = jnp.where(sub == 0, hi, jnp.where(sub == 1, ub - hi, 0.0)).astype(BF16)
        scaled = (src_t[:, b * BLK : (b + 1) * BLK].astype(F32) * ub).astype(BF16)
        left = jnp.concatenate([scaled, low], axis=0)
        x = lax.dot_general(left, slabs(kernel_t, b * SLABS, SLABS), NT, preferred_element_type=F32)
        if b == 0:
            total[...] = x
        else:
            total[...] += x
    w = weight[...]
    sums[...] = jnp.broadcast_to((w * stack(total[128:129, :] + total[129:130, :], 128))[None], sums.shape)
    w = flat(w)
    half = keep.shape[0]
    own = lax.rem(lax.axis_index("row"), 2) * half
    keep[...] = total[pl.ds(pl.multiple_of(own, half), half), :] * w
    send[...] = total[pl.ds(pl.multiple_of(half - own, half), half), :] * w


def on_first_core():
    return lax.rem(lax.axis_index("row"), 2) == 0


def share_of(major, minor):
    first = on_first_core()
    col = lax.axis_index("col")
    z = (col // 4) ^ jnp.where(first, major, minor)
    x = (col % 4) ^ jnp.where(first, minor, major)
    return z * 4 + x


SEND = ((1, 2), (3, 2))
STAY = ((0, 3), (0, 1))


def mix(left, kernel_t, scale, outs, offsets, src_count):
    for k in range(8):
        at = [share_of(offsets[h][k // 4], k % 4) * 2 + h for h in range(2)]
        pair = jnp.concatenate([kernel_t[i] for i in at], axis=1)
        x = jnp.dot(left, pair, preferred_element_type=F32)
        for h in range(2):
            u = scale[pl.ds(at[h], 1), :] * src_count
            outs[h][k * 128 : (k + 1) * 128, :] = x[:, h * 128 : (h + 1) * 128] * u


def target_send(
    parts, weight, before, tgt_t, kernel_t, scale, out_a, out_b, left, potential, gain, *, src_count, tgt_count
):
    total = jnp.sum(parts[...], axis=0)
    g = 1.0 / (tgt_count * total)
    gain[...] = g
    potential[...] = before[...] - math.log(tgt_count) - jnp.log(total)
    value = (tgt_t[...].astype(F32) * flat(weight[...] * g)).astype(BF16)
    left[...] = value
    mix(value, kernel_t, scale, (out_a, out_b), SEND, src_count)


def target_keep(left, kernel_t, scale, out_a, out_b, *, src_count):
    mix(left[...], kernel_t, scale, (out_a, out_b), STAY, src_count)


def moment_half(mine, gain, tgt, out):
    out[...] = jnp.dot(
        mine[...] * flat(gain[...]), tgt[...].astype(F32), precision=lax.Precision.HIGHEST, preferred_element_type=F32
    )


def in_order(mine, other):
    first = on_first_core()
    return jnp.concatenate([jnp.where(first, mine, other), jnp.where(first, other, mine)], axis=0)


def finish_sources(mine, other, gain, out, *, tgt_count):
    out[...] = (in_order(mine[...], other[...]) * (flat(gain[...]) * tgt_count)).T.astype(BF16)


def merge_first(keep_a, got_a, keep_b, got_b, moment, send_a, hold_a, send_b, hold_b):
    for keep, got, send, hold in ((keep_a, got_a, send_a, hold_a), (keep_b, got_b, send_b, hold_b)):
        hold[...] = keep[:512, :] + got[:512, :]
        send[:512, :] = keep[512:, :] + got[512:, :]
        send[512:, :] = moment[...]


def merge_second(hold_a, got_a, hold_b, got_b, moment, across, send_1, send_2, send_3, stay):
    total = (moment[...] + got_b[512:, :]) + (across[...] + got_a[512:, :])
    for minor, out in enumerate((stay, send_1, send_2, send_3)):
        rows = slice(minor * 128, (minor + 1) * 128)
        out[:128, :] = hold_a[rows, :] + got_a[rows, :]
        out[128:256, :] = hold_b[rows, :] + got_b[rows, :]
        out[256:, :] = total


def merge_moment(stay, got_1, got_2, got_3, out):
    out[...] = (stay[256:, :] + got_1[256:, :]) + (got_2[256:, :] + got_3[256:, :])


def merge_last(stay, got_1, got_2, got_3, bary):
    for half in range(2):
        rows = slice(half * 128, (half + 1) * 128)
        x = (stay[rows, :] + got_1[rows, :]) + (got_2[rows, :] + got_3[rows, :])
        bary[rows, :] = x.T.astype(BF16)


def finish_moment(mine, other, out):
    out[...] = in_order(mine[...], other[...])


def call(body, outs, *args, scratch=(), spaces=None, flops=1):
    spaces = spaces or {}
    return pl.pallas_call(
        body,
        out_shape=outs,
        in_specs=[pl.BlockSpec(memory_space=spaces.get(i, pltpu.VMEM)) for i in range(len(args))],
        out_specs=jax.tree.map(lambda _: pl.BlockSpec(memory_space=pltpu.VMEM), outs),
        scratch_shapes=list(scratch),
        cost_estimate=pl.CostEstimate(flops=flops, bytes_accessed=1, transcendentals=0),
        compiler_params=pltpu.CompilerParams(vmem_limit_bytes=VMEM_LIMIT),
    )(*args)


def f32(*shape):
    return jax.ShapeDtypeStruct(shape, F32)


def bf16(*shape):
    return jax.ShapeDtypeStruct(shape, BF16)


def near(x):
    return pltpu.with_memory_space_constraint(x, pltpu.VMEM)


def far(x):
    return pltpu.with_memory_space_constraint(x, pltpu.HBM)


def local(src_emb, tgt_emb, cost_factor, col_start):
    rows, cols = src_emb.shape[0], tgt_emb.shape[0]
    width = src_emb.shape[1]
    row_size, col_size = lax.axis_size("row"), lax.axis_size("col")
    src_count, tgt_count = rows * row_size, cols * col_size
    counts = dict(src_count=src_count, tgt_count=tgt_count)
    share = rows // col_size
    row_shape, col_shape = (rows // 128, 128), (cols // 128, 128)

    def swap(x):
        return lax.ppermute(x, "row", [(i, i ^ 1) for i in range(row_size)])

    def by_core(x, step):
        pairs = []
        for i in range(row_size * col_size):
            row, col = divmod(i, col_size)
            y, z, w = step(row % 2, row // 2, col // 4, col % 4)
            pairs.append((i, (y * 2 + row % 2) * col_size + z * 4 + w))
        return lax.ppermute(x, ("row", "col"), pairs)

    def major(x, k):
        return by_core(x, lambda c, y, z, w: (y, z, w ^ k) if c else (y, z ^ k, w))

    def minor(x, k):
        return by_core(x, lambda c, y, z, w: (y, z ^ k, w) if c else (y, z, w ^ k))

    def opposite_y(x):
        return by_core(x, lambda c, y, z, w: (y ^ 2, z, w))

    def along_y(x, k):
        return by_core(x, lambda c, y, z, w: (y ^ k ^ 2 * c, z, w))

    def exchange(x, axis):
        return lax.all_to_all(x, axis, 0, 0)

    lse, proj_t, aug, start = call(
        first_rows,
        [f32(col_size, *row_shape), bf16(width, rows), bf16(cols, 2 * width), f32(*col_shape)],
        far(src_emb), far(tgt_emb), far(cost_factor), far(col_start.reshape(col_shape)),
        scratch=[
            pltpu.VMEM((rows, width), BF16),
            pltpu.VMEM((width, width), BF16),
            pltpu.SemaphoreType.DMA((4,)),
        ],
        spaces={i: pltpu.HBM for i in range(4)},
    )
    parts = exchange(lse, "col")
    src_late, tgt_late, _ = lax.optimization_barrier((src_emb, tgt_emb, proj_t))
    src_t, tgt_t = call(transposes, [bf16(width, rows), bf16(width, cols)], src_late, tgt_late)
    parts, src_t, tgt_t = lax.optimization_barrier((parts, src_t, tgt_t))
    kernel_t, lse, shift, rho = call(
        first_columns,
        [pltpu.VMEM((rows // 128, cols, 128), BF16), f32(row_size, *col_shape), f32(*col_shape), f32(*row_shape)],
        parts, proj_t, aug, start,
        scratch=[pltpu.VMEM((cols, 128), F32), pltpu.VMEM((cols, 2 * width), BF16)],
    )
    parts = exchange(lse, "row")
    sums, weight, before = call(
        functools.partial(second_rows, **counts),
        [f32(col_size, *row_shape), f32(*col_shape), f32(*col_shape)],
        parts, shift, near(kernel_t),
    )
    parts = exchange(sums, "col")
    sums, keep, send, scale, row_potential = call(
        functools.partial(second_columns, src_count=src_count),
        [f32(row_size, *col_shape), f32(width // 2, cols), f32(width // 2, cols), f32(*row_shape), f32(*row_shape)],
        parts, rho, near(kernel_t), src_t, weight,
        scratch=[pltpu.VMEM((width + 16, cols), F32)],
    )
    parts = exchange(sums, "row")
    parts, send = lax.optimization_barrier((parts, send))
    other = swap(send)
    message = f32(8 * width, share // 2)
    send_a, send_b, left, col_potential, gain = call(
        functools.partial(target_send, **counts),
        [message, message, bf16(width, cols), f32(*col_shape), f32(*col_shape)],
        parts, weight, before, tgt_t, near(kernel_t), scale,
        flops=4 * width * cols * rows,
    )
    got_a, got_b = major(send_a, 1), major(send_b, 3)
    keep_a, keep_b = call(
        functools.partial(target_keep, src_count=src_count), [message, message], left, near(kernel_t), scale
    )
    mine = keep + other
    moment, = call(moment_half, [f32(width // 2, width)], mine, gain, tgt_emb)
    mine, moment = lax.optimization_barrier((mine, moment))
    rest = along_y(mine, 1)
    moment = (moment + along_y(moment, 1)) + (opposite_y(moment) + along_y(moment, 3))
    keep_a, moment, mine = lax.optimization_barrier((keep_a, moment, mine))
    both = [f32(576, 128), f32(512, 128)] * 2
    send_a, hold_a, send_b, hold_b = call(merge_first, both, keep_a, got_a, keep_b, got_b, moment)
    got_a, got_b, across = major(send_a, 3), major(send_b, 1), major(moment, 2)
    hold_a, mine = lax.optimization_barrier((hold_a, mine))
    mine = mine + rest
    rest = along_y(mine, 3)
    sends = call(merge_second, [f32(320, 128)] * 4, hold_a, got_a, hold_b, got_b, moment, across)
    stay = sends[3]
    got = [minor(sends[0], 1), minor(sends[1], 2), minor(sends[2], 3)]
    stay, mine = lax.optimization_barrier((stay, mine))
    mine = mine + rest
    bary_tgt, = call(
        functools.partial(finish_sources, tgt_count=tgt_count), [bf16(cols, width)], mine, swap(mine), gain
    )
    stay, bary_tgt = lax.optimization_barrier((stay, bary_tgt))
    moment, = call(merge_moment, [f32(width // 2, width)], stay, *got)
    other = swap(moment)
    bary_src, = call(merge_last, [bf16(share, width)], stay, *got)
    bary_src, moment = lax.optimization_barrier((bary_src, moment))
    moment, = call(finish_moment, [f32(width, width)], moment, other)
    return (bary_src, bary_tgt, moment, row_potential.reshape(rows), col_potential.reshape(cols))


def solution(mesh):
    placed = (P("row", None), P("col", None), P(), P("col"))
    return jax.shard_map(
        local,
        mesh=mesh,
        in_specs=placed,
        out_specs=(P(("row", "col"), None), P("col", None), P(), P("row"), P("col")),
        check_vma=False,
    )
```

```python
import functools
import math

import jax
import jax.numpy as jnp
from jax import lax
from jax.experimental import pallas as pl
from jax.experimental.pallas import tpu as pltpu
from jax.sharding import PartitionSpec as P

F32 = jnp.float32
BF16 = jnp.bfloat16
NT = (((1,), (1,)), ((), ()))
TINY = 2.0**-80
SMALL, LARGE = 1e-30, 1e30
GUESS = 0.3
BLK = 512
CHUNK = 256
SLABS = BLK // 128
VMEM_LIMIT = 24 * 1024 * 1024


def split3(x):
    hi = x.astype(BF16).astype(F32)
    mid = (x - hi).astype(BF16).astype(F32)
    lo = (x - hi - mid).astype(BF16).astype(F32)
    return hi, mid, lo


def iota(shape, dim):
    return lax.broadcasted_iota(jnp.int32, shape, dim)


def lanes(b, size):
    if isinstance(b, int):
        return slice(b * size, (b + 1) * size)
    return pl.ds(pl.multiple_of(b * size, size), size)


def aug_columns(shift):
    hi, mid, lo = split3(shift)
    lane = iota((shift.shape[0], 128), 1)
    out = jnp.where(lane < 3, 1.0, 0.0)
    out = jnp.where(lane == 3, hi, out)
    out = jnp.where(lane == 4, mid, out)
    out = jnp.where(lane == 5, lo, out)
    return out.astype(BF16)


def aug_rows(term):
    hi, mid, lo = split3(term)
    sub = iota((16, term.shape[1]), 0)
    out = jnp.where((sub >= 3) & (sub < 6), 1.0, 0.0)
    out = jnp.where(sub == 0, hi, out)
    out = jnp.where(sub == 1, mid, out)
    out = jnp.where(sub == 2, lo, out)
    zeros = jnp.zeros((112, term.shape[1]), BF16)
    return jnp.concatenate([out.astype(BF16), zeros], axis=0)


def log_sum(x):
    largest = jnp.max(x, axis=0, keepdims=True)
    return largest + jnp.log(jnp.sum(jnp.exp(x - largest), axis=0, keepdims=True))


def flat(x):
    return jnp.concatenate([x[i : i + 1, :] for i in range(x.shape[0])], axis=1)


def stack(x, width):
    return jnp.concatenate([x[:, i * width : (i + 1) * width] for i in range(x.shape[1] // width)], axis=0)


def column(x):
    return jnp.broadcast_to(x, (8, x.shape[1])).T[:, :1]


def identity(n):
    return jnp.where(iota((n, n), 0) == iota((n, n), 1), 1.0, 0.0).astype(BF16)


def first_rows(src_in, tgt_in, factor_in, start_in, lse, proj_t, aug, start, src, factor, sems):
    copies = [
        pltpu.make_async_copy(start_in, start, sems.at[0]),
        pltpu.make_async_copy(factor_in, factor, sems.at[1]),
        pltpu.make_async_copy(src_in, src, sems.at[2]),
        pltpu.make_async_copy(tgt_in, aug.at[:, pl.ds(0, 128)], sems.at[3]),
    ]
    for copy in copies:
        copy.start()
    copies[0].wait()
    aug[:, 128:] = aug_columns(column(flat(start[...])))
    for copy in copies[1:]:
        copy.wait()
    factor_t = factor[...].astype(F32).T.astype(BF16)
    proj_t[...] = lax.dot_general(factor_t, src[...], NT, preferred_element_type=F32).astype(BF16)
    blocks = src.shape[0] // BLK
    chunks = aug.shape[0] // CHUNK

    def scores(c, right):
        x = jnp.dot(aug[c * CHUNK : (c + 1) * CHUNK, :], right, preferred_element_type=F32)
        return x.reshape(CHUNK // 8, 8, BLK)

    tgt = aug[:, :128].astype(F32)
    reach = GUESS * jnp.sqrt(jnp.max(jnp.sum(tgt * tgt, axis=1, keepdims=True), axis=0, keepdims=True))
    totals, values = [], []
    for b in range(blocks):
        proj = proj_t[:, b * BLK : (b + 1) * BLK]
        wide = proj.astype(F32)
        shift = reach * jnp.sqrt(jnp.sum(wide * wide, axis=0, keepdims=True))
        right = jnp.concatenate([proj, aug_rows(-shift)], axis=0)
        total = jnp.zeros((8, BLK), F32)
        for c in range(chunks):
            total += jnp.sum(jnp.exp(scores(c, right)), axis=0)
        total = jnp.sum(total, axis=0, keepdims=True)
        totals.append(total)
        values.append(stack(shift + jnp.log(total), 128))
    lse[...] = jnp.broadcast_to(jnp.concatenate(values, axis=0)[None], lse.shape)
    totals = jnp.concatenate(totals, axis=0)
    good = jnp.where((totals > SMALL) & (totals < LARGE), 1.0, 0.0)

    @pl.when(jnp.min(good) < 0.5)
    def _():
        under = aug_rows(jnp.zeros((1, BLK), F32))

        def block(b, carry):
            right = jnp.concatenate([proj_t[:, lanes(b, BLK)], under], axis=0)
            largest = jnp.full((8, BLK), -jnp.inf, F32)
            total = jnp.zeros((8, BLK), F32)
            for c in range(chunks):
                x = scores(c, right)
                new = jnp.maximum(largest, jnp.max(x, axis=0))
                total = total * jnp.exp(largest - new) + jnp.sum(jnp.exp(x - new[None]), axis=0)
                largest = new
            top = jnp.max(largest, axis=0, keepdims=True)
            value = top + jnp.log(jnp.sum(total * jnp.exp(largest - top), axis=0, keepdims=True))
            for i in range(SLABS):
                row = jnp.broadcast_to(value[:, i * 128 : (i + 1) * 128][None], (lse.shape[0], 1, 128))
                lse[:, pl.ds(b * SLABS + i, 1), :] = row
            return carry

        lax.fori_loop(0, blocks, block, 0)


def transposes(src, tgt, src_t, tgt_t):
    eye = identity(128)
    tgt_t[...] = lax.dot_general(eye, tgt[...], NT, preferred_element_type=F32).astype(BF16)
    src_t[...] = lax.dot_general(eye, src[...], NT, preferred_element_type=F32).astype(BF16)


def first_columns(parts, proj_t, aug, start, kernel_t, lse, shift, rho, sums, spare):
    blocks = proj_t.shape[1] // BLK
    chunks = aug.shape[0] // CHUNK
    rho[...] = -log_sum(parts[...])[0]
    shift[...] = start[...]

    def right_of(b):
        term = jnp.concatenate([rho[pl.ds(b * SLABS + i, 1), :] for i in range(SLABS)], axis=1)
        return jnp.concatenate([proj_t[:, lanes(b, BLK)], aug_rows(term)], axis=0)

    def fold(x, op):
        out = x[:, :128]
        for i in range(1, BLK // 128):
            out = op(out, x[:, i * 128 : (i + 1) * 128])
        return out

    def fill(left, b):
        right = right_of(b)
        for c in range(chunks):
            rows = slice(c * CHUNK, (c + 1) * CHUNK)
            e = jnp.exp(jnp.dot(left[rows, :], right, preferred_element_type=F32))
            for i in range(SLABS):
                kernel_t[b * SLABS + i, rows, :] = e[:, i * 128 : (i + 1) * 128].astype(BF16)
            sums[rows, :] += fold(e, jnp.add)

    def column_sums():
        return stack(jnp.sum(sums[...].T, axis=0, keepdims=True), 128)

    sums[...] = jnp.zeros_like(sums)
    for b in range(blocks):
        fill(aug, b)
    total = column_sums()
    lse[...] = jnp.broadcast_to((jnp.log(total) - shift[...])[None], lse.shape)

    @pl.when(jnp.min(total) < TINY)
    def _():
        sums[...] = jnp.full(sums.shape, -jnp.inf, F32)

        def largest(b, carry):
            right = right_of(b)
            for c in range(chunks):
                rows = slice(c * CHUNK, (c + 1) * CHUNK)
                x = jnp.dot(aug[rows, :], right, preferred_element_type=F32)
                sums[rows, :] = jnp.maximum(sums[rows, :], fold(x, jnp.maximum))
            return carry

        lax.fori_loop(0, blocks, largest, 0)
        top = jnp.max(sums[...], axis=1, keepdims=True)
        spare[:, :128] = aug[:, :128]
        spare[:, 128:] = aug_columns(column(flat(start[...])) - top)
        shift[...] = start[...] - stack(jnp.broadcast_to(top, sums.shape).T[:1], 128)
        sums[...] = jnp.zeros_like(sums)

        def again(b, carry):
            fill(spare, b)
            return carry

        lax.fori_loop(0, blocks, again, 0)
        lse[...] = jnp.broadcast_to((jnp.log(column_sums()) - shift[...])[None], lse.shape)


def slabs(ref, first, count):
    return jnp.concatenate([ref[first + i] for i in range(count)], axis=1)


def second_rows(parts, shift, kernel_t, sums, weight, potential, *, src_count, tgt_count):
    total = log_sum(parts[...])[0]
    potential[...] = math.log(src_count) - math.log(tgt_count) - total
    w = jnp.exp(-math.log(tgt_count) - total - shift[...])
    weight[...] = w
    w = flat(w)
    hi = w.astype(BF16).astype(F32)
    sub = iota((16, w.shape[1]), 0)
    left = jnp.where(sub == 0, hi, jnp.where(sub == 1, w - hi, 0.0)).astype(BF16)
    values = []
    for b in range(kernel_t.shape[0] // SLABS):
        x = jnp.dot(left, slabs(kernel_t, b * SLABS, SLABS), preferred_element_type=F32)
        values.append(stack(x[:1] + x[1:2], 128))
    sums[...] = jnp.broadcast_to(jnp.concatenate(values, axis=0)[None], sums.shape)


def second_columns(parts, rho, kernel_t, src_t, weight, sums, keep, send, scale, potential, total, *, src_count):
    q = jnp.sum(parts[...], axis=0)
    u = 1.0 / (src_count * q)
    scale[...] = u
    potential[...] = rho[...] - 2.0 * math.log(src_count) - jnp.log(q)
    for b in range(kernel_t.shape[0] // SLABS):
        ub = flat(u[b * SLABS : (b + 1) * SLABS, :])
        hi = ub.astype(BF16).astype(F32)
        sub = iota((16, BLK), 0)
        low = jnp.where(sub == 0, hi, jnp.where(sub == 1, ub - hi, 0.0)).astype(BF16)
        scaled = (src_t[:, b * BLK : (b + 1) * BLK].astype(F32) * ub).astype(BF16)
        left = jnp.concatenate([scaled, low], axis=0)
        x = lax.dot_general(left, slabs(kernel_t, b * SLABS, SLABS), NT, preferred_element_type=F32)
        if b == 0:
            total[...] = x
        else:
            total[...] += x
    w = weight[...]
    sums[...] = jnp.broadcast_to((w * stack(total[128:129, :] + total[129:130, :], 128))[None], sums.shape)
    w = flat(w)
    half = keep.shape[0]
    own = lax.rem(lax.axis_index("row"), 2) * half
    keep[...] = total[pl.ds(pl.multiple_of(own, half), half), :] * w
    send[...] = total[pl.ds(pl.multiple_of(half - own, half), half), :] * w


def on_first_core():
    return lax.rem(lax.axis_index("row"), 2) == 0


def share_of(major, minor):
    first = on_first_core()
    col = lax.axis_index("col")
    z = (col // 4) ^ jnp.where(first, major, minor)
    x = (col % 4) ^ jnp.where(first, minor, major)
    return z * 4 + x


SEND = ((1, 2), (3, 2))
STAY = ((0, 3), (0, 1))


def mix(left, kernel_t, scale, outs, offsets, src_count):
    for k in range(8):
        at = [share_of(offsets[h][k // 4], k % 4) * 2 + h for h in range(2)]
        pair = jnp.concatenate([kernel_t[i] for i in at], axis=1)
        x = jnp.dot(left, pair, preferred_element_type=F32)
        for h in range(2):
            u = scale[pl.ds(at[h], 1), :] * src_count
            outs[h][k * 128 : (k + 1) * 128, :] = x[:, h * 128 : (h + 1) * 128] * u


def target_send(
    parts, weight, before, tgt_t, kernel_t, scale, out_a, out_b, left, potential, gain, *, src_count, tgt_count
):
    total = jnp.sum(parts[...], axis=0)
    g = 1.0 / (tgt_count * total)
    gain[...] = g
    potential[...] = before[...] - math.log(tgt_count) - jnp.log(total)
    value = (tgt_t[...].astype(F32) * flat(weight[...] * g)).astype(BF16)
    left[...] = value
    mix(value, kernel_t, scale, (out_a, out_b), SEND, src_count)


def target_keep(left, kernel_t, scale, out_a, out_b, *, src_count):
    mix(left[...], kernel_t, scale, (out_a, out_b), STAY, src_count)


def moment_half(mine, gain, tgt, out):
    out[...] = jnp.dot(
        mine[...] * flat(gain[...]), tgt[...].astype(F32), precision=lax.Precision.HIGHEST, preferred_element_type=F32
    )


def in_order(mine, other):
    first = on_first_core()
    return jnp.concatenate([jnp.where(first, mine, other), jnp.where(first, other, mine)], axis=0)


def finish_sources(mine, other, gain, out, *, tgt_count):
    out[...] = (in_order(mine[...], other[...]) * (flat(gain[...]) * tgt_count)).T.astype(BF16)


def merge_first(keep_a, got_a, keep_b, got_b, moment, send_a, hold_a, send_b, hold_b):
    for keep, got, send, hold in ((keep_a, got_a, send_a, hold_a), (keep_b, got_b, send_b, hold_b)):
        hold[...] = keep[:512, :] + got[:512, :]
        send[:512, :] = keep[512:, :] + got[512:, :]
        send[512:, :] = moment[...]


def merge_second(hold_a, got_a, hold_b, got_b, moment, across, send_1, send_2, send_3, stay):
    total = (moment[...] + got_b[512:, :]) + (across[...] + got_a[512:, :])
    for minor, out in enumerate((stay, send_1, send_2, send_3)):
        rows = slice(minor * 128, (minor + 1) * 128)
        out[:128, :] = hold_a[rows, :] + got_a[rows, :]
        out[128:256, :] = hold_b[rows, :] + got_b[rows, :]
        out[256:, :] = total


def merge_moment(stay, got_1, got_2, got_3, out):
    out[...] = (stay[256:, :] + got_1[256:, :]) + (got_2[256:, :] + got_3[256:, :])


def merge_last(stay, got_1, got_2, got_3, bary):
    for half in range(2):
        rows = slice(half * 128, (half + 1) * 128)
        x = (stay[rows, :] + got_1[rows, :]) + (got_2[rows, :] + got_3[rows, :])
        bary[rows, :] = x.T.astype(BF16)


def finish_moment(mine, other, out):
    out[...] = in_order(mine[...], other[...])


def call(body, outs, *args, scratch=(), spaces=None, flops=1):
    spaces = spaces or {}
    return pl.pallas_call(
        body,
        out_shape=outs,
        in_specs=[pl.BlockSpec(memory_space=spaces.get(i, pltpu.VMEM)) for i in range(len(args))],
        out_specs=jax.tree.map(lambda _: pl.BlockSpec(memory_space=pltpu.VMEM), outs),
        scratch_shapes=list(scratch),
        cost_estimate=pl.CostEstimate(flops=flops, bytes_accessed=1, transcendentals=0),
        compiler_params=pltpu.CompilerParams(vmem_limit_bytes=VMEM_LIMIT),
    )(*args)


def f32(*shape):
    return jax.ShapeDtypeStruct(shape, F32)


def bf16(*shape):
    return jax.ShapeDtypeStruct(shape, BF16)


def near(x):
    return pltpu.with_memory_space_constraint(x, pltpu.VMEM)


def far(x):
    return pltpu.with_memory_space_constraint(x, pltpu.HBM)


def local(src_emb, tgt_emb, cost_factor, col_start):
    rows, cols = src_emb.shape[0], tgt_emb.shape[0]
    width = src_emb.shape[1]
    row_size, col_size = lax.axis_size("row"), lax.axis_size("col")
    src_count, tgt_count = rows * row_size, cols * col_size
    counts = dict(src_count=src_count, tgt_count=tgt_count)
    share = rows // col_size
    row_shape, col_shape = (rows // 128, 128), (cols // 128, 128)

    def swap(x):
        return lax.ppermute(x, "row", [(i, i ^ 1) for i in range(row_size)])

    def by_core(x, step):
        pairs = []
        for i in range(row_size * col_size):
            row, col = divmod(i, col_size)
            y, z, w = step(row % 2, row // 2, col // 4, col % 4)
            pairs.append((i, (y * 2 + row % 2) * col_size + z * 4 + w))
        return lax.ppermute(x, ("row", "col"), pairs)

    def major(x, k):
        return by_core(x, lambda c, y, z, w: (y, z, w ^ k) if c else (y, z ^ k, w))

    def minor(x, k):
        return by_core(x, lambda c, y, z, w: (y, z ^ k, w) if c else (y, z, w ^ k))

    def opposite_y(x):
        return by_core(x, lambda c, y, z, w: (y ^ 2, z, w))

    def along_y(x, k):
        return by_core(x, lambda c, y, z, w: (y ^ k ^ 2 * c, z, w))

    def exchange(x, axis):
        return lax.all_to_all(x, axis, 0, 0)

    lse, proj_t, aug, start = call(
        first_rows,
        [f32(col_size, *row_shape), bf16(width, rows), bf16(cols, 2 * width), f32(*col_shape)],
        far(src_emb), far(tgt_emb), far(cost_factor), far(col_start.reshape(col_shape)),
        scratch=[
            pltpu.VMEM((rows, width), BF16),
            pltpu.VMEM((width, width), BF16),
            pltpu.SemaphoreType.DMA((4,)),
        ],
        spaces={i: pltpu.HBM for i in range(4)},
    )
    parts = exchange(lse, "col")
    src_late, tgt_late, _ = lax.optimization_barrier((src_emb, tgt_emb, proj_t))
    src_t, tgt_t = call(transposes, [bf16(width, rows), bf16(width, cols)], src_late, tgt_late)
    parts, src_t, tgt_t = lax.optimization_barrier((parts, src_t, tgt_t))
    kernel_t, lse, shift, rho = call(
        first_columns,
        [pltpu.VMEM((rows // 128, cols, 128), BF16), f32(row_size, *col_shape), f32(*col_shape), f32(*row_shape)],
        parts, proj_t, aug, start,
        scratch=[pltpu.VMEM((cols, 128), F32), pltpu.VMEM((cols, 2 * width), BF16)],
    )
    parts = exchange(lse, "row")
    sums, weight, before = call(
        functools.partial(second_rows, **counts),
        [f32(col_size, *row_shape), f32(*col_shape), f32(*col_shape)],
        parts, shift, near(kernel_t),
    )
    parts = exchange(sums, "col")
    sums, keep, send, scale, row_potential = call(
        functools.partial(second_columns, src_count=src_count),
        [f32(row_size, *col_shape), f32(width // 2, cols), f32(width // 2, cols), f32(*row_shape), f32(*row_shape)],
        parts, rho, near(kernel_t), src_t, weight,
        scratch=[pltpu.VMEM((width + 16, cols), F32)],
    )
    parts = exchange(sums, "row")
    parts, send = lax.optimization_barrier((parts, send))
    other = swap(send)
    message = f32(8 * width, share // 2)
    send_a, send_b, left, col_potential, gain = call(
        functools.partial(target_send, **counts),
        [message, message, bf16(width, cols), f32(*col_shape), f32(*col_shape)],
        parts, weight, before, tgt_t, near(kernel_t), scale,
        flops=4 * width * cols * rows,
    )
    got_a, got_b = major(send_a, 1), major(send_b, 3)
    keep_a, keep_b = call(
        functools.partial(target_keep, src_count=src_count), [message, message], left, near(kernel_t), scale
    )
    mine = keep + other
    moment, = call(moment_half, [f32(width // 2, width)], mine, gain, tgt_emb)
    mine = mine + along_y(mine, 1)
    moment = (moment + along_y(moment, 1)) + (opposite_y(moment) + along_y(moment, 3))
    keep_a, moment, mine = lax.optimization_barrier((keep_a, moment, mine))
    both = [f32(576, 128), f32(512, 128)] * 2
    send_a, hold_a, send_b, hold_b = call(merge_first, both, keep_a, got_a, keep_b, got_b, moment)
    got_a, got_b, across = major(send_a, 3), major(send_b, 1), major(moment, 2)
    hold_a, mine = lax.optimization_barrier((hold_a, mine))
    rest = along_y(mine, 3)
    sends = call(merge_second, [f32(320, 128)] * 4, hold_a, got_a, hold_b, got_b, moment, across)
    stay = sends[3]
    got = [minor(sends[0], 1), minor(sends[1], 2), minor(sends[2], 3)]
    stay, mine = lax.optimization_barrier((stay, mine))
    mine = mine + rest
    bary_tgt, = call(
        functools.partial(finish_sources, tgt_count=tgt_count), [bf16(cols, width)], mine, swap(mine), gain
    )
    stay, bary_tgt = lax.optimization_barrier((stay, bary_tgt))
    moment, = call(merge_moment, [f32(width // 2, width)], stay, *got)
    other = swap(moment)
    bary_src, = call(merge_last, [bf16(share, width)], stay, *got)
    bary_src, moment = lax.optimization_barrier((bary_src, moment))
    moment, = call(finish_moment, [f32(width, width)], moment, other)
    return (bary_src, bary_tgt, moment, row_potential.reshape(rows), col_potential.reshape(cols))


def solution(mesh):
    placed = (P("row", None), P("col", None), P(), P("col"))
    return jax.shard_map(
        local,
        mesh=mesh,
        in_specs=placed,
        out_specs=(P(("row", "col"), None), P("col", None), P(), P("row"), P("col")),
        check_vma=False,
    )
```

```python
import functools
import math

import jax
import jax.numpy as jnp
from jax import lax
from jax.experimental import pallas as pl
from jax.experimental.pallas import tpu as pltpu
from jax.sharding import PartitionSpec as P

F32 = jnp.float32
BF16 = jnp.bfloat16
NT = (((1,), (1,)), ((), ()))
TINY = 2.0**-80
SMALL, LARGE = 1e-30, 1e30
GUESS = 0.3
BLK = 512
CHUNK = 256
SLABS = BLK // 128
VMEM_LIMIT = 24 * 1024 * 1024


def split3(x):
    hi = x.astype(BF16).astype(F32)
    mid = (x - hi).astype(BF16).astype(F32)
    lo = (x - hi - mid).astype(BF16).astype(F32)
    return hi, mid, lo


def iota(shape, dim):
    return lax.broadcasted_iota(jnp.int32, shape, dim)


def lanes(b, size):
    if isinstance(b, int):
        return slice(b * size, (b + 1) * size)
    return pl.ds(pl.multiple_of(b * size, size), size)


def aug_columns(shift):
    hi, mid, lo = split3(shift)
    lane = iota((shift.shape[0], 128), 1)
    out = jnp.where(lane < 3, 1.0, 0.0)
    out = jnp.where(lane == 3, hi, out)
    out = jnp.where(lane == 4, mid, out)
    out = jnp.where(lane == 5, lo, out)
    return out.astype(BF16)


def aug_rows(term):
    hi, mid, lo = split3(term)
    sub = iota((16, term.shape[1]), 0)
    out = jnp.where((sub >= 3) & (sub < 6), 1.0, 0.0)
    out = jnp.where(sub == 0, hi, out)
    out = jnp.where(sub == 1, mid, out)
    out = jnp.where(sub == 2, lo, out)
    zeros = jnp.zeros((112, term.shape[1]), BF16)
    return jnp.concatenate([out.astype(BF16), zeros], axis=0)


def log_sum(x):
    largest = jnp.max(x, axis=0, keepdims=True)
    return largest + jnp.log(jnp.sum(jnp.exp(x - largest), axis=0, keepdims=True))


def flat(x):
    return jnp.concatenate([x[i : i + 1, :] for i in range(x.shape[0])], axis=1)


def stack(x, width):
    return jnp.concatenate([x[:, i * width : (i + 1) * width] for i in range(x.shape[1] // width)], axis=0)


def column(x):
    return jnp.broadcast_to(x, (8, x.shape[1])).T[:, :1]


def identity(n):
    return jnp.where(iota((n, n), 0) == iota((n, n), 1), 1.0, 0.0).astype(BF16)


def first_rows(src_in, tgt_in, factor_in, start_in, lse, proj_t, aug, start, src, factor, sems):
    copies = [
        pltpu.make_async_copy(start_in, start, sems.at[0]),
        pltpu.make_async_copy(factor_in, factor, sems.at[1]),
        pltpu.make_async_copy(src_in, src, sems.at[2]),
        pltpu.make_async_copy(tgt_in, aug.at[:, pl.ds(0, 128)], sems.at[3]),
    ]
    for copy in copies:
        copy.start()
    copies[0].wait()
    aug[:, 128:] = aug_columns(column(flat(start[...])))
    for copy in copies[1:]:
        copy.wait()
    factor_t = factor[...].astype(F32).T.astype(BF16)
    proj_t[...] = lax.dot_general(factor_t, src[...], NT, preferred_element_type=F32).astype(BF16)
    blocks = src.shape[0] // BLK
    chunks = aug.shape[0] // CHUNK

    def scores(c, right):
        x = jnp.dot(aug[c * CHUNK : (c + 1) * CHUNK, :], right, preferred_element_type=F32)
        return x.reshape(CHUNK // 8, 8, BLK)

    tgt = aug[:, :128].astype(F32)
    reach = GUESS * jnp.sqrt(jnp.max(jnp.sum(tgt * tgt, axis=1, keepdims=True), axis=0, keepdims=True))
    totals, values = [], []
    for b in range(blocks):
        proj = proj_t[:, b * BLK : (b + 1) * BLK]
        wide = proj.astype(F32)
        shift = reach * jnp.sqrt(jnp.sum(wide * wide, axis=0, keepdims=True))
        right = jnp.concatenate([proj, aug_rows(-shift)], axis=0)
        total = jnp.zeros((8, BLK), F32)
        for c in range(chunks):
            total += jnp.sum(jnp.exp(scores(c, right)), axis=0)
        total = jnp.sum(total, axis=0, keepdims=True)
        totals.append(total)
        values.append(stack(shift + jnp.log(total), 128))
    lse[...] = jnp.broadcast_to(jnp.concatenate(values, axis=0)[None], lse.shape)
    totals = jnp.concatenate(totals, axis=0)
    good = jnp.where((totals > SMALL) & (totals < LARGE), 1.0, 0.0)

    @pl.when(jnp.min(good) < 0.5)
    def _():
        under = aug_rows(jnp.zeros((1, BLK), F32))

        def block(b, carry):
            right = jnp.concatenate([proj_t[:, lanes(b, BLK)], under], axis=0)
            largest = jnp.full((8, BLK), -jnp.inf, F32)
            total = jnp.zeros((8, BLK), F32)
            for c in range(chunks):
                x = scores(c, right)
                new = jnp.maximum(largest, jnp.max(x, axis=0))
                total = total * jnp.exp(largest - new) + jnp.sum(jnp.exp(x - new[None]), axis=0)
                largest = new
            top = jnp.max(largest, axis=0, keepdims=True)
            value = top + jnp.log(jnp.sum(total * jnp.exp(largest - top), axis=0, keepdims=True))
            for i in range(SLABS):
                row = jnp.broadcast_to(value[:, i * 128 : (i + 1) * 128][None], (lse.shape[0], 1, 128))
                lse[:, pl.ds(b * SLABS + i, 1), :] = row
            return carry

        lax.fori_loop(0, blocks, block, 0)


def transposes(src, tgt, src_t, tgt_t):
    eye = identity(128)
    tgt_t[...] = lax.dot_general(eye, tgt[...], NT, preferred_element_type=F32).astype(BF16)
    src_t[...] = lax.dot_general(eye, src[...], NT, preferred_element_type=F32).astype(BF16)


def first_columns(parts, proj_t, aug, start, kernel_t, lse, shift, rho, sums, spare):
    blocks = proj_t.shape[1] // BLK
    chunks = aug.shape[0] // CHUNK
    rho[...] = -log_sum(parts[...])[0]
    shift[...] = start[...]

    def right_of(b):
        term = jnp.concatenate([rho[pl.ds(b * SLABS + i, 1), :] for i in range(SLABS)], axis=1)
        return jnp.concatenate([proj_t[:, lanes(b, BLK)], aug_rows(term)], axis=0)

    def fold(x, op):
        out = x[:, :128]
        for i in range(1, BLK // 128):
            out = op(out, x[:, i * 128 : (i + 1) * 128])
        return out

    def fill(left, b):
        right = right_of(b)
        for c in range(chunks):
            rows = slice(c * CHUNK, (c + 1) * CHUNK)
            e = jnp.exp(jnp.dot(left[rows, :], right, preferred_element_type=F32))
            for i in range(SLABS):
                kernel_t[b * SLABS + i, rows, :] = e[:, i * 128 : (i + 1) * 128].astype(BF16)
            sums[rows, :] += fold(e, jnp.add)

    def column_sums():
        return stack(jnp.sum(sums[...].T, axis=0, keepdims=True), 128)

    sums[...] = jnp.zeros_like(sums)
    for b in range(blocks):
        fill(aug, b)
    total = column_sums()
    lse[...] = jnp.broadcast_to((jnp.log(total) - shift[...])[None], lse.shape)

    @pl.when(jnp.min(total) < TINY)
    def _():
        sums[...] = jnp.full(sums.shape, -jnp.inf, F32)

        def largest(b, carry):
            right = right_of(b)
            for c in range(chunks):
                rows = slice(c * CHUNK, (c + 1) * CHUNK)
                x = jnp.dot(aug[rows, :], right, preferred_element_type=F32)
                sums[rows, :] = jnp.maximum(sums[rows, :], fold(x, jnp.maximum))
            return carry

        lax.fori_loop(0, blocks, largest, 0)
        top = jnp.max(sums[...], axis=1, keepdims=True)
        spare[:, :128] = aug[:, :128]
        spare[:, 128:] = aug_columns(column(flat(start[...])) - top)
        shift[...] = start[...] - stack(jnp.broadcast_to(top, sums.shape).T[:1], 128)
        sums[...] = jnp.zeros_like(sums)

        def again(b, carry):
            fill(spare, b)
            return carry

        lax.fori_loop(0, blocks, again, 0)
        lse[...] = jnp.broadcast_to((jnp.log(column_sums()) - shift[...])[None], lse.shape)


def slabs(ref, first, count):
    return jnp.concatenate([ref[first + i] for i in range(count)], axis=1)


def second_rows(parts, shift, kernel_t, sums, weight, potential, *, src_count, tgt_count):
    total = log_sum(parts[...])[0]
    potential[...] = math.log(src_count) - math.log(tgt_count) - total
    w = jnp.exp(-math.log(tgt_count) - total - shift[...])
    weight[...] = w
    w = flat(w)
    hi = w.astype(BF16).astype(F32)
    sub = iota((16, w.shape[1]), 0)
    left = jnp.where(sub == 0, hi, jnp.where(sub == 1, w - hi, 0.0)).astype(BF16)
    values = []
    for b in range(kernel_t.shape[0] // SLABS):
        x = jnp.dot(left, slabs(kernel_t, b * SLABS, SLABS), preferred_element_type=F32)
        values.append(stack(x[:1] + x[1:2], 128))
    sums[...] = jnp.broadcast_to(jnp.concatenate(values, axis=0)[None], sums.shape)


def second_columns(parts, rho, kernel_t, src_t, weight, sums, keep, send, scale, potential, total, *, src_count):
    q = jnp.sum(parts[...], axis=0)
    u = 1.0 / (src_count * q)
    scale[...] = u
    potential[...] = rho[...] - 2.0 * math.log(src_count) - jnp.log(q)
    for b in range(kernel_t.shape[0] // SLABS):
        ub = flat(u[b * SLABS : (b + 1) * SLABS, :])
        hi = ub.astype(BF16).astype(F32)
        sub = iota((16, BLK), 0)
        low = jnp.where(sub == 0, hi, jnp.where(sub == 1, ub - hi, 0.0)).astype(BF16)
        scaled = (src_t[:, b * BLK : (b + 1) * BLK].astype(F32) * ub).astype(BF16)
        left = jnp.concatenate([scaled, low], axis=0)
        x = lax.dot_general(left, slabs(kernel_t, b * SLABS, SLABS), NT, preferred_element_type=F32)
        if b == 0:
            total[...] = x
        else:
            total[...] += x
    w = weight[...]
    sums[...] = jnp.broadcast_to((w * stack(total[128:129, :] + total[129:130, :], 128))[None], sums.shape)
    w = flat(w)
    half = keep.shape[0]
    own = lax.rem(lax.axis_index("row"), 2) * half
    keep[...] = total[pl.ds(pl.multiple_of(own, half), half), :] * w
    send[...] = total[pl.ds(pl.multiple_of(half - own, half), half), :] * w


def on_first_core():
    return lax.rem(lax.axis_index("row"), 2) == 0


def share_of(major, minor):
    first = on_first_core()
    col = lax.axis_index("col")
    z = (col // 4) ^ jnp.where(first, major, minor)
    x = (col % 4) ^ jnp.where(first, minor, major)
    return z * 4 + x


SEND = ((1, 2), (3, 2))
STAY = ((0, 3), (0, 1))


def mix(left, kernel_t, scale, outs, offsets, src_count):
    for k in range(8):
        at = [share_of(offsets[h][k // 4], k % 4) * 2 + h for h in range(2)]
        pair = jnp.concatenate([kernel_t[i] for i in at], axis=1)
        x = jnp.dot(left, pair, preferred_element_type=F32)
        for h in range(2):
            u = scale[pl.ds(at[h], 1), :] * src_count
            outs[h][k * 128 : (k + 1) * 128, :] = x[:, h * 128 : (h + 1) * 128] * u


def target_send(
    parts, weight, before, tgt_t, kernel_t, scale, out_a, out_b, left, potential, gain, *, src_count, tgt_count
):
    total = jnp.sum(parts[...], axis=0)
    g = 1.0 / (tgt_count * total)
    gain[...] = g
    potential[...] = before[...] - math.log(tgt_count) - jnp.log(total)
    value = (tgt_t[...].astype(F32) * flat(weight[...] * g)).astype(BF16)
    left[...] = value
    mix(value, kernel_t, scale, (out_a, out_b), SEND, src_count)


def target_keep(left, kernel_t, scale, out_a, out_b, *, src_count):
    mix(left[...], kernel_t, scale, (out_a, out_b), STAY, src_count)


def moment_half(mine, gain, tgt, out):
    out[...] = jnp.dot(
        mine[...] * flat(gain[...]), tgt[...].astype(F32), precision=lax.Precision.HIGHEST, preferred_element_type=F32
    )


def in_order(mine, other):
    first = on_first_core()
    return jnp.concatenate([jnp.where(first, mine, other), jnp.where(first, other, mine)], axis=0)


def finish_sources(mine, other, gain, out, *, tgt_count):
    out[...] = (in_order(mine[...], other[...]) * (flat(gain[...]) * tgt_count)).T.astype(BF16)


def merge_first(keep_a, got_a, keep_b, got_b, moment, send_a, hold_a, send_b, hold_b):
    for keep, got, send, hold in ((keep_a, got_a, send_a, hold_a), (keep_b, got_b, send_b, hold_b)):
        hold[...] = keep[:512, :] + got[:512, :]
        send[:512, :] = keep[512:, :] + got[512:, :]
        send[512:, :] = moment[...]


def merge_second(hold_a, got_a, hold_b, got_b, moment, across, send_2, send_1, send_3, stay):
    total = (moment[...] + got_b[512:, :]) + (across[...] + got_a[512:, :])
    for minor, out in enumerate((stay, send_1, send_2, send_3)):
        rows = slice(minor * 128, (minor + 1) * 128)
        out[:128, :] = hold_a[rows, :] + got_a[rows, :]
        out[128:256, :] = hold_b[rows, :] + got_b[rows, :]
        out[256:, :] = total


def merge_moment(stay, got_2, got_1, got_3, out):
    out[...] = (stay[256:, :] + got_1[256:, :]) + (got_2[256:, :] + got_3[256:, :])


def merge_last(stay, got_2, got_1, got_3, bary):
    for half in range(2):
        rows = slice(half * 128, (half + 1) * 128)
        x = (stay[rows, :] + got_1[rows, :]) + (got_2[rows, :] + got_3[rows, :])
        bary[rows, :] = x.T.astype(BF16)


def finish_moment(mine, other, out):
    out[...] = in_order(mine[...], other[...])


def call(body, outs, *args, scratch=(), spaces=None, flops=1):
    spaces = spaces or {}
    return pl.pallas_call(
        body,
        out_shape=outs,
        in_specs=[pl.BlockSpec(memory_space=spaces.get(i, pltpu.VMEM)) for i in range(len(args))],
        out_specs=jax.tree.map(lambda _: pl.BlockSpec(memory_space=pltpu.VMEM), outs),
        scratch_shapes=list(scratch),
        cost_estimate=pl.CostEstimate(flops=flops, bytes_accessed=1, transcendentals=0),
        compiler_params=pltpu.CompilerParams(vmem_limit_bytes=VMEM_LIMIT),
    )(*args)


def f32(*shape):
    return jax.ShapeDtypeStruct(shape, F32)


def bf16(*shape):
    return jax.ShapeDtypeStruct(shape, BF16)


def near(x):
    return pltpu.with_memory_space_constraint(x, pltpu.VMEM)


def far(x):
    return pltpu.with_memory_space_constraint(x, pltpu.HBM)


def local(src_emb, tgt_emb, cost_factor, col_start):
    rows, cols = src_emb.shape[0], tgt_emb.shape[0]
    width = src_emb.shape[1]
    row_size, col_size = lax.axis_size("row"), lax.axis_size("col")
    src_count, tgt_count = rows * row_size, cols * col_size
    counts = dict(src_count=src_count, tgt_count=tgt_count)
    share = rows // col_size
    row_shape, col_shape = (rows // 128, 128), (cols // 128, 128)

    def swap(x):
        return lax.ppermute(x, "row", [(i, i ^ 1) for i in range(row_size)])

    def by_core(x, step):
        pairs = []
        for i in range(row_size * col_size):
            row, col = divmod(i, col_size)
            y, z, w = step(row % 2, row // 2, col // 4, col % 4)
            pairs.append((i, (y * 2 + row % 2) * col_size + z * 4 + w))
        return lax.ppermute(x, ("row", "col"), pairs)

    def major(x, k):
        return by_core(x, lambda c, y, z, w: (y, z, w ^ k) if c else (y, z ^ k, w))

    def minor(x, k):
        return by_core(x, lambda c, y, z, w: (y, z ^ k, w) if c else (y, z, w ^ k))

    def opposite_y(x):
        return by_core(x, lambda c, y, z, w: (y ^ 2, z, w))

    def along_y(x, k):
        return by_core(x, lambda c, y, z, w: (y ^ k ^ 2 * c, z, w))

    def exchange(x, axis):
        return lax.all_to_all(x, axis, 0, 0)

    lse, proj_t, aug, start = call(
        first_rows,
        [f32(col_size, *row_shape), bf16(width, rows), bf16(cols, 2 * width), f32(*col_shape)],
        far(src_emb), far(tgt_emb), far(cost_factor), far(col_start.reshape(col_shape)),
        scratch=[
            pltpu.VMEM((rows, width), BF16),
            pltpu.VMEM((width, width), BF16),
            pltpu.SemaphoreType.DMA((4,)),
        ],
        spaces={i: pltpu.HBM for i in range(4)},
    )
    parts = exchange(lse, "col")
    src_late, tgt_late, _ = lax.optimization_barrier((src_emb, tgt_emb, proj_t))
    src_t, tgt_t = call(transposes, [bf16(width, rows), bf16(width, cols)], src_late, tgt_late)
    parts, src_t, tgt_t = lax.optimization_barrier((parts, src_t, tgt_t))
    kernel_t, lse, shift, rho = call(
        first_columns,
        [pltpu.VMEM((rows // 128, cols, 128), BF16), f32(row_size, *col_shape), f32(*col_shape), f32(*row_shape)],
        parts, proj_t, aug, start,
        scratch=[pltpu.VMEM((cols, 128), F32), pltpu.VMEM((cols, 2 * width), BF16)],
    )
    parts = exchange(lse, "row")
    sums, weight, before = call(
        functools.partial(second_rows, **counts),
        [f32(col_size, *row_shape), f32(*col_shape), f32(*col_shape)],
        parts, shift, near(kernel_t),
    )
    parts = exchange(sums, "col")
    sums, keep, send, scale, row_potential = call(
        functools.partial(second_columns, src_count=src_count),
        [f32(row_size, *col_shape), f32(width // 2, cols), f32(width // 2, cols), f32(*row_shape), f32(*row_shape)],
        parts, rho, near(kernel_t), src_t, weight,
        scratch=[pltpu.VMEM((width + 16, cols), F32)],
    )
    parts = exchange(sums, "row")
    parts, send = lax.optimization_barrier((parts, send))
    other = swap(send)
    message = f32(8 * width, share // 2)
    send_a, send_b, left, col_potential, gain = call(
        functools.partial(target_send, **counts),
        [message, message, bf16(width, cols), f32(*col_shape), f32(*col_shape)],
        parts, weight, before, tgt_t, near(kernel_t), scale,
        flops=4 * width * cols * rows,
    )
    got_a, got_b = major(send_a, 1), major(send_b, 3)
    keep_a, keep_b = call(
        functools.partial(target_keep, src_count=src_count), [message, message], left, near(kernel_t), scale
    )
    mine = keep + other
    moment, = call(moment_half, [f32(width // 2, width)], mine, gain, tgt_emb)
    mine = mine + along_y(mine, 1)
    moment = (moment + along_y(moment, 1)) + (opposite_y(moment) + along_y(moment, 3))
    keep_a, moment, mine = lax.optimization_barrier((keep_a, moment, mine))
    both = [f32(576, 128), f32(512, 128)] * 2
    send_a, hold_a, send_b, hold_b = call(merge_first, both, keep_a, got_a, keep_b, got_b, moment)
    got_a, got_b, across = major(send_a, 3), major(send_b, 1), major(moment, 2)
    hold_a, mine = lax.optimization_barrier((hold_a, mine))
    rest = along_y(mine, 3)
    sends = call(merge_second, [f32(320, 128)] * 4, hold_a, got_a, hold_b, got_b, moment, across)
    stay = sends[3]
    got = [minor(sends[0], 2), minor(sends[1], 1), minor(sends[2], 3)]
    stay, mine = lax.optimization_barrier((stay, mine))
    mine = mine + rest
    bary_tgt, = call(
        functools.partial(finish_sources, tgt_count=tgt_count), [bf16(cols, width)], mine, swap(mine), gain
    )
    stay, bary_tgt = lax.optimization_barrier((stay, bary_tgt))
    moment, = call(merge_moment, [f32(width // 2, width)], stay, *got)
    other = swap(moment)
    bary_src, = call(merge_last, [bf16(share, width)], stay, *got)
    bary_src, moment = lax.optimization_barrier((bary_src, moment))
    moment, = call(finish_moment, [f32(width, width)], moment, other)
    return (bary_src, bary_tgt, moment, row_potential.reshape(rows), col_potential.reshape(cols))


def solution(mesh):
    placed = (P("row", None), P("col", None), P(), P("col"))
    return jax.shard_map(
        local,
        mesh=mesh,
        in_specs=placed,
        out_specs=(P(("row", "col"), None), P("col", None), P(), P("row"), P("col")),
        check_vma=False,
    )
```

```python
import functools
import math

import jax
import jax.numpy as jnp
from jax import lax
from jax.experimental import pallas as pl
from jax.experimental.pallas import tpu as pltpu
from jax.sharding import PartitionSpec as P

F32 = jnp.float32
BF16 = jnp.bfloat16
NT = (((1,), (1,)), ((), ()))
TINY = 2.0**-80
SMALL, LARGE = 1e-30, 1e30
GUESS = 0.3
BLK = 512
CHUNK = 256
SLABS = BLK // 128
VMEM_LIMIT = 24 * 1024 * 1024


def split3(x):
    hi = x.astype(BF16).astype(F32)
    mid = (x - hi).astype(BF16).astype(F32)
    lo = (x - hi - mid).astype(BF16).astype(F32)
    return hi, mid, lo


def iota(shape, dim):
    return lax.broadcasted_iota(jnp.int32, shape, dim)


def lanes(b, size):
    if isinstance(b, int):
        return slice(b * size, (b + 1) * size)
    return pl.ds(pl.multiple_of(b * size, size), size)


def aug_columns(shift):
    hi, mid, lo = split3(shift)
    lane = iota((shift.shape[0], 128), 1)
    out = jnp.where(lane < 3, 1.0, 0.0)
    out = jnp.where(lane == 3, hi, out)
    out = jnp.where(lane == 4, mid, out)
    out = jnp.where(lane == 5, lo, out)
    return out.astype(BF16)


def aug_rows(term):
    hi, mid, lo = split3(term)
    sub = iota((16, term.shape[1]), 0)
    out = jnp.where((sub >= 3) & (sub < 6), 1.0, 0.0)
    out = jnp.where(sub == 0, hi, out)
    out = jnp.where(sub == 1, mid, out)
    out = jnp.where(sub == 2, lo, out)
    zeros = jnp.zeros((112, term.shape[1]), BF16)
    return jnp.concatenate([out.astype(BF16), zeros], axis=0)


def log_sum(x):
    largest = jnp.max(x, axis=0, keepdims=True)
    return largest + jnp.log(jnp.sum(jnp.exp(x - largest), axis=0, keepdims=True))


def flat(x):
    return jnp.concatenate([x[i : i + 1, :] for i in range(x.shape[0])], axis=1)


def stack(x, width):
    return jnp.concatenate([x[:, i * width : (i + 1) * width] for i in range(x.shape[1] // width)], axis=0)


def column(x):
    return jnp.broadcast_to(x, (8, x.shape[1])).T[:, :1]


def identity(n):
    return jnp.where(iota((n, n), 0) == iota((n, n), 1), 1.0, 0.0).astype(BF16)


def first_rows(src_in, tgt_in, factor_in, start_in, lse, proj_t, aug, start, src, factor, sems):
    copies = [
        pltpu.make_async_copy(start_in, start, sems.at[0]),
        pltpu.make_async_copy(factor_in, factor, sems.at[1]),
        pltpu.make_async_copy(src_in, src, sems.at[2]),
        pltpu.make_async_copy(tgt_in, aug.at[:, pl.ds(0, 128)], sems.at[3]),
    ]
    for copy in copies:
        copy.start()
    copies[0].wait()
    aug[:, 128:] = aug_columns(column(flat(start[...])))
    for copy in copies[1:]:
        copy.wait()
    factor_t = factor[...].astype(F32).T.astype(BF16)
    proj_t[...] = lax.dot_general(factor_t, src[...], NT, preferred_element_type=F32).astype(BF16)
    blocks = src.shape[0] // BLK
    chunks = aug.shape[0] // CHUNK

    def scores(c, right):
        x = jnp.dot(aug[c * CHUNK : (c + 1) * CHUNK, :], right, preferred_element_type=F32)
        return x.reshape(CHUNK // 8, 8, BLK)

    tgt = aug[:, :128].astype(F32)
    reach = GUESS * jnp.sqrt(jnp.max(jnp.sum(tgt * tgt, axis=1, keepdims=True), axis=0, keepdims=True))
    totals, values = [], []
    for b in range(blocks):
        proj = proj_t[:, b * BLK : (b + 1) * BLK]
        wide = proj.astype(F32)
        shift = reach * jnp.sqrt(jnp.sum(wide * wide, axis=0, keepdims=True))
        right = jnp.concatenate([proj, aug_rows(-shift)], axis=0)
        total = jnp.zeros((8, BLK), F32)
        for c in range(chunks):
            total += jnp.sum(jnp.exp(scores(c, right)), axis=0)
        total = jnp.sum(total, axis=0, keepdims=True)
        totals.append(total)
        values.append(stack(shift + jnp.log(total), 128))
    lse[...] = jnp.broadcast_to(jnp.concatenate(values, axis=0)[None], lse.shape)
    totals = jnp.concatenate(totals, axis=0)
    good = jnp.where((totals > SMALL) & (totals < LARGE), 1.0, 0.0)

    @pl.when(jnp.min(good) < 0.5)
    def _():
        under = aug_rows(jnp.zeros((1, BLK), F32))

        def block(b, carry):
            right = jnp.concatenate([proj_t[:, lanes(b, BLK)], under], axis=0)
            largest = jnp.full((8, BLK), -jnp.inf, F32)
            total = jnp.zeros((8, BLK), F32)
            for c in range(chunks):
                x = scores(c, right)
                new = jnp.maximum(largest, jnp.max(x, axis=0))
                total = total * jnp.exp(largest - new) + jnp.sum(jnp.exp(x - new[None]), axis=0)
                largest = new
            top = jnp.max(largest, axis=0, keepdims=True)
            value = top + jnp.log(jnp.sum(total * jnp.exp(largest - top), axis=0, keepdims=True))
            for i in range(SLABS):
                row = jnp.broadcast_to(value[:, i * 128 : (i + 1) * 128][None], (lse.shape[0], 1, 128))
                lse[:, pl.ds(b * SLABS + i, 1), :] = row
            return carry

        lax.fori_loop(0, blocks, block, 0)


def transposes(src, tgt, src_t, tgt_t):
    eye = identity(128)
    tgt_t[...] = lax.dot_general(eye, tgt[...], NT, preferred_element_type=F32).astype(BF16)
    src_t[...] = lax.dot_general(eye, src[...], NT, preferred_element_type=F32).astype(BF16)


def first_columns(parts, proj_t, aug, start, kernel_t, lse, shift, rho, sums, spare):
    blocks = proj_t.shape[1] // BLK
    chunks = aug.shape[0] // CHUNK
    rho[...] = -log_sum(parts[...])[0]
    shift[...] = start[...]

    def right_of(b):
        term = jnp.concatenate([rho[pl.ds(b * SLABS + i, 1), :] for i in range(SLABS)], axis=1)
        return jnp.concatenate([proj_t[:, lanes(b, BLK)], aug_rows(term)], axis=0)

    def fold(x, op):
        out = x[:, :128]
        for i in range(1, BLK // 128):
            out = op(out, x[:, i * 128 : (i + 1) * 128])
        return out

    def fill(left, b):
        right = right_of(b)
        for c in range(chunks):
            rows = slice(c * CHUNK, (c + 1) * CHUNK)
            e = jnp.exp(jnp.dot(left[rows, :], right, preferred_element_type=F32))
            for i in range(SLABS):
                kernel_t[b * SLABS + i, rows, :] = e[:, i * 128 : (i + 1) * 128].astype(BF16)
            sums[rows, :] += fold(e, jnp.add)

    def column_sums():
        return stack(jnp.sum(sums[...].T, axis=0, keepdims=True), 128)

    sums[...] = jnp.zeros_like(sums)
    for b in range(blocks):
        fill(aug, b)
    total = column_sums()
    lse[...] = jnp.broadcast_to((jnp.log(total) - shift[...])[None], lse.shape)

    @pl.when(jnp.min(total) < TINY)
    def _():
        sums[...] = jnp.full(sums.shape, -jnp.inf, F32)

        def largest(b, carry):
            right = right_of(b)
            for c in range(chunks):
                rows = slice(c * CHUNK, (c + 1) * CHUNK)
                x = jnp.dot(aug[rows, :], right, preferred_element_type=F32)
                sums[rows, :] = jnp.maximum(sums[rows, :], fold(x, jnp.maximum))
            return carry

        lax.fori_loop(0, blocks, largest, 0)
        top = jnp.max(sums[...], axis=1, keepdims=True)
        spare[:, :128] = aug[:, :128]
        spare[:, 128:] = aug_columns(column(flat(start[...])) - top)
        shift[...] = start[...] - stack(jnp.broadcast_to(top, sums.shape).T[:1], 128)
        sums[...] = jnp.zeros_like(sums)

        def again(b, carry):
            fill(spare, b)
            return carry

        lax.fori_loop(0, blocks, again, 0)
        lse[...] = jnp.broadcast_to((jnp.log(column_sums()) - shift[...])[None], lse.shape)


def slabs(ref, first, count):
    return jnp.concatenate([ref[first + i] for i in range(count)], axis=1)


def second_rows(parts, shift, kernel_t, sums, weight, potential, *, src_count, tgt_count):
    total = log_sum(parts[...])[0]
    potential[...] = math.log(src_count) - math.log(tgt_count) - total
    w = jnp.exp(-math.log(tgt_count) - total - shift[...])
    weight[...] = w
    w = flat(w)
    hi = w.astype(BF16).astype(F32)
    sub = iota((16, w.shape[1]), 0)
    left = jnp.where(sub == 0, hi, jnp.where(sub == 1, w - hi, 0.0)).astype(BF16)
    values = []
    for b in range(kernel_t.shape[0] // SLABS):
        x = jnp.dot(left, slabs(kernel_t, b * SLABS, SLABS), preferred_element_type=F32)
        values.append(stack(x[:1] + x[1:2], 128))
    sums[...] = jnp.broadcast_to(jnp.concatenate(values, axis=0)[None], sums.shape)


def second_columns(parts, rho, kernel_t, src_t, weight, sums, keep, send, scale, potential, total, *, src_count):
    q = jnp.sum(parts[...], axis=0)
    u = 1.0 / (src_count * q)
    scale[...] = u
    potential[...] = rho[...] - 2.0 * math.log(src_count) - jnp.log(q)
    for b in range(kernel_t.shape[0] // SLABS):
        ub = flat(u[b * SLABS : (b + 1) * SLABS, :])
        hi = ub.astype(BF16).astype(F32)
        sub = iota((16, BLK), 0)
        low = jnp.where(sub == 0, hi, jnp.where(sub == 1, ub - hi, 0.0)).astype(BF16)
        scaled = (src_t[:, b * BLK : (b + 1) * BLK].astype(F32) * ub).astype(BF16)
        left = jnp.concatenate([scaled, low], axis=0)
        x = lax.dot_general(left, slabs(kernel_t, b * SLABS, SLABS), NT, preferred_element_type=F32)
        if b == 0:
            total[...] = x
        else:
            total[...] += x
    w = weight[...]
    sums[...] = jnp.broadcast_to((w * stack(total[128:129, :] + total[129:130, :], 128))[None], sums.shape)
    w = flat(w)
    half = keep.shape[0]
    own = lax.rem(lax.axis_index("row"), 2) * half
    keep[...] = total[pl.ds(pl.multiple_of(own, half), half), :] * w
    send[...] = total[pl.ds(pl.multiple_of(half - own, half), half), :] * w


def on_first_core():
    return lax.rem(lax.axis_index("row"), 2) == 0


def share_of(major, minor):
    first = on_first_core()
    col = lax.axis_index("col")
    z = (col // 4) ^ jnp.where(first, major, minor)
    x = (col % 4) ^ jnp.where(first, minor, major)
    return z * 4 + x


SEND = ((1, 2), (3, 2))
STAY = ((0, 3), (0, 1))


def mix(left, kernel_t, scale, outs, offsets, src_count):
    for k in range(8):
        at = [share_of(offsets[h][k // 4], k % 4) * 2 + h for h in range(2)]
        pair = jnp.concatenate([kernel_t[i] for i in at], axis=1)
        x = jnp.dot(left, pair, preferred_element_type=F32)
        for h in range(2):
            u = scale[pl.ds(at[h], 1), :] * src_count
            outs[h][k * 128 : (k + 1) * 128, :] = x[:, h * 128 : (h + 1) * 128] * u


def target_send(
    parts, weight, before, tgt_t, kernel_t, scale, out_a, out_b, left, potential, gain, *, src_count, tgt_count
):
    total = jnp.sum(parts[...], axis=0)
    g = 1.0 / (tgt_count * total)
    gain[...] = g
    potential[...] = before[...] - math.log(tgt_count) - jnp.log(total)
    value = (tgt_t[...].astype(F32) * flat(weight[...] * g)).astype(BF16)
    left[...] = value
    mix(value, kernel_t, scale, (out_a, out_b), SEND, src_count)


def target_keep(left, kernel_t, scale, out_a, out_b, *, src_count):
    mix(left[...], kernel_t, scale, (out_a, out_b), STAY, src_count)


def moment_half(mine, gain, tgt, out, both):
    x = jnp.dot(
        mine[...] * flat(gain[...]), tgt[...].astype(F32), precision=lax.Precision.HIGHEST, preferred_element_type=F32
    )
    out[...] = x
    both[:, : mine.shape[1]] = mine[...]
    both[:, mine.shape[1] :] = x


def in_order(mine, other):
    first = on_first_core()
    return jnp.concatenate([jnp.where(first, mine, other), jnp.where(first, other, mine)], axis=0)


def finish_sources(mine, other, gain, out, *, tgt_count):
    out[...] = (in_order(mine[...], other[...]) * (flat(gain[...]) * tgt_count)).T.astype(BF16)


def merge_first(keep_a, got_a, keep_b, got_b, moment, send_a, hold_a, send_b, hold_b):
    for keep, got, send, hold in ((keep_a, got_a, send_a, hold_a), (keep_b, got_b, send_b, hold_b)):
        hold[...] = keep[:512, :] + got[:512, :]
        send[:512, :] = keep[512:, :] + got[512:, :]
        send[512:, :] = moment[...]


def merge_second(hold_a, got_a, hold_b, got_b, moment, across, send_2, send_1, send_3, stay):
    total = (moment[...] + got_b[512:, :]) + (across[...] + got_a[512:, :])
    for minor, out in enumerate((stay, send_1, send_2, send_3)):
        rows = slice(minor * 128, (minor + 1) * 128)
        out[:128, :] = hold_a[rows, :] + got_a[rows, :]
        out[128:256, :] = hold_b[rows, :] + got_b[rows, :]
        out[256:, :] = total


def merge_moment(stay, got_2, got_1, got_3, out):
    out[...] = (stay[256:, :] + got_1[256:, :]) + (got_2[256:, :] + got_3[256:, :])


def merge_last(stay, got_2, got_1, got_3, bary):
    for half in range(2):
        rows = slice(half * 128, (half + 1) * 128)
        x = (stay[rows, :] + got_1[rows, :]) + (got_2[rows, :] + got_3[rows, :])
        bary[rows, :] = x.T.astype(BF16)


def finish_moment(mine, other, out):
    out[...] = in_order(mine[...], other[...])


def call(body, outs, *args, scratch=(), spaces=None, flops=1):
    spaces = spaces or {}
    return pl.pallas_call(
        body,
        out_shape=outs,
        in_specs=[pl.BlockSpec(memory_space=spaces.get(i, pltpu.VMEM)) for i in range(len(args))],
        out_specs=jax.tree.map(lambda _: pl.BlockSpec(memory_space=pltpu.VMEM), outs),
        scratch_shapes=list(scratch),
        cost_estimate=pl.CostEstimate(flops=flops, bytes_accessed=1, transcendentals=0),
        compiler_params=pltpu.CompilerParams(vmem_limit_bytes=VMEM_LIMIT),
    )(*args)


def f32(*shape):
    return jax.ShapeDtypeStruct(shape, F32)


def bf16(*shape):
    return jax.ShapeDtypeStruct(shape, BF16)


def near(x):
    return pltpu.with_memory_space_constraint(x, pltpu.VMEM)


def far(x):
    return pltpu.with_memory_space_constraint(x, pltpu.HBM)


def local(src_emb, tgt_emb, cost_factor, col_start):
    rows, cols = src_emb.shape[0], tgt_emb.shape[0]
    width = src_emb.shape[1]
    row_size, col_size = lax.axis_size("row"), lax.axis_size("col")
    src_count, tgt_count = rows * row_size, cols * col_size
    counts = dict(src_count=src_count, tgt_count=tgt_count)
    share = rows // col_size
    row_shape, col_shape = (rows // 128, 128), (cols // 128, 128)

    def swap(x):
        return lax.ppermute(x, "row", [(i, i ^ 1) for i in range(row_size)])

    def by_core(x, step):
        pairs = []
        for i in range(row_size * col_size):
            row, col = divmod(i, col_size)
            y, z, w = step(row % 2, row // 2, col // 4, col % 4)
            pairs.append((i, (y * 2 + row % 2) * col_size + z * 4 + w))
        return lax.ppermute(x, ("row", "col"), pairs)

    def major(x, k):
        return by_core(x, lambda c, y, z, w: (y, z, w ^ k) if c else (y, z ^ k, w))

    def minor(x, k):
        return by_core(x, lambda c, y, z, w: (y, z ^ k, w) if c else (y, z, w ^ k))

    def opposite_y(x):
        return by_core(x, lambda c, y, z, w: (y ^ 2, z, w))

    def along_y(x, k):
        return by_core(x, lambda c, y, z, w: (y ^ k ^ 2 * c, z, w))

    def exchange(x, axis):
        return lax.all_to_all(x, axis, 0, 0)

    lse, proj_t, aug, start = call(
        first_rows,
        [f32(col_size, *row_shape), bf16(width, rows), bf16(cols, 2 * width), f32(*col_shape)],
        far(src_emb), far(tgt_emb), far(cost_factor), far(col_start.reshape(col_shape)),
        scratch=[
            pltpu.VMEM((rows, width), BF16),
            pltpu.VMEM((width, width), BF16),
            pltpu.SemaphoreType.DMA((4,)),
        ],
        spaces={i: pltpu.HBM for i in range(4)},
    )
    parts = exchange(lse, "col")
    src_late, tgt_late, _ = lax.optimization_barrier((src_emb, tgt_emb, proj_t))
    src_t, tgt_t = call(transposes, [bf16(width, rows), bf16(width, cols)], src_late, tgt_late)
    parts, src_t, tgt_t = lax.optimization_barrier((parts, src_t, tgt_t))
    kernel_t, lse, shift, rho = call(
        first_columns,
        [pltpu.VMEM((rows // 128, cols, 128), BF16), f32(row_size, *col_shape), f32(*col_shape), f32(*row_shape)],
        parts, proj_t, aug, start,
        scratch=[pltpu.VMEM((cols, 128), F32), pltpu.VMEM((cols, 2 * width), BF16)],
    )
    parts = exchange(lse, "row")
    sums, weight, before = call(
        functools.partial(second_rows, **counts),
        [f32(col_size, *row_shape), f32(*col_shape), f32(*col_shape)],
        parts, shift, near(kernel_t),
    )
    parts = exchange(sums, "col")
    sums, keep, send, scale, row_potential = call(
        functools.partial(second_columns, src_count=src_count),
        [f32(row_size, *col_shape), f32(width // 2, cols), f32(width // 2, cols), f32(*row_shape), f32(*row_shape)],
        parts, rho, near(kernel_t), src_t, weight,
        scratch=[pltpu.VMEM((width + 16, cols), F32)],
    )
    parts = exchange(sums, "row")
    parts, send = lax.optimization_barrier((parts, send))
    other = swap(send)
    message = f32(8 * width, share // 2)
    send_a, send_b, left, col_potential, gain = call(
        functools.partial(target_send, **counts),
        [message, message, bf16(width, cols), f32(*col_shape), f32(*col_shape)],
        parts, weight, before, tgt_t, near(kernel_t), scale,
        flops=4 * width * cols * rows,
    )
    got_a, got_b = major(send_a, 1), major(send_b, 3)
    keep_a, keep_b = call(
        functools.partial(target_keep, src_count=src_count), [message, message], left, near(kernel_t), scale
    )
    mine = keep + other
    moment, both = call(
        moment_half, [f32(width // 2, width), f32(width // 2, cols + width)], mine, gain, tgt_emb
    )
    both = both + along_y(both, 1)
    mine = both[:, :cols]
    moment = both[:, cols:] + (opposite_y(moment) + along_y(moment, 3))
    keep_a, moment, mine = lax.optimization_barrier((keep_a, moment, mine))
    both = [f32(576, 128), f32(512, 128)] * 2
    send_a, hold_a, send_b, hold_b = call(merge_first, both, keep_a, got_a, keep_b, got_b, moment)
    got_a, got_b, across = major(send_a, 3), major(send_b, 1), major(moment, 2)
    hold_a, mine = lax.optimization_barrier((hold_a, mine))
    rest = along_y(mine, 3)
    sends = call(merge_second, [f32(320, 128)] * 4, hold_a, got_a, hold_b, got_b, moment, across)
    stay = sends[3]
    got = [minor(sends[0], 2), minor(sends[1], 1), minor(sends[2], 3)]
    stay, mine = lax.optimization_barrier((stay, mine))
    mine = mine + rest
    bary_tgt, = call(
        functools.partial(finish_sources, tgt_count=tgt_count), [bf16(cols, width)], mine, swap(mine), gain
    )
    stay, bary_tgt = lax.optimization_barrier((stay, bary_tgt))
    moment, = call(merge_moment, [f32(width // 2, width)], stay, *got)
    other = swap(moment)
    bary_src, = call(merge_last, [bf16(share, width)], stay, *got)
    bary_src, moment = lax.optimization_barrier((bary_src, moment))
    moment, = call(finish_moment, [f32(width, width)], moment, other)
    return (bary_src, bary_tgt, moment, row_potential.reshape(rows), col_potential.reshape(cols))


def solution(mesh):
    placed = (P("row", None), P("col", None), P(), P("col"))
    return jax.shard_map(
        local,
        mesh=mesh,
        in_specs=placed,
        out_specs=(P(("row", "col"), None), P("col", None), P(), P("row"), P("col")),
        check_vma=False,
    )
```

```python
import functools
import math

import jax
import jax.numpy as jnp
from jax import lax
from jax.experimental import pallas as pl
from jax.experimental.pallas import tpu as pltpu
from jax.sharding import PartitionSpec as P

F32 = jnp.float32
BF16 = jnp.bfloat16
NT = (((1,), (1,)), ((), ()))
TINY = 2.0**-80
SMALL, LARGE = 1e-30, 1e30
GUESS = 0.3
BLK = 512
CHUNK = 256
SLABS = BLK // 128
VMEM_LIMIT = 24 * 1024 * 1024


def split3(x):
    hi = x.astype(BF16).astype(F32)
    mid = (x - hi).astype(BF16).astype(F32)
    lo = (x - hi - mid).astype(BF16).astype(F32)
    return hi, mid, lo


def iota(shape, dim):
    return lax.broadcasted_iota(jnp.int32, shape, dim)


def lanes(b, size):
    if isinstance(b, int):
        return slice(b * size, (b + 1) * size)
    return pl.ds(pl.multiple_of(b * size, size), size)


def aug_columns(shift):
    hi, mid, lo = split3(shift)
    lane = iota((shift.shape[0], 128), 1)
    out = jnp.where(lane < 3, 1.0, 0.0)
    out = jnp.where(lane == 3, hi, out)
    out = jnp.where(lane == 4, mid, out)
    out = jnp.where(lane == 5, lo, out)
    return out.astype(BF16)


def aug_rows(term):
    hi, mid, lo = split3(term)
    sub = iota((16, term.shape[1]), 0)
    out = jnp.where((sub >= 3) & (sub < 6), 1.0, 0.0)
    out = jnp.where(sub == 0, hi, out)
    out = jnp.where(sub == 1, mid, out)
    out = jnp.where(sub == 2, lo, out)
    zeros = jnp.zeros((112, term.shape[1]), BF16)
    return jnp.concatenate([out.astype(BF16), zeros], axis=0)


def log_sum(x):
    largest = jnp.max(x, axis=0, keepdims=True)
    return largest + jnp.log(jnp.sum(jnp.exp(x - largest), axis=0, keepdims=True))


def flat(x):
    return jnp.concatenate([x[i : i + 1, :] for i in range(x.shape[0])], axis=1)


def stack(x, width):
    return jnp.concatenate([x[:, i * width : (i + 1) * width] for i in range(x.shape[1] // width)], axis=0)


def column(x):
    return jnp.broadcast_to(x, (8, x.shape[1])).T[:, :1]


def identity(n):
    return jnp.where(iota((n, n), 0) == iota((n, n), 1), 1.0, 0.0).astype(BF16)


def first_rows(src_in, tgt_in, factor_in, start_in, lse, proj_t, aug, start, src, factor, sems):
    copies = [
        pltpu.make_async_copy(start_in, start, sems.at[0]),
        pltpu.make_async_copy(factor_in, factor, sems.at[1]),
        pltpu.make_async_copy(src_in, src, sems.at[2]),
        pltpu.make_async_copy(tgt_in, aug.at[:, pl.ds(0, 128)], sems.at[3]),
    ]
    for copy in copies:
        copy.start()
    copies[0].wait()
    aug[:, 128:] = aug_columns(column(flat(start[...])))
    for copy in copies[1:]:
        copy.wait()
    factor_t = factor[...].astype(F32).T.astype(BF16)
    proj_t[...] = lax.dot_general(factor_t, src[...], NT, preferred_element_type=F32).astype(BF16)
    blocks = src.shape[0] // BLK
    chunks = aug.shape[0] // CHUNK

    def scores(c, right):
        x = jnp.dot(aug[c * CHUNK : (c + 1) * CHUNK, :], right, preferred_element_type=F32)
        return x.reshape(CHUNK // 8, 8, BLK)

    tgt = aug[:, :128].astype(F32)
    reach = GUESS * jnp.sqrt(jnp.max(jnp.sum(tgt * tgt, axis=1, keepdims=True), axis=0, keepdims=True))
    totals, values = [], []
    for b in range(blocks):
        proj = proj_t[:, b * BLK : (b + 1) * BLK]
        wide = proj.astype(F32)
        shift = reach * jnp.sqrt(jnp.sum(wide * wide, axis=0, keepdims=True))
        right = jnp.concatenate([proj, aug_rows(-shift)], axis=0)
        total = jnp.zeros((8, BLK), F32)
        for c in range(chunks):
            total += jnp.sum(jnp.exp(scores(c, right)), axis=0)
        total = jnp.sum(total, axis=0, keepdims=True)
        totals.append(total)
        values.append(stack(shift + jnp.log(total), 128))
    lse[...] = jnp.broadcast_to(jnp.concatenate(values, axis=0)[None], lse.shape)
    totals = jnp.concatenate(totals, axis=0)
    good = jnp.where((totals > SMALL) & (totals < LARGE), 1.0, 0.0)

    @pl.when(jnp.min(good) < 0.5)
    def _():
        under = aug_rows(jnp.zeros((1, BLK), F32))

        def block(b, carry):
            right = jnp.concatenate([proj_t[:, lanes(b, BLK)], under], axis=0)
            largest = jnp.full((8, BLK), -jnp.inf, F32)
            total = jnp.zeros((8, BLK), F32)
            for c in range(chunks):
                x = scores(c, right)
                new = jnp.maximum(largest, jnp.max(x, axis=0))
                total = total * jnp.exp(largest - new) + jnp.sum(jnp.exp(x - new[None]), axis=0)
                largest = new
            top = jnp.max(largest, axis=0, keepdims=True)
            value = top + jnp.log(jnp.sum(total * jnp.exp(largest - top), axis=0, keepdims=True))
            for i in range(SLABS):
                row = jnp.broadcast_to(value[:, i * 128 : (i + 1) * 128][None], (lse.shape[0], 1, 128))
                lse[:, pl.ds(b * SLABS + i, 1), :] = row
            return carry

        lax.fori_loop(0, blocks, block, 0)


def transposes(src, tgt, src_t, tgt_t):
    eye = identity(128)
    tgt_t[...] = lax.dot_general(eye, tgt[...], NT, preferred_element_type=F32).astype(BF16)
    src_t[...] = lax.dot_general(eye, src[...], NT, preferred_element_type=F32).astype(BF16)


def first_columns(parts, proj_t, aug, start, kernel_t, lse, shift, rho, sums, spare):
    blocks = proj_t.shape[1] // BLK
    chunks = aug.shape[0] // CHUNK
    rho[...] = -log_sum(parts[...])[0]
    shift[...] = start[...]

    def right_of(b):
        term = jnp.concatenate([rho[pl.ds(b * SLABS + i, 1), :] for i in range(SLABS)], axis=1)
        return jnp.concatenate([proj_t[:, lanes(b, BLK)], aug_rows(term)], axis=0)

    def fold(x, op):
        out = x[:, :128]
        for i in range(1, BLK // 128):
            out = op(out, x[:, i * 128 : (i + 1) * 128])
        return out

    def fill(left, b):
        right = right_of(b)
        for c in range(chunks):
            rows = slice(c * CHUNK, (c + 1) * CHUNK)
            e = jnp.exp(jnp.dot(left[rows, :], right, preferred_element_type=F32))
            for i in range(SLABS):
                kernel_t[b * SLABS + i, rows, :] = e[:, i * 128 : (i + 1) * 128].astype(BF16)
            sums[rows, :] += fold(e, jnp.add)

    def column_sums():
        return stack(jnp.sum(sums[...].T, axis=0, keepdims=True), 128)

    sums[...] = jnp.zeros_like(sums)
    for b in range(blocks):
        fill(aug, b)
    total = column_sums()
    lse[...] = jnp.broadcast_to((jnp.log(total) - shift[...])[None], lse.shape)

    @pl.when(jnp.min(total) < TINY)
    def _():
        sums[...] = jnp.full(sums.shape, -jnp.inf, F32)

        def largest(b, carry):
            right = right_of(b)
            for c in range(chunks):
                rows = slice(c * CHUNK, (c + 1) * CHUNK)
                x = jnp.dot(aug[rows, :], right, preferred_element_type=F32)
                sums[rows, :] = jnp.maximum(sums[rows, :], fold(x, jnp.maximum))
            return carry

        lax.fori_loop(0, blocks, largest, 0)
        top = jnp.max(sums[...], axis=1, keepdims=True)
        spare[:, :128] = aug[:, :128]
        spare[:, 128:] = aug_columns(column(flat(start[...])) - top)
        shift[...] = start[...] - stack(jnp.broadcast_to(top, sums.shape).T[:1], 128)
        sums[...] = jnp.zeros_like(sums)

        def again(b, carry):
            fill(spare, b)
            return carry

        lax.fori_loop(0, blocks, again, 0)
        lse[...] = jnp.broadcast_to((jnp.log(column_sums()) - shift[...])[None], lse.shape)


def slabs(ref, first, count):
    return jnp.concatenate([ref[first + i] for i in range(count)], axis=1)


def second_rows(parts, shift, kernel_t, sums, weight, potential, *, src_count, tgt_count):
    total = log_sum(parts[...])[0]
    potential[...] = math.log(src_count) - math.log(tgt_count) - total
    w = jnp.exp(-math.log(tgt_count) - total - shift[...])
    weight[...] = w
    w = flat(w)
    hi = w.astype(BF16).astype(F32)
    sub = iota((16, w.shape[1]), 0)
    left = jnp.where(sub == 0, hi, jnp.where(sub == 1, w - hi, 0.0)).astype(BF16)
    values = []
    for b in range(kernel_t.shape[0] // SLABS):
        x = jnp.dot(left, slabs(kernel_t, b * SLABS, SLABS), preferred_element_type=F32)
        values.append(stack(x[:1] + x[1:2], 128))
    sums[...] = jnp.broadcast_to(jnp.concatenate(values, axis=0)[None], sums.shape)


def second_columns(parts, rho, kernel_t, src_t, weight, sums, keep, send, scale, potential, total, *, src_count):
    q = jnp.sum(parts[...], axis=0)
    u = 1.0 / (src_count * q)
    scale[...] = u
    potential[...] = rho[...] - 2.0 * math.log(src_count) - jnp.log(q)
    for b in range(kernel_t.shape[0] // SLABS):
        ub = flat(u[b * SLABS : (b + 1) * SLABS, :])
        hi = ub.astype(BF16).astype(F32)
        sub = iota((16, BLK), 0)
        low = jnp.where(sub == 0, hi, jnp.where(sub == 1, ub - hi, 0.0)).astype(BF16)
        scaled = (src_t[:, b * BLK : (b + 1) * BLK].astype(F32) * ub).astype(BF16)
        left = jnp.concatenate([scaled, low], axis=0)
        x = lax.dot_general(left, slabs(kernel_t, b * SLABS, SLABS), NT, preferred_element_type=F32)
        if b == 0:
            total[...] = x
        else:
            total[...] += x
    w = weight[...]
    sums[...] = jnp.broadcast_to((w * stack(total[128:129, :] + total[129:130, :], 128))[None], sums.shape)
    w = flat(w)
    half = keep.shape[0]
    own = lax.rem(lax.axis_index("row"), 2) * half
    keep[...] = total[pl.ds(pl.multiple_of(own, half), half), :] * w
    send[...] = total[pl.ds(pl.multiple_of(half - own, half), half), :] * w


def on_first_core():
    return lax.rem(lax.axis_index("row"), 2) == 0


def share_of(major, minor):
    first = on_first_core()
    col = lax.axis_index("col")
    z = (col // 4) ^ jnp.where(first, major, minor)
    x = (col % 4) ^ jnp.where(first, minor, major)
    return z * 4 + x


SEND = ((1, 2), (3, 2))
STAY = ((0, 3), (0, 1))


def mix(left, kernel_t, scale, outs, offsets, src_count):
    for k in range(8):
        at = [share_of(offsets[h][k // 4], k % 4) * 2 + h for h in range(2)]
        pair = jnp.concatenate([kernel_t[i] for i in at], axis=1)
        x = jnp.dot(left, pair, preferred_element_type=F32)
        for h in range(2):
            u = scale[pl.ds(at[h], 1), :] * src_count
            outs[h][k * 128 : (k + 1) * 128, :] = x[:, h * 128 : (h + 1) * 128] * u


def target_send(
    parts, weight, before, tgt_t, kernel_t, scale, out_a, out_b, left, potential, gain, *, src_count, tgt_count
):
    total = jnp.sum(parts[...], axis=0)
    g = 1.0 / (tgt_count * total)
    gain[...] = g
    potential[...] = before[...] - math.log(tgt_count) - jnp.log(total)
    value = (tgt_t[...].astype(F32) * flat(weight[...] * g)).astype(BF16)
    left[...] = value
    mix(value, kernel_t, scale, (out_a, out_b), SEND, src_count)


def target_keep(left, kernel_t, scale, out_a, out_b, *, src_count):
    mix(left[...], kernel_t, scale, (out_a, out_b), STAY, src_count)


def moment_half(mine, gain, tgt, out, both):
    x = jnp.dot(
        mine[...] * flat(gain[...]), tgt[...].astype(F32), precision=lax.Precision.HIGHEST, preferred_element_type=F32
    )
    out[...] = x
    both[:, : mine.shape[1]] = mine[...]
    both[:, mine.shape[1] :] = x


def in_order(mine, other):
    first = on_first_core()
    return jnp.concatenate([jnp.where(first, mine, other), jnp.where(first, other, mine)], axis=0)


def finish_sources(mine, other, gain, out, *, tgt_count):
    out[...] = (in_order(mine[...], other[...]) * (flat(gain[...]) * tgt_count)).T.astype(BF16)


def merge_first(keep_a, got_a, keep_b, got_b, moment, send_a, hold_a, send_b, hold_b):
    for keep, got, send, hold in ((keep_a, got_a, send_a, hold_a), (keep_b, got_b, send_b, hold_b)):
        hold[...] = keep[:512, :] + got[:512, :]
        send[:512, :] = keep[512:, :] + got[512:, :]
        send[512:, :] = moment[...]


def merge_second(hold_a, got_a, hold_b, got_b, moment, across, send_2, send_1, send_3, stay):
    total = (moment[...] + got_b[512:, :]) + (across[...] + got_a[512:, :])
    for minor, out in enumerate((stay, send_1, send_2, send_3)):
        rows = slice(minor * 128, (minor + 1) * 128)
        out[:128, :] = hold_a[rows, :] + got_a[rows, :]
        out[128:256, :] = hold_b[rows, :] + got_b[rows, :]
        out[256:, :] = total


def merge_moment(stay, got_2, got_1, got_3, out):
    out[...] = (stay[256:, :] + got_1[256:, :]) + (got_2[256:, :] + got_3[256:, :])


def merge_last(stay, got_2, got_1, got_3, bary):
    for half in range(2):
        rows = slice(half * 128, (half + 1) * 128)
        x = (stay[rows, :] + got_1[rows, :]) + (got_2[rows, :] + got_3[rows, :])
        bary[rows, :] = x.T.astype(BF16)


def finish_moment(mine, other, out):
    out[...] = in_order(mine[...], other[...])


def call(body, outs, *args, scratch=(), spaces=None, flops=1):
    spaces = spaces or {}
    return pl.pallas_call(
        body,
        out_shape=outs,
        in_specs=[pl.BlockSpec(memory_space=spaces.get(i, pltpu.VMEM)) for i in range(len(args))],
        out_specs=jax.tree.map(lambda _: pl.BlockSpec(memory_space=pltpu.VMEM), outs),
        scratch_shapes=list(scratch),
        cost_estimate=pl.CostEstimate(flops=flops, bytes_accessed=1, transcendentals=0),
        compiler_params=pltpu.CompilerParams(vmem_limit_bytes=VMEM_LIMIT),
    )(*args)


def f32(*shape):
    return jax.ShapeDtypeStruct(shape, F32)


def bf16(*shape):
    return jax.ShapeDtypeStruct(shape, BF16)


def near(x):
    return pltpu.with_memory_space_constraint(x, pltpu.VMEM)


def far(x):
    return pltpu.with_memory_space_constraint(x, pltpu.HBM)


def local(src_emb, tgt_emb, cost_factor, col_start):
    rows, cols = src_emb.shape[0], tgt_emb.shape[0]
    width = src_emb.shape[1]
    row_size, col_size = lax.axis_size("row"), lax.axis_size("col")
    src_count, tgt_count = rows * row_size, cols * col_size
    counts = dict(src_count=src_count, tgt_count=tgt_count)
    share = rows // col_size
    row_shape, col_shape = (rows // 128, 128), (cols // 128, 128)

    def swap(x):
        return lax.ppermute(x, "row", [(i, i ^ 1) for i in range(row_size)])

    def by_core(x, step):
        pairs = []
        for i in range(row_size * col_size):
            row, col = divmod(i, col_size)
            y, z, w = step(row % 2, row // 2, col // 4, col % 4)
            pairs.append((i, (y * 2 + row % 2) * col_size + z * 4 + w))
        return lax.ppermute(x, ("row", "col"), pairs)

    def major(x, k):
        return by_core(x, lambda c, y, z, w: (y, z, w ^ k) if c else (y, z ^ k, w))

    def minor(x, k):
        return by_core(x, lambda c, y, z, w: (y, z ^ k, w) if c else (y, z, w ^ k))

    def opposite_y(x):
        return by_core(x, lambda c, y, z, w: (y ^ 2, z, w))

    def along_y(x, k):
        return by_core(x, lambda c, y, z, w: (y ^ k ^ 2 * c, z, w))

    def exchange(x, axis):
        return lax.all_to_all(x, axis, 0, 0)

    lse, proj_t, aug, start = call(
        first_rows,
        [f32(col_size, *row_shape), bf16(width, rows), bf16(cols, 2 * width), f32(*col_shape)],
        far(src_emb), far(tgt_emb), far(cost_factor), far(col_start.reshape(col_shape)),
        scratch=[
            pltpu.VMEM((rows, width), BF16),
            pltpu.VMEM((width, width), BF16),
            pltpu.SemaphoreType.DMA((4,)),
        ],
        spaces={i: pltpu.HBM for i in range(4)},
    )
    parts = exchange(lse, "col")
    src_late, tgt_late, _ = lax.optimization_barrier((src_emb, tgt_emb, proj_t))
    src_t, tgt_t = call(transposes, [bf16(width, rows), bf16(width, cols)], src_late, tgt_late)
    parts, src_t, tgt_t = lax.optimization_barrier((parts, src_t, tgt_t))
    kernel_t, lse, shift, rho = call(
        first_columns,
        [pltpu.VMEM((rows // 128, cols, 128), BF16), f32(row_size, *col_shape), f32(*col_shape), f32(*row_shape)],
        parts, proj_t, aug, start,
        scratch=[pltpu.VMEM((cols, 128), F32), pltpu.VMEM((cols, 2 * width), BF16)],
    )
    parts = exchange(lse, "row")
    sums, weight, before = call(
        functools.partial(second_rows, **counts),
        [f32(col_size, *row_shape), f32(*col_shape), f32(*col_shape)],
        parts, shift, near(kernel_t),
    )
    parts = exchange(sums, "col")
    sums, keep, send, scale, row_potential = call(
        functools.partial(second_columns, src_count=src_count),
        [f32(row_size, *col_shape), f32(width // 2, cols), f32(width // 2, cols), f32(*row_shape), f32(*row_shape)],
        parts, rho, near(kernel_t), src_t, weight,
        scratch=[pltpu.VMEM((width + 16, cols), F32)],
    )
    parts = exchange(sums, "row")
    parts, send = lax.optimization_barrier((parts, send))
    other = swap(send)
    message = f32(8 * width, share // 2)
    send_a, send_b, left, col_potential, gain = call(
        functools.partial(target_send, **counts),
        [message, message, bf16(width, cols), f32(*col_shape), f32(*col_shape)],
        parts, weight, before, tgt_t, near(kernel_t), scale,
        flops=4 * width * cols * rows,
    )
    got_a, got_b = major(send_a, 1), major(send_b, 3)
    keep_a, keep_b = call(
        functools.partial(target_keep, src_count=src_count), [message, message], left, near(kernel_t), scale
    )
    mine = keep + other
    moment, both = call(
        moment_half, [f32(width // 2, width), f32(width // 2, cols + width)], mine, gain, tgt_emb
    )
    both = both + along_y(both, 1)
    mine = both[:, :cols]
    moment = both[:, cols:] + (opposite_y(moment) + along_y(moment, 3))
    rest = along_y(mine, 3)
    keep_a, moment, mine = lax.optimization_barrier((keep_a, moment, mine))
    both = [f32(576, 128), f32(512, 128)] * 2
    send_a, hold_a, send_b, hold_b = call(merge_first, both, keep_a, got_a, keep_b, got_b, moment)
    got_a, got_b, across = major(send_a, 3), major(send_b, 1), major(moment, 2)
    sends = call(merge_second, [f32(320, 128)] * 4, hold_a, got_a, hold_b, got_b, moment, across)
    stay = sends[3]
    got = [minor(sends[0], 2), minor(sends[1], 1), minor(sends[2], 3)]
    stay, mine = lax.optimization_barrier((stay, mine))
    mine = mine + rest
    bary_tgt, = call(
        functools.partial(finish_sources, tgt_count=tgt_count), [bf16(cols, width)], mine, swap(mine), gain
    )
    stay, bary_tgt = lax.optimization_barrier((stay, bary_tgt))
    moment, = call(merge_moment, [f32(width // 2, width)], stay, *got)
    other = swap(moment)
    bary_src, = call(merge_last, [bf16(share, width)], stay, *got)
    bary_src, moment = lax.optimization_barrier((bary_src, moment))
    moment, = call(finish_moment, [f32(width, width)], moment, other)
    return (bary_src, bary_tgt, moment, row_potential.reshape(rows), col_potential.reshape(cols))


def solution(mesh):
    placed = (P("row", None), P("col", None), P(), P("col"))
    return jax.shard_map(
        local,
        mesh=mesh,
        in_specs=placed,
        out_specs=(P(("row", "col"), None), P("col", None), P(), P("row"), P("col")),
        check_vma=False,
    )
```
